32 devices in a mesh: grp: 2 (over y), dom: 8 (over z, x), col: 2 (over core).
Axes of the slice: x: 2, y: 2, z: 4, core: 2. Of those that a mesh axis runs over, the one named last changes fastest.
Arguments:
- features: bfloat16 [49152, 128], P(('grp', 'dom', 'col')), parts along dimension 0, may hold values from -6 to 6
- first_weight: bfloat16 [128, 1024], replicated, may hold values from -0.5 to 0.5
- first_bias: float32 [1024], replicated, may hold values from -3 to 3
- second_weight: bfloat16 [1024, 1024], replicated, may hold values from -0.1875 to 0.1875
- second_bias: float32 [1024], replicated, may hold values from -3 to 3
- third_weight: bfloat16 [1024, 172], replicated, may hold values from -0.1875 to 0.1875
- local_tiles: bfloat16 [16, 2, 16, 128, 128], P(('grp', 'dom'), 'col'), parts along dimension 0, may hold values from 0 to 1, as said below
- local_target: int32 [16, 2, 16], P(('grp', 'dom'), 'col'), parts along dimension 0, may hold values from 0 to 23
- local_source: int32 [16, 2, 16], P(('grp', 'dom'), 'col'), parts along dimension 0, may hold values from 0 to 23
- halo_tiles: bfloat16 [16, 2, 16, 128, 128], P(('grp', 'dom'), 'col'), parts along dimension 0, may hold values from 0 to 1, as said below
- halo_target: int32 [16, 2, 16], P(('grp', 'dom'), 'col'), parts along dimension 0, may hold values from 0 to 23
- halo_block: int32 [16, 2, 16], P(('grp', 'dom'), 'col'), parts along dimension 0, may hold values from 0 to 15
- send_rows: int32 [16, 8, 256], P(('grp', 'dom')), parts along dimension 0, may hold values from 0 to 3071
- send_count: int32 [16, 8], P(('grp', 'dom')), parts along dimension 0, may hold values from 0 to 256, as said below
- degree: int32 [49152], P(('grp', 'dom')), parts along dimension 0, may hold values from 2 to 5
- batch_nodes: int32 [16, 256], P(('grp', 'dom')), parts along dimension 0, may hold values from 0 to 3071
- labels: int32 [16, 256], P(('grp', 'dom')), parts along dimension 0, may hold values from 0 to 171
- batch_logits: float32 [16, 256, 172], P(('grp', 'dom')), parts along dimension 0, may hold values from -18 to 350
Outputs:
- first_weight_gradient: float32 [256, 1024], P('grp'), parts along dimension 0
- first_bias_gradient: float32 [2048], P('grp'), parts along dimension 0
- second_weight_gradient: float32 [2048, 1024], P('grp'), parts along dimension 0
- second_bias_gradient: float32 [2048], P('grp'), parts along dimension 0
- third_weight_gradient: float32 [2048, 172], P('grp'), parts along dimension 0
The draws below stay inside these ranges and needn't reach their ends.
There are 2 independent parts, one for each index of `grp`. The reference program is written for one: setup_inputs(seed, part) draws one part's arguments, and reference() takes and returns one part's arrays. A program takes and returns all parts, laid end to end along the dimension named above; an argument that names none is the same for every part. Nothing has to cross between parts.
Inputs may be any that keep to these rules, and one draw needn't show every extreme that they name: `local_tiles`: entries are 0 or 1, the edges between two blocks of nodes. `halo_tiles`: entries are 0 or 1, the edges between two blocks of nodes. `send_count`: some destinations receive 256 live rows from every source partition.
All inputs are finite; a program needn't handle non-finite values.
Results may differ from the reference program's by a relative error of at most 0.013.
Values may be sent and summed in bfloat16 or wider, within the bound.
No kernel may reach another device: no remote copies, remote signals or barrier semaphores. Data moves between devices by JAX's collectives and lax.ppermute only.
A program may use at most 128 MiB of HBM per device.

```python
from functools import partial
import jax
import jax.numpy as jnp
from jax import lax

FEAT = 128
CLASSES = 172
HID = 1024
BLK = 128
HOPS = 4
RB = 24
TL = 16
TH = 16
HALO_DEV = 2048
BATCH_DEV = 256
CAP = 256
NODES = 24576
N_DOM = 8
N_COL = 2


def tile_pattern(key, shape):
    key_perm, key_extra = jax.random.split(key)
    block_size = shape[-1]
    ordered = jnp.broadcast_to(jnp.arange(block_size, dtype=jnp.int32), shape[:-1])
    shuffled = jax.random.permutation(key_perm, ordered, axis=-1, independent=True)
    diagonal = shuffled[..., :, None] == jnp.arange(block_size, dtype=jnp.int32)
    extras = jax.random.randint(key_extra, shape, 0, block_size) == 0
    return (diagonal | extras).astype(jnp.float32)


def draw_local_tiles(key, part):
    key = jax.random.fold_in(key, 3)
    return tile_pattern(key, (N_DOM, N_COL, TL, BLK, BLK)).astype(jnp.bfloat16)


def draw_halo_tiles(key, part):
    key = jax.random.fold_in(key, 5)
    return tile_pattern(key, (N_DOM, N_COL, TH, BLK, BLK)).astype(jnp.bfloat16)


def draw_send_count(key, part):
    key = jax.random.fold_in(key, 7)
    first, second, third = jax.random.split(key, 3)
    base = jax.random.randint(first, (N_DOM, N_DOM), CAP // 4, CAP // 2 + 1)
    marked = jax.random.randint(second, (N_DOM,), 0, 8) == 0
    forced = jax.random.randint(third, (), 0, N_DOM)
    marked = marked | (jnp.arange(N_DOM) == forced)
    return jnp.where(marked[None, :], CAP, base).astype(jnp.int32)


def draw_batch_logits(key, part):
    key = jax.random.fold_in(key, 11)
    keys = jax.random.split(key, 1)
    shape = (N_DOM, BATCH_DEV, CLASSES)
    base = jnp.clip(3.0 * jax.random.normal(keys[0], shape, jnp.float32), -18.0, 18.0)
    return base


def with_ends(result, rng, smallest, high):
    index_at = [jax.random.randint(jax.random.fold_in(rng, axis), (), 0, length) for axis, length in enumerate(result.shape)]
    main_axis = result.shape.index(max(result.shape))
    beside = index_at[:main_axis] + [(index_at[main_axis] + 1) % result.shape[main_axis]] + index_at[main_axis + 1:]
    return result.at[tuple(index_at)].set(smallest).at[tuple(beside)].set(high)


def steps_of(rng, extent, cuts, least, largest):
    factor_of, own = 1.0, jax.random.fold_in(rng, 6)
    for axis_at, shards_of in cuts:
        draws = jnp.exp(jax.random.uniform(jax.random.fold_in(own, axis_at), (shards_of,), jnp.float32, least / len(cuts), largest / len(cuts)))
        factor_of = factor_of * jnp.repeat(draws, extent[axis_at] // shards_of).reshape([-1 if axis == axis_at else 1 for axis in range(len(extent))])
    return factor_of


def normal_values(own_key, shape, spread, bound, cuts=(), kind=jnp.bfloat16):
    level = steps_of(own_key, shape, cuts, -0.22, 0.18) if cuts else 1.0
    drawn = jax.random.normal(own_key, shape, jnp.float32) * spread * level
    return jnp.minimum(jnp.maximum(drawn, -bound), bound).astype(kind)


def setup_inputs(seed: int = 0, part: int = 0) -> dict:
    seeds = jax.random.split(jax.random.key(seed), 19)
    own_keys = jax.random.split(jax.random.fold_in(seeds[18], part), 19)
    features = normal_values(own_keys[0], (NODES, FEAT), 1.0, 6.0, ((0, 16),))
    first_weight = normal_values(seeds[1], (FEAT, HID), FEAT ** -0.5, 0.5)
    first_bias = normal_values(seeds[2], (HID,), 0.5, 3.0, (), jnp.float32)
    second_weight = normal_values(seeds[3], (HID, HID), HID ** -0.5, 0.1875)
    second_bias = normal_values(seeds[4], (HID,), 0.5, 3.0, (), jnp.float32)
    third_weight = normal_values(seeds[5], (HID, CLASSES), HID ** -0.5, 0.1875)
    local_tiles = draw_local_tiles(jax.random.fold_in(jax.random.fold_in(seeds[18], part), 71), part)
    local_target = with_ends(jax.random.randint(own_keys[7], (N_DOM, N_COL, TL), 0, RB), jax.random.fold_in(own_keys[7], 1), 0, RB - 1).astype(jnp.int32)
    local_source = with_ends(jax.random.randint(own_keys[8], (N_DOM, N_COL, TL), 0, RB), jax.random.fold_in(own_keys[8], 1), 0, RB - 1).astype(jnp.int32)
    halo_tiles = draw_halo_tiles(jax.random.fold_in(jax.random.fold_in(seeds[18], part), 71), part)
    halo_target = with_ends(jax.random.randint(own_keys[10], (N_DOM, N_COL, TH), 0, RB), jax.random.fold_in(own_keys[10], 1), 0, RB - 1).astype(jnp.int32)
    halo_block = with_ends(jax.random.randint(own_keys[11], (N_DOM, N_COL, TH), 0, HALO_DEV // BLK), jax.random.fold_in(own_keys[11], 1), 0, (HALO_DEV // BLK) - 1).astype(jnp.int32)
    send_rows = with_ends(jax.random.randint(own_keys[12], (N_DOM, N_DOM, CAP), 0, RB * BLK), jax.random.fold_in(own_keys[12], 1), 0, (RB * BLK) - 1).astype(jnp.int32)
    send_count = draw_send_count(jax.random.fold_in(jax.random.fold_in(seeds[18], part), 71), part)
    degree = with_ends(jax.random.randint(own_keys[14], (NODES,), max(2, 2 * N_COL * TL // RB), max(2, 2 * N_COL * TL // RB) + 2 * N_COL * TH // RB + 2), jax.random.fold_in(own_keys[14], 1), max(2, 2 * N_COL * TL // RB), (max(2, 2 * N_COL * TL // RB) + 2 * N_COL * TH // RB + 2) - 1).astype(jnp.int32)
    batch_nodes = with_ends(jax.random.randint(own_keys[15], (N_DOM, BATCH_DEV), 0, RB * BLK), jax.random.fold_in(own_keys[15], 1), 0, (RB * BLK) - 1).astype(jnp.int32)
    labels = with_ends(jax.random.randint(own_keys[16], (N_DOM, BATCH_DEV), 0, CLASSES), jax.random.fold_in(own_keys[16], 1), 0, CLASSES - 1).astype(jnp.int32)
    batch_logits = draw_batch_logits(jax.random.fold_in(jax.random.fold_in(seeds[18], part), 71), part)
    return dict(features=features, first_weight=first_weight, first_bias=first_bias, second_weight=second_weight, second_bias=second_bias, third_weight=third_weight, local_tiles=local_tiles, local_target=local_target, local_source=local_source, halo_tiles=halo_tiles, halo_target=halo_target, halo_block=halo_block, send_rows=send_rows, send_count=send_count, degree=degree, batch_nodes=batch_nodes, labels=labels, batch_logits=batch_logits)


teleport = 0.1

def loss_gradient(batch_nodes, labels, batch_logits, node_rows):
    probs = jax.nn.softmax(batch_logits.astype(jnp.float32), axis=-1)
    classes = batch_logits.shape[-1]
    onehot = (labels[:, None] == jnp.arange(classes, dtype=jnp.int32)[None, :]).astype(jnp.float32)
    return jnp.zeros((node_rows, classes), jnp.float32).at[batch_nodes].add(probs - onehot)

def tile_sum(tiles, targets, blocks, block_count):
    product = jnp.einsum('tij,tjc->tic', tiles.astype(jnp.float32), blocks.astype(jnp.float32), precision=lax.Precision.HIGHEST)
    empty = jnp.zeros((block_count, tiles.shape[1], product.shape[-1]), jnp.float32)
    return empty.at[targets].add(product)

def backward_rows(feature_rows, delta_rows, first_weight, first_bias, second_weight, second_bias, third_weight):
    pre_first = jnp.dot(feature_rows, first_weight, preferred_element_type=jnp.float32) + first_bias
    hidden_first = jax.nn.gelu(pre_first).astype(jnp.bfloat16)
    pre_second = jnp.dot(hidden_first, second_weight, preferred_element_type=jnp.float32) + second_bias
    hidden_second = jax.nn.gelu(pre_second).astype(jnp.bfloat16)
    third_grad = jnp.dot(hidden_second.T, delta_rows, preferred_element_type=jnp.float32)
    back_second = jnp.dot(delta_rows, third_weight.T, preferred_element_type=jnp.float32)
    unused_second, slope_second = jax.vjp(jax.nn.gelu, pre_second)
    second_delta = slope_second(back_second)[0].astype(jnp.bfloat16)
    second_grad = jnp.dot(hidden_first.T, second_delta, preferred_element_type=jnp.float32)
    second_bias_grad = lax.optimization_barrier(jnp.sum(second_delta.astype(jnp.float32), axis=0))
    back_first = jnp.dot(second_delta, second_weight.T, preferred_element_type=jnp.float32)
    unused_first, slope_first = jax.vjp(jax.nn.gelu, pre_first)
    first_delta = slope_first(back_first)[0].astype(jnp.bfloat16)
    first_grad = jnp.dot(feature_rows.T, first_delta, preferred_element_type=jnp.float32)
    first_bias_grad = lax.optimization_barrier(jnp.sum(first_delta.astype(jnp.float32), axis=0))
    return (first_grad, first_bias_grad, second_grad, second_bias_grad, third_grad)

def reference(features, first_weight, first_bias, second_weight, second_bias, third_weight, local_tiles, local_target, local_source, halo_tiles, halo_target, halo_block, send_rows, send_count, degree, batch_nodes, labels, batch_logits):
    node_rows = RB * BLK
    inv_root = lax.rsqrt(degree.astype(jnp.float32)).reshape(N_DOM, node_rows, 1)
    loss_grad = jax.vmap(partial(loss_gradient, node_rows=node_rows))(batch_nodes, labels, batch_logits)
    slots = jnp.arange(CAP, dtype=jnp.int32)
    owners = jnp.arange(N_DOM, dtype=jnp.int32)

    def apply(scaled):

        def one(part_index):
            wanted = send_rows[:, part_index, :]
            arrived = scaled[owners[:, None], wanted]
            live = slots[None, :] < send_count[:, part_index][:, None]
            arrived = jnp.where(live[..., None], arrived, jnp.zeros((), jnp.bfloat16))
            arrived = arrived.reshape(HALO_DEV // BLK, BLK, CLASSES)
            own = scaled[part_index].reshape(RB, BLK, CLASSES)
            total = jnp.zeros((node_rows, CLASSES), jnp.float32)
            for core in range(N_COL):
                near = tile_sum(local_tiles[part_index, core], local_target[part_index, core], own[local_source[part_index, core]], RB)
                far = tile_sum(halo_tiles[part_index, core], halo_target[part_index, core], arrived[halo_block[part_index, core]], RB)
                share = (near + far).reshape(node_rows, CLASSES).astype(jnp.bfloat16)
                total = total + lax.optimization_barrier(share).astype(jnp.float32)
            return total
        return lax.map(one, owners)
    current = loss_grad
    accrued = teleport * loss_grad
    for hop in range(HOPS):
        scaled = (inv_root * current).astype(jnp.bfloat16)
        current = (1.0 - teleport) * inv_root * apply(scaled)
        accrued = accrued + (teleport if hop + 1 < HOPS else 1.0) * current
    delta = accrued.astype(jnp.bfloat16)
    feature_parts = features.reshape(N_DOM, node_rows, FEAT)

    def step_part(carry, pieces):
        terms = backward_rows(pieces[0], pieces[1], first_weight, first_bias, second_weight, second_bias, third_weight)
        return (tuple((a + b for a, b in zip(carry, terms))), None)
    start = (jnp.zeros((FEAT, HID), jnp.float32), jnp.zeros((HID,), jnp.float32), jnp.zeros((HID, HID), jnp.float32), jnp.zeros((HID,), jnp.float32), jnp.zeros((HID, CLASSES), jnp.float32))
    totals, unused = lax.scan(step_part, start, (feature_parts, delta))
    return (totals[0], totals[1], totals[2], totals[3], totals[4])
```

```python
import functools
import math

import jax
import jax.numpy as jnp
from jax import lax
from jax.experimental import pallas as pl
from jax.experimental.pallas import tpu as pltpu
from jax.sharding import PartitionSpec as P

HOPS = 4
teleport = 0.1
LANES = 128
UNROLL = 16
VMEM_LIMIT = 40 * 1024 * 1024

bf16 = jnp.bfloat16
f32 = jnp.float32


def vmem():
    return pl.BlockSpec(memory_space=pltpu.VMEM)


def smem():
    return pl.BlockSpec(memory_space=pltpu.SMEM)


def params():
    return pltpu.CompilerParams(vmem_limit_bytes=VMEM_LIMIT)


def is_packed(slots, class_half):
    return slots % 64 == 0 and class_half <= 96


def packed_rows(slots, class_half):
    return slots * 3 // 4 if is_packed(slots, class_half) else slots


def gather_rows(v_ref, idx_ref, stage_ref):
    def body(g, carry):
        base = pl.multiple_of(g * UNROLL, UNROLL)
        for u in range(UNROLL):
            stage_ref[pl.ds(base + u, 1), :] = v_ref[pl.ds(idx_ref[base + u], 1), :]
        return carry

    lax.fori_loop(0, stage_ref.shape[0] // UNROLL, body, 0)


def pack_rows(stage_ref, out_ref, slots, class_half):
    peers = out_ref.shape[0]
    if not is_packed(slots, class_half):

        def plain(j, carry):
            base = pl.multiple_of(j * slots, slots)
            out_ref[j] = stage_ref[pl.ds(base, slots), :].astype(bf16)
            return carry

        lax.fori_loop(0, peers, plain, 0)
        return
    half, quarter = slots // 2, slots // 4
    lane_a = lax.broadcasted_iota(jnp.int32, (half, LANES), 1)
    lane_b = lax.broadcasted_iota(jnp.int32, (quarter, LANES), 1) // 32

    def body(j, carry):
        base = pl.multiple_of(j * slots, slots)
        low = stage_ref[pl.ds(base, half), :]
        high = stage_ref[pl.ds(base + half, half), :]
        out_ref[j, 0:half] = jnp.where(lane_a < 64, low, pltpu.roll(high, 64, 1)).astype(bf16)
        parts = (low[:quarter], low[quarter:], high[:quarter], high[quarter:])
        packed = jnp.zeros((quarter, LANES), f32)
        for g in range(4):
            packed = jnp.where(lane_b == g, pltpu.roll(parts[g], (g * 32 - 64) % LANES, 1), packed)
        out_ref[j, half : half + quarter] = packed.astype(bf16)
        return carry

    lax.fori_loop(0, peers, body, 0)


def unpack_rows(recv_ref, rows_ref, slots, class_half):
    peers = recv_ref.shape[0]
    if not is_packed(slots, class_half):

        def plain(j, carry):
            rows_ref[pl.ds(pl.multiple_of(j * slots, slots), slots), :] = recv_ref[j]
            return carry

        lax.fori_loop(0, peers, plain, 0)
        return
    half, quarter = slots // 2, slots // 4
    lane = lax.broadcasted_iota(jnp.int32, (quarter, LANES), 1)

    def body(j, carry):
        base = pl.multiple_of(j * slots, slots)
        wide = recv_ref[j, 0:half].astype(f32)
        narrow = recv_ref[j, half : half + quarter].astype(f32)
        turned = pltpu.roll(wide, 64, 1)
        fronts = (wide[:quarter], wide[quarter:], turned[:quarter], turned[quarter:])
        for g in range(4):
            back = pltpu.roll(narrow, (64 - g * 32) % LANES, 1)
            back = jnp.where(lane < 96, back, 0.0)
            rows_ref[pl.ds(base + g * quarter, quarter), :] = jnp.where(
                lane < 64, fronts[g], back
            ).astype(bf16)
        return carry

    lax.fori_loop(0, peers, body, 0)


def first_kernel(slots, class_half, classes, core_ref, idx_ref, nodes_ref, labels_ref, logits_ref, degree_ref,
                 out_ref, value_ref, accrued_ref, root_ref, wide_ref, diff_ref, v_ref, stage_ref):
    batch = logits_ref.shape[0]
    blocks, block = degree_ref.shape
    rows = blocks * block
    core = core_ref[0]
    wide_ref[...] = jnp.zeros_like(wide_ref)
    logits = logits_ref[...]
    shifted = jnp.exp(logits - jnp.max(logits, axis=-1, keepdims=True))
    wide_ref[:, :classes] = shifted / jnp.sum(shifted, axis=-1, keepdims=True)
    probs = wide_ref[...]
    turned = pltpu.roll(probs, wide_ref.shape[1] - class_half, 1)[:, :LANES]
    lane = lax.broadcasted_iota(jnp.int32, (batch, LANES), 1)
    chosen = jnp.where(core == 0, probs[:, :LANES], turned)
    diff_ref[...] = jnp.where(lane < class_half, chosen, 0.0)
    v_ref[...] = jnp.zeros_like(v_ref)
    lane_row = lax.broadcasted_iota(jnp.int32, (1, LANES), 1)
    inside = lane_row < class_half
    start = core * class_half

    def add_row(i, carry):
        hot = jnp.where((lane_row == labels_ref[i] - start) & inside, 1.0, 0.0)
        at = pl.ds(nodes_ref[i], 1)
        v_ref[at, :] = v_ref[at, :] + (diff_ref[pl.ds(i, 1), :] - hot)
        return carry

    lax.fori_loop(0, batch, add_row, 0, unroll=8)

    def scale(b, carry):
        at = pl.ds(pl.multiple_of(b * block, block), block)
        inv = lax.rsqrt(degree_ref[pl.ds(b, 1), :].astype(f32))
        root = jnp.transpose(jnp.broadcast_to(inv, (block, block)))
        root_ref[at, :] = root
        grad = v_ref[at, :]
        accrued_ref[at, :] = teleport * grad
        scaled = root * grad
        value_ref[at, :] = scaled.astype(bf16)
        v_ref[at, :] = scaled
        return carry

    lax.fori_loop(0, blocks, scale, 0)
    gather_rows(v_ref, idx_ref, stage_ref)
    pack_rows(stage_ref, out_ref, slots, class_half)


def add_tiles(acc_ref, source_ref, tile_refs, meta_ref, target_base, source_base, stride):
    count, block = tile_refs[0].shape[0], tile_refs[0].shape[1]
    for which, tiles in enumerate(tile_refs):
        for t in range(count):
            target = meta_ref[which * stride + target_base + t]
            source = meta_ref[which * stride + source_base + t]
            product = jnp.dot(
                tiles[t],
                source_ref[pl.ds(pl.multiple_of(source * block, block), block), :],
                preferred_element_type=f32,
            )
            at = pl.ds(pl.multiple_of(target * block, block), block)
            acc_ref[at, :] = acc_ref[at, :] + product


def near_kernel(stride, meta_ref, value_ref, own_ref, other_ref, near_ref):
    near_ref[...] = jnp.zeros_like(near_ref)
    count = own_ref.shape[0]
    add_tiles(near_ref, value_ref, (own_ref, other_ref), meta_ref, 0, count, stride)


def far_kernel(slots, class_half, base, stride, last, core_ref, meta_ref, idx_ref, recv_ref, near_ref, own_ref,
               other_ref, root_ref, accrued_ref, *rest):
    if last:
        keep_ref, send_ref, rows_ref, acc_ref = rest
    else:
        out_ref, value_ref, total_ref, rows_ref, acc_ref, stage_ref = rest
    block = own_ref.shape[1]
    count = own_ref.shape[0]
    rows = near_ref.shape[0]
    blocks = rows // block
    unpack_rows(recv_ref, rows_ref, slots, class_half)
    acc_ref[pl.ds(0, rows), :] = near_ref[...]
    add_tiles(acc_ref, rows_ref, (own_ref, other_ref), meta_ref, base, base + count, stride)
    rate = 1.0 - teleport
    if last:
        half_rows = rows // 2
        core = core_ref[0]
        for out, part in ((send_ref, 1 - core), (keep_ref, core)):

            def finish(b, carry, out=out, part=part):
                to = pl.ds(pl.multiple_of(b * block, block), block)
                at = pl.ds(pl.multiple_of(part * half_rows + b * block, block), block)
                current = rate * root_ref[at, :] * acc_ref[at, :]
                out[to, :] = (accrued_ref[at, :] + current).astype(bf16)
                return carry

            lax.fori_loop(0, half_rows // block, finish, 0)
        return
    acc_ref[pl.ds(rows, 8), :] = jnp.zeros((8, LANES), f32)

    def scale(b, carry):
        at = pl.ds(pl.multiple_of(b * block, block), block)
        root = root_ref[at, :]
        current = rate * root * acc_ref[at, :]
        total_ref[at, :] = accrued_ref[at, :] + teleport * current
        scaled = root * current
        value_ref[at, :] = scaled.astype(bf16)
        acc_ref[at, :] = scaled
        return carry

    lax.fori_loop(0, blocks, scale, 0)
    gather_rows(acc_ref, idx_ref, stage_ref)
    pack_rows(stage_ref, out_ref, slots, class_half)


def gelu_parts(x):
    k = math.sqrt(2.0 / math.pi)
    square = x * x
    t = jnp.tanh(x * (k + (k * 0.044715) * square))
    half_up = 0.5 + 0.5 * t
    slope = half_up + (0.5 * x) * (1.0 - t * t) * (k + (3.0 * k * 0.044715) * square)
    return (x * half_up).astype(bf16), slope.astype(bf16)


def swap_cores(x):
    return lax.ppermute(x, "col", [(0, 1), (1, 0)])


def exchange(x, first_step, second_step):
    domains, cores = lax.axis_size("dom"), lax.axis_size("col")
    steps = (first_step, second_step)
    pairs = [
        (d * cores + c, (d ^ steps[c]) * cores + c) for d in range(domains) for c in range(cores)
    ]
    return lax.ppermute(x, ("dom", "col"), pairs)


def halving_steps():
    domains = lax.axis_size("dom")
    bits = [1 << b for b in range(domains.bit_length() - 1)]
    other = list(bits)
    if len(bits) > 1:
        other[0], other[1] = other[1], other[0]
    return list(zip(bits, other))


def split(x, axis):
    half = x.shape[axis] // 2
    return lax.slice_in_dim(x, 0, half, axis=axis), lax.slice_in_dim(x, half, 2 * half, axis=axis)


def sum_over_domains(x):
    me, core = lax.axis_index("dom"), lax.axis_index("col")
    plan = []
    width, depth = x.shape[1], x.shape[0]
    for steps in halving_steps():
        if width > LANES:
            plan.append((steps, 1))
            width //= 2
        else:
            plan.append((steps, 0))
            depth //= 2
    current = x
    bits = []
    for (a, b), axis in plan:
        up = jnp.where(core == 0, me & a, me & b) != 0
        bits.append(up)
        low, high = split(current, axis)
        got = exchange(jnp.where(up, low, high), a, b)
        keep = jnp.where(up, high, low)
        current = (keep.astype(f32) + got.astype(f32)).astype(bf16)
    for ((a, b), axis), up in zip(plan[::-1], bits[::-1]):
        got = exchange(current, a, b)
        current = jnp.where(
            up,
            jnp.concatenate([got, current], axis),
            jnp.concatenate([current, got], axis),
        )
    return current


def shards(
    features,
    first_weight,
    first_bias,
    second_weight,
    second_bias,
    third_weight,
    local_tiles,
    local_target,
    local_source,
    halo_tiles,
    halo_target,
    halo_block,
    send_rows,
    send_count,
    degree,
    batch_nodes,
    labels,
    batch_logits,
):
    rows = degree.shape[0]
    classes = batch_logits.shape[-1]
    batch = batch_logits.shape[1]
    block = local_tiles.shape[-1]
    blocks = rows // block
    peers, slots = send_rows.shape[1], send_rows.shape[2]
    hidden = second_weight.shape[0]
    class_half = (classes // 2 + 7) // 8 * 8
    core = lax.axis_index("col").astype(jnp.int32)
    core_arg = core.reshape(1)
    packed = packed_rows(slots, class_half)
    local_count, halo_count = local_tiles.shape[2], halo_tiles.shape[2]

    meta_own = jnp.concatenate([local_target[0, 0], local_source[0, 0], halo_target[0, 0], halo_block[0, 0]])
    stride = meta_own.shape[0]
    meta = jnp.concatenate([meta_own, swap_cores(meta_own)])
    own_local, own_halo = local_tiles[0, 0], halo_tiles[0, 0]
    other_local, other_halo = swap_cores(own_local), swap_cores(own_halo)

    live = jnp.arange(slots, dtype=jnp.int32)[None, :] < send_count[0][:, None]
    idx = jnp.where(live, send_rows[0], rows).reshape(-1)

    out_type = jax.ShapeDtypeStruct((peers, packed, LANES), bf16)
    value_type = jax.ShapeDtypeStruct((rows, LANES), bf16)
    wide_type = jax.ShapeDtypeStruct((rows, LANES), f32)
    half_type = jax.ShapeDtypeStruct((rows // 2, LANES), bf16)
    stage = pltpu.VMEM((peers * slots, LANES), f32)

    out, value, accrued, root = pl.pallas_call(
        functools.partial(first_kernel, slots, class_half, classes),
        out_shape=(out_type, value_type, wide_type, wide_type),
        in_specs=[smem(), smem(), smem(), smem(), vmem(), vmem()],
        out_specs=(vmem(), vmem(), vmem(), vmem()),
        scratch_shapes=[
            pltpu.VMEM((batch, 2 * LANES), f32),
            pltpu.VMEM((batch, LANES), f32),
            pltpu.VMEM((rows + 8, LANES), f32),
            stage,
        ],
        compiler_params=params(),
        name="first",
    )(core_arg, idx, batch_nodes[0], labels[0], batch_logits[0], degree.reshape(blocks, block))

    near_call = pl.pallas_call(
        functools.partial(near_kernel, stride),
        out_shape=wide_type,
        in_specs=[smem(), vmem(), vmem(), vmem()],
        out_specs=vmem(),
        compiler_params=params(),
        cost_estimate=pl.CostEstimate(flops=4 * local_count * block**3, bytes_accessed=4 * 2**20, transcendentals=0),
        name="near",
    )

    x = features
    for hop in range(HOPS):
        last = hop + 1 == HOPS
        landed = lax.all_to_all(out, "dom", split_axis=0, concat_axis=0, tiled=True)
        near = near_call(meta, value, own_local, other_local)
        if hop == 0:
            x, _ = lax.optimization_barrier((x, value))
            pre_first = jnp.dot(x, first_weight, preferred_element_type=f32) + first_bias
            hidden_first, slope_first = gelu_parts(pre_first)
        if hop == 1:
            hidden_first, _ = lax.optimization_barrier((hidden_first, value))
            pre_second = jnp.dot(hidden_first, second_weight, preferred_element_type=f32) + second_bias
            hidden_second, slope_second = gelu_parts(pre_second)
        scratch = [pltpu.VMEM((peers * slots, LANES), bf16), pltpu.VMEM((rows + 8, LANES), f32)]
        result = pl.pallas_call(
            functools.partial(far_kernel, slots, class_half, 2 * local_count, stride, last),
            out_shape=(half_type, half_type) if last else (out_type, value_type, wide_type),
            in_specs=[smem(), smem(), smem()] + [vmem()] * 6,
            out_specs=(vmem(), vmem()) if last else (vmem(), vmem(), vmem()),
            scratch_shapes=scratch if last else scratch + [stage],
            compiler_params=params(),
            name="far_last" if last else "far",
        )(core_arg, meta, idx, landed, near, own_halo, other_halo, root, accrued)
        if last:
            keep, send = result
        else:
            out, value, accrued = result

    got = swap_cores(send)
    delta = jnp.concatenate([keep, got], axis=1)
    low = jnp.pad(third_weight[:, :class_half], ((0, 0), (0, LANES - class_half)))
    high = jnp.pad(third_weight[:, class_half:], ((0, 0), (0, LANES - classes + class_half)))
    third = jnp.where(core == 0, jnp.concatenate([low, high], 1), jnp.concatenate([high, low], 1))

    def contract(a, b):
        return lax.dot_general(a, b, (((0,), (0,)), ((), ())), preferred_element_type=f32)

    third_grad = contract(delta, hidden_second).astype(bf16)
    back_second = lax.dot_general(delta, third, (((1,), (1,)), ((), ())), preferred_element_type=f32)
    second_delta = (slope_second.astype(f32) * back_second).astype(bf16)
    second_grad = contract(hidden_first, second_delta).astype(bf16)
    second_bias_grad = jnp.sum(second_delta.astype(f32), axis=0).astype(bf16)
    back_first = lax.dot_general(
        second_delta, second_weight, (((1,), (1,)), ((), ())), preferred_element_type=f32
    )
    first_delta = (slope_first.astype(f32) * back_first).astype(bf16)
    first_grad = contract(x, first_delta).astype(bf16)
    first_bias_grad = jnp.sum(first_delta.astype(f32), axis=0).astype(bf16)

    feat = first_grad.shape[0]
    parts = hidden // 2, feat // 2, class_half
    used = sum(parts) + 1
    domains = lax.axis_size("dom")
    column_splits = (hidden // LANES).bit_length() - 1
    grain = 8 * max(1, domains >> column_splits)
    total_rows = -(-used // grain) * grain

    def bundle(part, third_part, bias_row):
        second_rows = lax.dynamic_slice_in_dim(second_grad, part * parts[0], parts[0], 0)
        first_rows = lax.dynamic_slice_in_dim(first_grad, part * parts[1], parts[1], 0)
        bias = jnp.broadcast_to(bias_row[None], (total_rows - used + 1, hidden))
        return jnp.concatenate([second_rows, first_rows, third_part[:class_half], bias], 0)

    is_first = core == 0
    keep_rows = bundle(core, third_grad[:LANES], jnp.where(is_first, first_bias_grad, second_bias_grad))
    send_rows_ = bundle(1 - core, third_grad[LANES:], jnp.where(is_first, second_bias_grad, first_bias_grad))
    got_rows = swap_cores(send_rows_)
    mine = sum_over_domains((keep_rows.astype(f32) + got_rows.astype(f32)).astype(bf16))
    theirs = swap_cores(mine)
    low = jnp.where(is_first, mine, theirs).astype(f32)
    high = jnp.where(is_first, theirs, mine).astype(f32)
    a, b, c = parts[0], parts[0] + parts[1], used - 1
    return (
        jnp.concatenate([low[a:b], high[a:b]], 0),
        low[c],
        jnp.concatenate([low[:a], high[:a]], 0),
        high[c],
        jnp.concatenate([low[b:c], high[b : b + classes - class_half]], 0).T,
    )


def solution(mesh):
    return jax.shard_map(
        shards,
        mesh=mesh,
        in_specs=(
            P(("grp", "dom", "col"), None),
            P(),
            P(),
            P(),
            P(),
            P(),
            P(("grp", "dom"), "col", None, None, None),
            P(("grp", "dom"), "col", None),
            P(("grp", "dom"), "col", None),
            P(("grp", "dom"), "col", None, None, None),
            P(("grp", "dom"), "col", None),
            P(("grp", "dom"), "col", None),
            P(("grp", "dom"), None, None),
            P(("grp", "dom"), None),
            P(("grp", "dom")),
            P(("grp", "dom"), None),
            P(("grp", "dom"), None),
            P(("grp", "dom"), None, None),
        ),
        out_specs=(P("grp", None), P("grp"), P("grp", None), P("grp"), P("grp", None)),
        check_vma=False,
    )
```

```python
import functools
import math

import jax
import jax.numpy as jnp
from jax import lax
from jax.experimental import pallas as pl
from jax.experimental.pallas import tpu as pltpu
from jax.sharding import PartitionSpec as P

HOPS = 4
teleport = 0.1
LANES = 128
UNROLL = 16
VMEM_LIMIT = 60 * 1024 * 1024

bf16 = jnp.bfloat16
f32 = jnp.float32


def vmem():
    return pl.BlockSpec(memory_space=pltpu.VMEM)


def smem():
    return pl.BlockSpec(memory_space=pltpu.SMEM)


def hbm():
    return pl.BlockSpec(memory_space=pltpu.HBM)


def params():
    return pltpu.CompilerParams(vmem_limit_bytes=VMEM_LIMIT)


def is_packed(slots, class_half):
    return slots % 64 == 0 and class_half <= 96


def packed_rows(slots, class_half):
    return slots * 3 // 4 if is_packed(slots, class_half) else slots


def send_packed(v_ref, idx_ref, stage_ref, packed_ref, out_ref, sems, class_half):
    peers, slots = idx_ref.shape

    def gather(j):
        def body(g, carry):
            base = pl.multiple_of(g * UNROLL, UNROLL)
            for u in range(UNROLL):
                stage_ref[pl.ds(base + u, 1), :] = v_ref[pl.ds(idx_ref[j, base + u], 1), :]
            return carry

        lax.fori_loop(0, slots // UNROLL, body, 0)

    half, quarter = slots // 2, slots // 4
    lane_a = lax.broadcasted_iota(jnp.int32, (half, LANES), 1)
    lane_b = lax.broadcasted_iota(jnp.int32, (quarter, LANES), 1) // 32

    def peer(j, carry):
        gather(j)
        if is_packed(slots, class_half):
            low = stage_ref[0:half, :]
            high = stage_ref[half : 2 * half, :]
            packed_ref[j, 0:half] = jnp.where(lane_a < 64, low, pltpu.roll(high, 64, 1)).astype(bf16)
            parts = (low[:quarter], low[quarter:], high[:quarter], high[quarter:])
            narrow = jnp.zeros((quarter, LANES), f32)
            for g in range(4):
                narrow = jnp.where(lane_b == g, pltpu.roll(parts[g], (g * 32 - 64) % LANES, 1), narrow)
            packed_ref[j, half : half + quarter] = narrow.astype(bf16)
        else:
            packed_ref[j] = stage_ref[...].astype(bf16)
        pltpu.make_async_copy(packed_ref.at[j], out_ref.at[j], sems.at[j]).start()
        return carry

    lax.fori_loop(0, peers, peer, 0)


def wait_packed(packed_ref, out_ref, sems):
    def peer(j, carry):
        pltpu.make_async_copy(packed_ref.at[j], out_ref.at[j], sems.at[j]).wait()
        return carry

    lax.fori_loop(0, packed_ref.shape[0], peer, 0)


def unpack_rows(recv_ref, rows_ref, slots, class_half):
    peers = recv_ref.shape[0]
    if not is_packed(slots, class_half):

        def plain(j, carry):
            rows_ref[pl.ds(pl.multiple_of(j * slots, slots), slots), :] = recv_ref[j]
            return carry

        lax.fori_loop(0, peers, plain, 0)
        return
    half, quarter = slots // 2, slots // 4
    lane = lax.broadcasted_iota(jnp.int32, (quarter, LANES), 1)

    def body(j, carry):
        base = pl.multiple_of(j * slots, slots)
        wide = recv_ref[j, 0:half].astype(f32)
        narrow = recv_ref[j, half : half + quarter].astype(f32)
        turned = pltpu.roll(wide, 64, 1)
        fronts = (wide[:quarter], wide[quarter:], turned[:quarter], turned[quarter:])
        for g in range(4):
            back = pltpu.roll(narrow, (64 - g * 32) % LANES, 1)
            back = jnp.where(lane < 96, back, 0.0)
            rows_ref[pl.ds(base + g * quarter, quarter), :] = jnp.where(
                lane < 64, fronts[g], back
            ).astype(bf16)
        return carry

    lax.fori_loop(0, peers, body, 0)


def root_columns(degree_ref, function):
    blocks, block = degree_ref.shape
    values = function(degree_ref[...].astype(f32))
    return jnp.transpose(jnp.concatenate([values, jnp.zeros((block - blocks, block), f32)], 0))


def over_lanes(columns, b):
    return jnp.broadcast_to(columns[:, b : b + 1], columns.shape)


def first_kernel(class_half, core_ref, count_ref, nodes_ref, labels_ref, rows_ref, logits_ref, degree_ref,
                 out_ref, value_ref, idx_ref, wide_ref, diff_ref, v_ref, stage_ref, packed_ref, value_v, idx_v, idx_s,
                 sems, own_sems):
    classes, batch = logits_ref.shape
    peers, slots = rows_ref.shape
    blocks, block = degree_ref.shape
    rows = blocks * block
    core = core_ref[0]
    slot = lax.broadcasted_iota(jnp.int32, (1, slots), 1)
    for j in range(peers):
        idx_v[j : j + 1, :] = jnp.where(slot < count_ref[j], rows_ref[j : j + 1, :], rows)
    to_smem = pltpu.make_async_copy(idx_v, idx_s, own_sems.at[0])
    to_smem.start()
    to_hbm = pltpu.make_async_copy(idx_v, idx_ref, own_sems.at[1])
    to_hbm.start()
    logits = logits_ref[...]
    shifted = jnp.exp(logits - jnp.max(logits, axis=0, keepdims=True))
    wide_ref[...] = jnp.zeros_like(wide_ref)
    wide_ref[0:classes, :] = shifted / jnp.sum(shifted, axis=0, keepdims=True)
    chosen = wide_ref[pl.ds(pl.multiple_of(core * class_half, 8), LANES), :]
    lane = lax.broadcasted_iota(jnp.int32, (batch, LANES), 1)
    diff_ref[...] = jnp.where(lane < class_half, jnp.transpose(chosen), 0.0)
    v_ref[...] = jnp.zeros_like(v_ref)
    lane_row = lax.broadcasted_iota(jnp.int32, (1, LANES), 1)
    inside = lane_row < class_half
    start = core * class_half

    def add_row(i, carry):
        hot = jnp.where((lane_row == labels_ref[i] - start) & inside, 1.0, 0.0)
        at = pl.ds(nodes_ref[i], 1)
        v_ref[at, :] = v_ref[at, :] + (diff_ref[pl.ds(i, 1), :] - hot)
        return carry

    lax.fori_loop(0, batch, add_row, 0, unroll=8)
    roots = root_columns(degree_ref, lax.rsqrt)
    for b in range(blocks):
        at = slice(b * block, (b + 1) * block)
        scaled = over_lanes(roots, b) * v_ref[at, :]
        value_v[at, :] = scaled.astype(bf16)
        v_ref[at, :] = scaled
    value_copy = pltpu.make_async_copy(value_v, value_ref, own_sems.at[2])
    value_copy.start()
    to_smem.wait()
    send_packed(v_ref, idx_s, stage_ref, packed_ref, out_ref, sems, class_half)
    to_hbm.wait()
    value_copy.wait()
    wait_packed(packed_ref, out_ref, sems)


def add_tiles(acc_ref, source_ref, tile_refs, meta_ref, target_base, source_base, stride):
    count, block = tile_refs[0].shape[0], tile_refs[0].shape[1]
    for which, tiles in enumerate(tile_refs):
        for t in range(count):
            target = meta_ref[which * stride + target_base + t]
            source = meta_ref[which * stride + source_base + t]
            product = jnp.dot(
                tiles[t],
                source_ref[pl.ds(pl.multiple_of(source * block, block), block), :],
                preferred_element_type=f32,
            )
            at = pl.ds(pl.multiple_of(target * block, block), block)
            acc_ref[at, :] = acc_ref[at, :] + product


def near_kernel(stride, last, meta_ref, degree_ref, own_ref, other_ref, *rest):
    count = own_ref.shape[0]
    values = 1 if not last else HOPS
    value_refs, rest = rest[:values], rest[values:]
    near_ref, value_vs, own_v, other_v, acc_ref, sems = rest
    copies = [pltpu.make_async_copy(value_refs[i], value_vs.at[i], sems.at[i]) for i in range(values)]
    copies.append(pltpu.make_async_copy(own_ref, own_v, sems.at[HOPS]))
    copies.append(pltpu.make_async_copy(other_ref, other_v, sems.at[HOPS + 1]))
    for copy in copies:
        copy.start()
    blocks, block = degree_ref.shape
    if not last:
        acc_ref[...] = jnp.zeros_like(acc_ref)
    for copy in copies:
        copy.wait()
    if last:
        columns = root_columns(degree_ref, lambda degree: (teleport / (1.0 - teleport)) * degree)
        for b in range(blocks):
            at = slice(b * block, (b + 1) * block)
            total = value_vs[0, at, :].astype(f32)
            for i in range(1, values):
                total = total + value_vs[i, at, :].astype(f32)
            acc_ref[at, :] = over_lanes(columns, b) * total
    add_tiles(acc_ref, value_vs.at[0], (own_v, other_v), meta_ref, 0, count, stride)
    out = pltpu.make_async_copy(acc_ref, near_ref, sems.at[HOPS + 2])
    out.start()
    out.wait()


def far_kernel(class_half, base, stride, last, core_ref, meta_ref, idx_ref, degree_ref, recv_ref, own_ref,
               other_ref, near_ref, *rest):
    if last:
        keep_ref, send_ref, rows_ref, acc_ref, own_sems = rest
    else:
        out_ref, value_ref, rows_ref, acc_ref, stage_ref, packed_ref, value_v, sems, own_sems = rest
    count, block = own_ref.shape[0], own_ref.shape[1]
    slots = idx_ref.shape[1]
    blocks = degree_ref.shape[0]
    rows = blocks * block
    near_copy = pltpu.make_async_copy(near_ref, acc_ref.at[pl.ds(0, rows)], own_sems.at[0])
    near_copy.start()
    roots = root_columns(degree_ref, lax.rsqrt)
    unpack_rows(recv_ref, rows_ref, slots, class_half)
    near_copy.wait()
    add_tiles(acc_ref, rows_ref, (own_ref, other_ref), meta_ref, base, base + count, stride)
    rate = 1.0 - teleport
    if last:
        half_blocks = blocks // 2
        core = core_ref[0]
        for b in range(half_blocks):
            to = slice(b * block, (b + 1) * block)
            outs = []
            for b_at in (b, half_blocks + b):
                at = slice(b_at * block, (b_at + 1) * block)
                outs.append((rate * over_lanes(roots, b_at) * acc_ref[at, :]).astype(bf16))
            keep_ref[to, :] = jnp.where(core == 0, outs[0], outs[1])
            send_ref[to, :] = jnp.where(core == 0, outs[1], outs[0])
        return
    acc_ref[pl.ds(rows, 8), :] = jnp.zeros((8, LANES), f32)
    for b in range(blocks):
        at = slice(b * block, (b + 1) * block)
        root = over_lanes(roots, b)
        scaled = (rate * root * root) * acc_ref[at, :]
        value_v[at, :] = scaled.astype(bf16)
        acc_ref[at, :] = scaled
    value_copy = pltpu.make_async_copy(value_v, value_ref, own_sems.at[1])
    value_copy.start()
    send_packed(acc_ref, idx_ref, stage_ref, packed_ref, out_ref, sems, class_half)
    value_copy.wait()
    wait_packed(packed_ref, out_ref, sems)


def forward_kernel(x_ref, weight_ref, bias_ref, hidden_ref, slope_ref):
    width = min(256, weight_ref.shape[1])

    def body(j, carry):
        at = pl.ds(pl.multiple_of(j * width, width), width)
        pre = jnp.dot(x_ref[...], weight_ref[:, at], preferred_element_type=f32) + bias_ref[:, at]
        hidden, slope = gelu_parts(pre)
        hidden_ref[:, at] = hidden
        slope_ref[:, at] = slope
        return carry

    lax.fori_loop(0, weight_ref.shape[1] // width, body, 0)


def forward_layer(x, weight, bias, name):
    rows, depth = x.shape
    width = weight.shape[1]
    step = 256 if rows % 256 == 0 else rows
    kind = jax.ShapeDtypeStruct((rows, width), bf16)
    return pl.pallas_call(
        forward_kernel,
        grid=(rows // step,),
        out_shape=(kind, kind),
        in_specs=[
            pl.BlockSpec((step, depth), lambda i: (i, 0)),
            pl.BlockSpec((depth, width), lambda i: (0, 0)),
            pl.BlockSpec((1, width), lambda i: (0, 0)),
        ],
        out_specs=(pl.BlockSpec((step, width), lambda i: (i, 0)), pl.BlockSpec((step, width), lambda i: (i, 0))),
        compiler_params=params(),
        cost_estimate=pl.CostEstimate(
            flops=2 * rows * depth * width + 20 * rows * width, bytes_accessed=8 * 2**20, transcendentals=rows * width
        ),
        name=name,
    )(x, weight, bias.reshape(1, width))


def gelu_parts(x):
    k = math.sqrt(2.0 / math.pi)
    square = x * x
    t = jnp.tanh(x * (k + (k * 0.044715) * square))
    half_up = 0.5 + 0.5 * t
    slope = half_up + (0.5 * x) * (1.0 - t * t) * (k + (3.0 * k * 0.044715) * square)
    return (x * half_up).astype(bf16), slope.astype(bf16)


def swap_cores(x):
    return lax.ppermute(x, "col", [(0, 1), (1, 0)])


def exchange(x, first_step, second_step):
    domains, cores = lax.axis_size("dom"), lax.axis_size("col")
    steps = (first_step, second_step)
    pairs = [
        (d * cores + c, (d ^ steps[c]) * cores + c) for d in range(domains) for c in range(cores)
    ]
    return lax.ppermute(x, ("dom", "col"), pairs)


def halving_steps():
    domains = lax.axis_size("dom")
    bits = [1 << b for b in range(domains.bit_length() - 1)]
    other = list(bits)
    if len(bits) > 1:
        other[0], other[1] = other[1], other[0]
    return list(zip(bits, other))


def split(x, axis):
    half = x.shape[axis] // 2
    return lax.slice_in_dim(x, 0, half, axis=axis), lax.slice_in_dim(x, half, 2 * half, axis=axis)


def sum_over_domains(x):
    me, core = lax.axis_index("dom"), lax.axis_index("col")
    plan = []
    width, depth = x.shape[1], x.shape[0]
    for steps in halving_steps():
        if width > LANES:
            plan.append((steps, 1))
            width //= 2
        else:
            plan.append((steps, 0))
            depth //= 2
    current = x
    bits = []
    for (a, b), axis in plan:
        up = jnp.where(core == 0, me & a, me & b) != 0
        bits.append(up)
        low, high = split(current, axis)
        got = exchange(jnp.where(up, low, high), a, b)
        keep = jnp.where(up, high, low)
        current = (keep.astype(f32) + got.astype(f32)).astype(bf16)
    for ((a, b), axis), up in zip(plan[::-1], bits[::-1]):
        got = exchange(current, a, b)
        current = jnp.where(
            up,
            jnp.concatenate([got, current], axis),
            jnp.concatenate([current, got], axis),
        )
    return current


def shards(
    features,
    first_weight,
    first_bias,
    second_weight,
    second_bias,
    third_weight,
    local_tiles,
    local_target,
    local_source,
    halo_tiles,
    halo_target,
    halo_block,
    send_rows,
    send_count,
    degree,
    batch_nodes,
    labels,
    batch_logits,
):
    rows = degree.shape[0]
    classes = batch_logits.shape[-1]
    batch = batch_logits.shape[1]
    block = local_tiles.shape[-1]
    blocks = rows // block
    peers, slots = send_rows.shape[1], send_rows.shape[2]
    hidden = second_weight.shape[0]
    class_half = (classes // 2 + 7) // 8 * 8
    core = lax.axis_index("col").astype(jnp.int32)
    core_arg = core.reshape(1)
    packed = packed_rows(slots, class_half)
    local_count, halo_count = local_tiles.shape[2], halo_tiles.shape[2]

    meta_own = jnp.concatenate([local_target[0, 0], local_source[0, 0], halo_target[0, 0], halo_block[0, 0]])
    stride = meta_own.shape[0]
    meta = jnp.concatenate([meta_own, swap_cores(meta_own)])
    own_local, own_halo = local_tiles[0, 0], halo_tiles[0, 0]
    other_local, other_halo = swap_cores(own_local), swap_cores(own_halo)

    degree_blocks = degree.reshape(blocks, block)
    out_type = jax.ShapeDtypeStruct((peers, packed, LANES), bf16)
    value_type = jax.ShapeDtypeStruct((rows, LANES), bf16)
    half_type = jax.ShapeDtypeStruct((rows // 2, LANES), bf16)
    acc = pltpu.VMEM((rows + 8, LANES), f32)
    sending = [
        pltpu.VMEM((slots, LANES), f32),
        pltpu.VMEM((peers, packed, LANES), bf16),
        pltpu.VMEM((rows, LANES), bf16),
    ]
    peer_sems = pltpu.SemaphoreType.DMA((peers,))

    out, value, idx = pl.pallas_call(
        functools.partial(first_kernel, class_half),
        out_shape=(out_type, value_type, jax.ShapeDtypeStruct((peers, slots), jnp.int32)),
        in_specs=[smem()] * 4 + [vmem()] * 3,
        out_specs=(hbm(), hbm(), hbm()),
        scratch_shapes=[
            pltpu.VMEM((2 * LANES, batch), f32),
            pltpu.VMEM((batch, LANES), f32),
            acc,
            *sending,
            pltpu.VMEM((peers, slots), jnp.int32),
            pltpu.SMEM((peers, slots), jnp.int32),
            peer_sems,
            pltpu.SemaphoreType.DMA((3,)),
        ],
        compiler_params=params(),
        name="first",
    )(core_arg, send_count[0], batch_nodes[0], labels[0], send_rows[0], batch_logits[0].T, degree_blocks)

    values = []
    for hop in range(HOPS):
        last = hop + 1 == HOPS
        values.insert(0, value)
        landed = lax.all_to_all(out, "dom", split_axis=0, concat_axis=0, tiled=True)
        near_values = values if last else values[:1]
        near = pl.pallas_call(
            functools.partial(near_kernel, stride, last),
            out_shape=jax.ShapeDtypeStruct((rows, LANES), f32),
            in_specs=[smem(), vmem(), hbm(), hbm()] + [hbm()] * len(near_values),
            out_specs=hbm(),
            scratch_shapes=[
                pltpu.VMEM((len(near_values), rows, LANES), bf16),
                pltpu.VMEM((local_count, block, block), bf16),
                pltpu.VMEM((local_count, block, block), bf16),
                pltpu.VMEM((rows, LANES), f32),
                pltpu.SemaphoreType.DMA((HOPS + 3,)),
            ],
            compiler_params=params(),
            cost_estimate=pl.CostEstimate(
                flops=4 * local_count * block**3, bytes_accessed=4 * 2**20, transcendentals=0
            ),
            name="near_last" if last else "near",
        )(meta, degree_blocks, own_local, other_local, *near_values)
        if hop == 0:
            x, _ = lax.optimization_barrier((features, value))
            hidden_first, slope_first = forward_layer(x, first_weight, first_bias, "forward_one")
            near, hidden_first, slope_first = lax.optimization_barrier((near, hidden_first, slope_first))
        if hop == 1:
            tied, _ = lax.optimization_barrier((hidden_first, value))
            hidden_second, slope_second = forward_layer(tied, second_weight, second_bias, "forward_two")
            near, hidden_second, slope_second = lax.optimization_barrier((near, hidden_second, slope_second))
        result = pl.pallas_call(
            functools.partial(far_kernel, class_half, 2 * local_count, stride, last),
            out_shape=(half_type, half_type) if last else (out_type, value_type),
            in_specs=[smem(), smem(), smem()] + [vmem()] * 4 + [hbm()],
            out_specs=(vmem(), vmem()) if last else (hbm(), hbm()),
            scratch_shapes=[pltpu.VMEM((peers * slots, LANES), bf16), acc]
            + ([] if last else sending + [peer_sems])
            + [pltpu.SemaphoreType.DMA((2,))],
            compiler_params=params(),
            name="far_last" if last else "far",
        )(core_arg, meta, idx, degree_blocks, landed, own_halo, other_halo, near)
        if last:
            keep, send = result
        else:
            out, value = result

    got = swap_cores(send)
    delta = jnp.concatenate([keep, got], axis=1)
    low = jnp.pad(third_weight[:, :class_half], ((0, 0), (0, LANES - class_half)))
    high = jnp.pad(third_weight[:, class_half:], ((0, 0), (0, LANES - classes + class_half)))
    third = jnp.where(core == 0, jnp.concatenate([low, high], 1), jnp.concatenate([high, low], 1))

    def contract(a, b):
        return lax.dot_general(a, b, (((0,), (0,)), ((), ())), preferred_element_type=f32)

    third_grad = contract(delta, hidden_second).astype(bf16)
    back_second = lax.dot_general(delta, third, (((1,), (1,)), ((), ())), preferred_element_type=f32)
    second_delta = (slope_second.astype(f32) * back_second).astype(bf16)
    second_grad = contract(hidden_first, second_delta).astype(bf16)
    second_bias_grad = jnp.sum(second_delta.astype(f32), axis=0).astype(bf16)
    back_first = lax.dot_general(
        second_delta, second_weight, (((1,), (1,)), ((), ())), preferred_element_type=f32
    )
    first_delta = (slope_first.astype(f32) * back_first).astype(bf16)
    first_grad = contract(x, first_delta).astype(bf16)
    first_bias_grad = jnp.sum(first_delta.astype(f32), axis=0).astype(bf16)

    feat = first_grad.shape[0]
    parts = hidden // 2, feat // 2, class_half
    used = sum(parts) + 1
    domains = lax.axis_size("dom")
    column_splits = (hidden // LANES).bit_length() - 1
    grain = 8 * max(1, domains >> column_splits)
    total_rows = -(-used // grain) * grain

    def bundle(part, third_part, bias_row):
        second_rows = lax.dynamic_slice_in_dim(second_grad, part * parts[0], parts[0], 0)
        first_rows = lax.dynamic_slice_in_dim(first_grad, part * parts[1], parts[1], 0)
        bias = jnp.broadcast_to(bias_row[None], (total_rows - used + 1, hidden))
        return jnp.concatenate([second_rows, first_rows, third_part[:class_half], bias], 0)

    is_first = core == 0
    keep_rows = bundle(core, third_grad[:LANES], jnp.where(is_first, first_bias_grad, second_bias_grad))
    send_rows_ = bundle(1 - core, third_grad[LANES:], jnp.where(is_first, second_bias_grad, first_bias_grad))
    got_rows = swap_cores(send_rows_)
    mine = sum_over_domains((keep_rows.astype(f32) + got_rows.astype(f32)).astype(bf16))
    theirs = swap_cores(mine)
    low = jnp.where(is_first, mine, theirs).astype(f32)
    high = jnp.where(is_first, theirs, mine).astype(f32)
    a, b, c = parts[0], parts[0] + parts[1], used - 1
    return (
        jnp.concatenate([low[a:b], high[a:b]], 0),
        low[c],
        jnp.concatenate([low[:a], high[:a]], 0),
        high[c],
        jnp.concatenate([low[b:c], high[b : b + classes - class_half]], 0).T,
    )


def solution(mesh):
    return jax.shard_map(
        shards,
        mesh=mesh,
        in_specs=(
            P(("grp", "dom", "col"), None),
            P(),
            P(),
            P(),
            P(),
            P(),
            P(("grp", "dom"), "col", None, None, None),
            P(("grp", "dom"), "col", None),
            P(("grp", "dom"), "col", None),
            P(("grp", "dom"), "col", None, None, None),
            P(("grp", "dom"), "col", None),
            P(("grp", "dom"), "col", None),
            P(("grp", "dom"), None, None),
            P(("grp", "dom"), None),
            P(("grp", "dom")),
            P(("grp", "dom"), None),
            P(("grp", "dom"), None),
            P(("grp", "dom"), None, None),
        ),
        out_specs=(P("grp", None), P("grp"), P("grp", None), P("grp"), P("grp", None)),
        check_vma=False,
    )
```

```python
import functools
import math

import jax
import jax.numpy as jnp
from jax import lax
from jax.experimental import pallas as pl
from jax.experimental.pallas import tpu as pltpu
from jax.sharding import PartitionSpec as P

HOPS = 4
teleport = 0.1
LANES = 128
UNROLL = 16
VMEM_LIMIT = 60 * 1024 * 1024

bf16 = jnp.bfloat16
f32 = jnp.float32


def vmem():
    return pl.BlockSpec(memory_space=pltpu.VMEM)


def smem():
    return pl.BlockSpec(memory_space=pltpu.SMEM)


def hbm():
    return pl.BlockSpec(memory_space=pltpu.HBM)


def params():
    return pltpu.CompilerParams(vmem_limit_bytes=VMEM_LIMIT)


def is_packed(slots, class_half):
    return slots % 64 == 0 and class_half <= 96


def packed_rows(slots, class_half):
    return slots * 3 // 4 if is_packed(slots, class_half) else slots


def send_packed(v_ref, count_ref, idx_ref, stage_ref, packed_ref, out_ref, sems, slots, class_half):
    peers = packed_ref.shape[0]

    def gather(j, carry):
        first = j * slots

        def body(g, inner):
            base = pl.multiple_of(first + g * UNROLL, UNROLL)
            for u in range(UNROLL):
                stage_ref[pl.ds(base + u, 1), :] = v_ref[pl.ds(idx_ref[base + u], 1), :]
            return inner

        return lax.fori_loop(0, (count_ref[j] + (UNROLL - 1)) // UNROLL, body, carry)

    lax.fori_loop(0, peers, gather, 0)
    half, quarter = slots // 2, slots // 4
    row = lax.broadcasted_iota(jnp.int32, (slots, LANES), 0)
    lane_a = lax.broadcasted_iota(jnp.int32, (half, LANES), 1)
    lane_b = lax.broadcasted_iota(jnp.int32, (quarter, LANES), 1) // 32

    def peer(j, carry):
        base = pl.multiple_of(j * slots, slots)
        taken = jnp.where(row < count_ref[j], stage_ref[pl.ds(base, slots), :], 0.0)
        if is_packed(slots, class_half):
            low, high = taken[:half], taken[half:]
            packed_ref[j, 0:half] = jnp.where(lane_a < 64, low, pltpu.roll(high, 64, 1)).astype(bf16)
            parts = (low[:quarter], low[quarter:], high[:quarter], high[quarter:])
            narrow = jnp.zeros((quarter, LANES), f32)
            for g in range(4):
                narrow = jnp.where(lane_b == g, pltpu.roll(parts[g], (g * 32 - 64) % LANES, 1), narrow)
            packed_ref[j, half : half + quarter] = narrow.astype(bf16)
        else:
            packed_ref[j] = taken.astype(bf16)
        pltpu.make_async_copy(packed_ref.at[j], out_ref.at[j], sems.at[j]).start()
        return carry

    lax.fori_loop(0, peers, peer, 0)


def wait_packed(packed_ref, out_ref, sems):
    def peer(j, carry):
        pltpu.make_async_copy(packed_ref.at[j], out_ref.at[j], sems.at[j]).wait()
        return carry

    lax.fori_loop(0, packed_ref.shape[0], peer, 0)


def unpack_rows(recv_ref, rows_ref, slots, class_half):
    peers = recv_ref.shape[0]
    if not is_packed(slots, class_half):

        def plain(j, carry):
            rows_ref[pl.ds(pl.multiple_of(j * slots, slots), slots), :] = recv_ref[j]
            return carry

        lax.fori_loop(0, peers, plain, 0)
        return
    half, quarter = slots // 2, slots // 4
    lane = lax.broadcasted_iota(jnp.int32, (quarter, LANES), 1)

    def body(j, carry):
        base = pl.multiple_of(j * slots, slots)
        wide = recv_ref[j, 0:half].astype(f32)
        narrow = recv_ref[j, half : half + quarter].astype(f32)
        turned = pltpu.roll(wide, 64, 1)
        fronts = (wide[:quarter], wide[quarter:], turned[:quarter], turned[quarter:])
        for g in range(4):
            back = pltpu.roll(narrow, (64 - g * 32) % LANES, 1)
            back = jnp.where(lane < 96, back, 0.0)
            rows_ref[pl.ds(base + g * quarter, quarter), :] = jnp.where(
                lane < 64, fronts[g], back
            ).astype(bf16)
        return carry

    lax.fori_loop(0, peers, body, 0)


def root_columns(degree_ref, function):
    blocks, block = degree_ref.shape
    values = function(degree_ref[...].astype(f32))
    return jnp.transpose(jnp.concatenate([values, jnp.zeros((block - blocks, block), f32)], 0))


def over_lanes(columns, b):
    return jnp.broadcast_to(columns[:, b : b + 1], columns.shape)


def first_kernel(slots, class_half, core_ref, count_ref, idx_ref, nodes_ref, labels_ref, logits_ref, degree_ref,
                 out_ref, value_ref, wide_ref, diff_ref, v_ref, stage_ref, packed_ref, value_v, sems, own_sems):
    classes, batch = logits_ref.shape
    blocks, block = degree_ref.shape
    core = core_ref[0]
    logits = logits_ref[...]
    shifted = jnp.exp(logits - jnp.max(logits, axis=0, keepdims=True))
    hot = lax.broadcasted_iota(jnp.int32, (classes, batch), 0) == labels_ref[...]
    probs = shifted / jnp.sum(shifted, axis=0, keepdims=True)
    wide_ref[...] = jnp.zeros_like(wide_ref)
    wide_ref[0:classes, :] = probs - jnp.where(hot, 1.0, 0.0)
    chosen = wide_ref[pl.ds(pl.multiple_of(core * class_half, 8), LANES), :]
    lane = lax.broadcasted_iota(jnp.int32, (batch, LANES), 1)
    diff_ref[...] = jnp.where(lane < class_half, jnp.transpose(chosen), 0.0)
    v_ref[...] = jnp.zeros_like(v_ref)

    def add_row(i, carry):
        at = pl.ds(nodes_ref[i], 1)
        v_ref[at, :] = v_ref[at, :] + diff_ref[pl.ds(i, 1), :]
        return carry

    lax.fori_loop(0, batch, add_row, 0, unroll=8)
    roots = root_columns(degree_ref, lax.rsqrt)
    for b in range(blocks):
        at = slice(b * block, (b + 1) * block)
        scaled = over_lanes(roots, b) * v_ref[at, :]
        value_v[at, :] = scaled.astype(bf16)
        v_ref[at, :] = scaled
    value_copy = pltpu.make_async_copy(value_v, value_ref, own_sems.at[0])
    value_copy.start()
    send_packed(v_ref, count_ref, idx_ref, stage_ref, packed_ref, out_ref, sems, slots, class_half)
    value_copy.wait()
    wait_packed(packed_ref, out_ref, sems)


def add_tiles(acc_ref, source_ref, tile_refs, meta_ref, target_base, source_base, stride):
    count, block = tile_refs[0].shape[0], tile_refs[0].shape[1]
    for which, tiles in enumerate(tile_refs):
        for t in range(count):
            target = meta_ref[which * stride + target_base + t]
            source = meta_ref[which * stride + source_base + t]
            product = jnp.dot(
                tiles[t],
                source_ref[pl.ds(pl.multiple_of(source * block, block), block), :],
                preferred_element_type=f32,
            )
            at = pl.ds(pl.multiple_of(target * block, block), block)
            acc_ref[at, :] = acc_ref[at, :] + product


def near_kernel(stride, last, meta_ref, degree_ref, own_ref, other_ref, *rest):
    count = own_ref.shape[0]
    values = 1 if not last else HOPS
    value_refs, rest = rest[:values], rest[values:]
    near_ref, value_vs, own_v, other_v, acc_ref, sems = rest
    copies = [pltpu.make_async_copy(value_refs[i], value_vs.at[i], sems.at[i]) for i in range(values)]
    copies.append(pltpu.make_async_copy(own_ref, own_v, sems.at[HOPS]))
    copies.append(pltpu.make_async_copy(other_ref, other_v, sems.at[HOPS + 1]))
    for copy in copies:
        copy.start()
    blocks, block = degree_ref.shape
    if not last:
        acc_ref[...] = jnp.zeros_like(acc_ref)
    for copy in copies:
        copy.wait()
    if last:
        columns = root_columns(degree_ref, lambda degree: (teleport / (1.0 - teleport)) * degree)
        for b in range(blocks):
            at = slice(b * block, (b + 1) * block)
            total = value_vs[0, at, :].astype(f32)
            for i in range(1, values):
                total = total + value_vs[i, at, :].astype(f32)
            acc_ref[at, :] = over_lanes(columns, b) * total
    add_tiles(acc_ref, value_vs.at[0], (own_v, other_v), meta_ref, 0, count, stride)
    out = pltpu.make_async_copy(acc_ref, near_ref, sems.at[HOPS + 2])
    out.start()
    out.wait()


def far_kernel(slots, class_half, base, stride, last, core_ref, meta_ref, count_ref, idx_ref, degree_ref, recv_ref,
               own_ref, other_ref, near_ref, *rest):
    if last:
        keep_ref, send_ref, recv_v, own_v, other_v, rows_ref, acc_ref, own_sems = rest
    else:
        (out_ref, value_ref, recv_v, own_v, other_v, rows_ref, acc_ref, stage_ref, packed_ref, value_v, sems,
         own_sems) = rest
    count, block = own_ref.shape[0], own_ref.shape[1]
    blocks = degree_ref.shape[0]
    copies = [
        pltpu.make_async_copy(recv_ref, recv_v, own_sems.at[0]),
        pltpu.make_async_copy(near_ref, acc_ref, own_sems.at[1]),
        pltpu.make_async_copy(own_ref, own_v, own_sems.at[2]),
        pltpu.make_async_copy(other_ref, other_v, own_sems.at[3]),
    ]
    for copy in copies:
        copy.start()
    roots = root_columns(degree_ref, lax.rsqrt)
    copies[0].wait()
    unpack_rows(recv_v, rows_ref, slots, class_half)
    for copy in copies[1:]:
        copy.wait()
    add_tiles(acc_ref, rows_ref, (own_v, other_v), meta_ref, base, base + count, stride)
    rate = 1.0 - teleport
    if last:
        half_blocks = blocks // 2
        core = core_ref[0]
        for b in range(half_blocks):
            to = slice(b * block, (b + 1) * block)
            outs = []
            for b_at in (b, half_blocks + b):
                at = slice(b_at * block, (b_at + 1) * block)
                outs.append((rate * over_lanes(roots, b_at) * acc_ref[at, :]).astype(bf16))
            keep_ref[to, :] = jnp.where(core == 0, outs[0], outs[1])
            send_ref[to, :] = jnp.where(core == 0, outs[1], outs[0])
        return
    for b in range(blocks):
        at = slice(b * block, (b + 1) * block)
        root = over_lanes(roots, b)
        scaled = (rate * root * root) * acc_ref[at, :]
        value_v[at, :] = scaled.astype(bf16)
        acc_ref[at, :] = scaled
    value_copy = pltpu.make_async_copy(value_v, value_ref, own_sems.at[4])
    value_copy.start()
    send_packed(acc_ref, count_ref, idx_ref, stage_ref, packed_ref, out_ref, sems, slots, class_half)
    value_copy.wait()
    wait_packed(packed_ref, out_ref, sems)


def forward_kernel(x_ref, weight_ref, bias_ref, *rest):
    hidden_ref, slope_ref = rest[-2:]
    width = min(256, weight_ref.shape[1])

    def body(j, carry):
        at = pl.ds(pl.multiple_of(j * width, width), width)
        pre = jnp.dot(x_ref[...], weight_ref[:, at], preferred_element_type=f32) + bias_ref[:, at]
        hidden, slope = gelu_parts(pre)
        hidden_ref[:, at] = hidden
        slope_ref[:, at] = slope
        return carry

    lax.fori_loop(0, weight_ref.shape[1] // width, body, 0)


def forward_layer(x, weight, bias, part, parts, earlier, name):
    rows, depth = x.shape
    width = weight.shape[1]
    step = 256 if rows % (256 * parts) == 0 else rows // parts
    steps = rows // step // parts
    first = part * steps
    kind = jax.ShapeDtypeStruct((rows, width), bf16)
    block = pl.BlockSpec((step, width), lambda i: (first + i, 0))
    return pl.pallas_call(
        forward_kernel,
        grid=(steps,),
        out_shape=(kind, kind),
        in_specs=[
            pl.BlockSpec((step, depth), lambda i: (first + i, 0)),
            pl.BlockSpec((depth, width), lambda i: (0, 0)),
            pl.BlockSpec((1, width), lambda i: (0, 0)),
        ]
        + [hbm()] * len(earlier),
        out_specs=(block, block),
        input_output_aliases={3 + i: i for i in range(len(earlier))},
        compiler_params=params(),
        cost_estimate=pl.CostEstimate(
            flops=(2 * rows * depth * width + 20 * rows * width) // parts,
            bytes_accessed=8 * 2**20 // parts,
            transcendentals=rows * width // parts,
        ),
        name=name,
    )(x, weight, bias.reshape(1, width), *earlier)


def gelu_parts(x):
    k = math.sqrt(2.0 / math.pi)
    square = x * x
    t = jnp.tanh(x * (k + (k * 0.044715) * square))
    half_up = 0.5 + 0.5 * t
    slope = half_up + (0.5 * x) * (1.0 - t * t) * (k + (3.0 * k * 0.044715) * square)
    return (x * half_up).astype(bf16), slope.astype(bf16)


def swap_cores(x):
    return lax.ppermute(x, "col", [(0, 1), (1, 0)])


def exchange(x, first_step, second_step):
    domains, cores = lax.axis_size("dom"), lax.axis_size("col")
    steps = (first_step, second_step)
    pairs = [
        (d * cores + c, (d ^ steps[c]) * cores + c) for d in range(domains) for c in range(cores)
    ]
    return lax.ppermute(x, ("dom", "col"), pairs)


def halving_steps():
    domains = lax.axis_size("dom")
    bits = [1 << b for b in range(domains.bit_length() - 1)]
    other = list(bits)
    if len(bits) > 1:
        other[0], other[1] = other[1], other[0]
    return list(zip(bits, other))


def split(x, axis):
    half = x.shape[axis] // 2
    return lax.slice_in_dim(x, 0, half, axis=axis), lax.slice_in_dim(x, half, 2 * half, axis=axis)


def sum_over_domains(x):
    me, core = lax.axis_index("dom"), lax.axis_index("col")
    plan = []
    width, depth = x.shape[1], x.shape[0]
    for steps in halving_steps():
        if width > LANES:
            plan.append((steps, 1))
            width //= 2
        else:
            plan.append((steps, 0))
            depth //= 2
    current = x
    bits = []
    for (a, b), axis in plan:
        up = jnp.where(core == 0, me & a, me & b) != 0
        bits.append(up)
        low, high = split(current, axis)
        got = exchange(jnp.where(up, low, high), a, b)
        keep = jnp.where(up, high, low)
        current = (keep.astype(f32) + got.astype(f32)).astype(bf16)
    for ((a, b), axis), up in zip(plan[::-1], bits[::-1]):
        got = exchange(current, a, b)
        current = jnp.where(
            up,
            jnp.concatenate([got, current], axis),
            jnp.concatenate([current, got], axis),
        )
    return current


def shards(
    features,
    first_weight,
    first_bias,
    second_weight,
    second_bias,
    third_weight,
    local_tiles,
    local_target,
    local_source,
    halo_tiles,
    halo_target,
    halo_block,
    send_rows,
    send_count,
    degree,
    batch_nodes,
    labels,
    batch_logits,
):
    rows = degree.shape[0]
    classes = batch_logits.shape[-1]
    batch = batch_logits.shape[1]
    block = local_tiles.shape[-1]
    blocks = rows // block
    peers, slots = send_rows.shape[1], send_rows.shape[2]
    hidden = second_weight.shape[0]
    class_half = (classes // 2 + 7) // 8 * 8
    core = lax.axis_index("col").astype(jnp.int32)
    core_arg = core.reshape(1)
    packed = packed_rows(slots, class_half)
    local_count, halo_count = local_tiles.shape[2], halo_tiles.shape[2]

    meta_own = jnp.concatenate([local_target[0, 0], local_source[0, 0], halo_target[0, 0], halo_block[0, 0]])
    stride = meta_own.shape[0]
    meta = jnp.concatenate([meta_own, swap_cores(meta_own)])
    own_local, own_halo = local_tiles[0, 0], halo_tiles[0, 0]
    other_local, other_halo = swap_cores(own_local), swap_cores(own_halo)

    degree_blocks = degree.reshape(blocks, block)
    out_type = jax.ShapeDtypeStruct((peers, packed, LANES), bf16)
    value_type = jax.ShapeDtypeStruct((rows, LANES), bf16)
    half_type = jax.ShapeDtypeStruct((rows // 2, LANES), bf16)
    acc = pltpu.VMEM((rows, LANES), f32)
    sending = [
        pltpu.VMEM((peers * slots, LANES), f32),
        pltpu.VMEM((peers, packed, LANES), bf16),
        pltpu.VMEM((rows, LANES), bf16),
    ]
    peer_sems = pltpu.SemaphoreType.DMA((peers,))

    idx = send_rows[0].reshape(-1)
    counts = send_count[0]
    out, value = pl.pallas_call(
        functools.partial(first_kernel, slots, class_half),
        out_shape=(out_type, value_type),
        in_specs=[smem()] * 4 + [vmem()] * 3,
        out_specs=(hbm(), hbm()),
        scratch_shapes=[
            pltpu.VMEM((2 * LANES, batch), f32),
            pltpu.VMEM((batch, LANES), f32),
            acc,
            *sending,
            peer_sems,
            pltpu.SemaphoreType.DMA((1,)),
        ],
        compiler_params=params(),
        name="first",
    )(core_arg, counts, idx, batch_nodes[0], labels, batch_logits[0].T, degree_blocks)

    values = []
    for hop in range(HOPS):
        last = hop + 1 == HOPS
        values.insert(0, value)
        landed = lax.all_to_all(out, "dom", split_axis=0, concat_axis=0, tiled=True)
        near_values = values if last else values[:1]
        near = pl.pallas_call(
            functools.partial(near_kernel, stride, last),
            out_shape=jax.ShapeDtypeStruct((rows, LANES), f32),
            in_specs=[smem(), vmem(), hbm(), hbm()] + [hbm()] * len(near_values),
            out_specs=hbm(),
            scratch_shapes=[
                pltpu.VMEM((len(near_values), rows, LANES), bf16),
                pltpu.VMEM((local_count, block, block), bf16),
                pltpu.VMEM((local_count, block, block), bf16),
                pltpu.VMEM((rows, LANES), f32),
                pltpu.SemaphoreType.DMA((HOPS + 3,)),
            ],
            compiler_params=params(),
            cost_estimate=pl.CostEstimate(
                flops=4 * local_count * block**3, bytes_accessed=4 * 2**20, transcendentals=0
            ),
            name="near_last" if last else "near",
        )(meta, degree_blocks, own_local, other_local, *near_values)
        if hop == 0:
            x, _ = lax.optimization_barrier((features, value))
            hidden_first, slope_first = forward_layer(x, first_weight, first_bias, 0, 1, (), "forward_one")
            near, hidden_first, slope_first = lax.optimization_barrier((near, hidden_first, slope_first))
        if hop in (1, 2):
            tied, _ = lax.optimization_barrier((hidden_first, value))
            second = forward_layer(
                tied, second_weight, second_bias, hop - 1, 2, () if hop == 1 else second, "forward_two"
            )
            near, *second = lax.optimization_barrier((near, *second))
        result = pl.pallas_call(
            functools.partial(far_kernel, slots, class_half, 2 * local_count, stride, last),
            out_shape=(half_type, half_type) if last else (out_type, value_type),
            in_specs=[smem()] * 4 + [vmem()] + [hbm()] * 4,
            out_specs=(vmem(), vmem()) if last else (hbm(), hbm()),
            scratch_shapes=[
                pltpu.VMEM((peers, packed, LANES), bf16),
                pltpu.VMEM((halo_count, block, block), bf16),
                pltpu.VMEM((halo_count, block, block), bf16),
                pltpu.VMEM((peers * slots, LANES), bf16),
                acc,
            ]
            + ([] if last else sending + [peer_sems])
            + [pltpu.SemaphoreType.DMA((5,))],
            compiler_params=params(),
            name="far_last" if last else "far",
        )(core_arg, meta, counts, idx, degree_blocks, landed, own_halo, other_halo, near)
        if last:
            keep, send = result
        else:
            out, value = result

    hidden_second, slope_second = second
    got = swap_cores(send)
    delta = jnp.concatenate([keep, got], axis=1)
    low = jnp.pad(third_weight[:, :class_half], ((0, 0), (0, LANES - class_half)))
    high = jnp.pad(third_weight[:, class_half:], ((0, 0), (0, LANES - classes + class_half)))
    third = jnp.where(core == 0, jnp.concatenate([low, high], 1), jnp.concatenate([high, low], 1))

    def contract(a, b):
        return lax.dot_general(a, b, (((0,), (0,)), ((), ())), preferred_element_type=f32)

    third_grad = contract(delta, hidden_second).astype(bf16)
    back_second = lax.dot_general(delta, third, (((1,), (1,)), ((), ())), preferred_element_type=f32)
    second_delta = (slope_second.astype(f32) * back_second).astype(bf16)
    second_grad = contract(hidden_first, second_delta).astype(bf16)
    second_bias_grad = jnp.sum(second_delta.astype(f32), axis=0).astype(bf16)
    back_first = lax.dot_general(
        second_delta, second_weight, (((1,), (1,)), ((), ())), preferred_element_type=f32
    )
    first_delta = (slope_first.astype(f32) * back_first).astype(bf16)
    first_grad = contract(x, first_delta).astype(bf16)
    first_bias_grad = jnp.sum(first_delta.astype(f32), axis=0).astype(bf16)

    feat = first_grad.shape[0]
    parts = hidden // 2, feat // 2, class_half
    used = sum(parts) + 1
    domains = lax.axis_size("dom")
    column_splits = (hidden // LANES).bit_length() - 1
    grain = 8 * max(1, domains >> column_splits)
    total_rows = -(-used // grain) * grain

    def bundle(part, third_part, bias_row):
        second_rows = lax.dynamic_slice_in_dim(second_grad, part * parts[0], parts[0], 0)
        first_rows = lax.dynamic_slice_in_dim(first_grad, part * parts[1], parts[1], 0)
        bias = jnp.broadcast_to(bias_row[None], (total_rows - used + 1, hidden))
        return jnp.concatenate([second_rows, first_rows, third_part[:class_half], bias], 0)

    is_first = core == 0
    keep_rows = bundle(core, third_grad[:LANES], jnp.where(is_first, first_bias_grad, second_bias_grad))
    send_rows_ = bundle(1 - core, third_grad[LANES:], jnp.where(is_first, second_bias_grad, first_bias_grad))
    got_rows = swap_cores(send_rows_)
    mine = sum_over_domains((keep_rows.astype(f32) + got_rows.astype(f32)).astype(bf16))
    theirs = swap_cores(mine)
    low = jnp.where(is_first, mine, theirs).astype(f32)
    high = jnp.where(is_first, theirs, mine).astype(f32)
    a, b, c = parts[0], parts[0] + parts[1], used - 1
    return (
        jnp.concatenate([low[a:b], high[a:b]], 0),
        low[c],
        jnp.concatenate([low[:a], high[:a]], 0),
        high[c],
        jnp.concatenate([low[b:c], high[b : b + classes - class_half]], 0).T,
    )


def solution(mesh):
    return jax.shard_map(
        shards,
        mesh=mesh,
        in_specs=(
            P(("grp", "dom", "col"), None),
            P(),
            P(),
            P(),
            P(),
            P(),
            P(("grp", "dom"), "col", None, None, None),
            P(("grp", "dom"), "col", None),
            P(("grp", "dom"), "col", None),
            P(("grp", "dom"), "col", None, None, None),
            P(("grp", "dom"), "col", None),
            P(("grp", "dom"), "col", None),
            P(("grp", "dom"), None, None),
            P(("grp", "dom"), None),
            P(("grp", "dom")),
            P(("grp", "dom"), None),
            P(("grp", "dom"), None),
            P(("grp", "dom"), None, None),
        ),
        out_specs=(P("grp", None), P("grp"), P("grp", None), P("grp"), P("grp", None)),
        check_vma=False,
    )
```

```python
import functools
import math

import jax
import jax.numpy as jnp
from jax import lax
from jax.experimental import pallas as pl
from jax.experimental.pallas import tpu as pltpu
from jax.sharding import PartitionSpec as P

HOPS = 4
teleport = 0.1
LANES = 128
UNROLL = 16
VMEM_LIMIT = 60 * 1024 * 1024

bf16 = jnp.bfloat16
f32 = jnp.float32


def vmem():
    return pl.BlockSpec(memory_space=pltpu.VMEM)


def smem():
    return pl.BlockSpec(memory_space=pltpu.SMEM)


def hbm():
    return pl.BlockSpec(memory_space=pltpu.HBM)


def params():
    return pltpu.CompilerParams(vmem_limit_bytes=VMEM_LIMIT)


def is_packed(slots, class_half):
    return slots % 64 == 0 and class_half <= 96


def packed_rows(slots, class_half):
    return slots * 3 // 4 if is_packed(slots, class_half) else slots


def send_packed(v_ref, count_ref, idx_ref, stage_ref, packed_ref, out_ref, sems, slots, class_half):
    peers = packed_ref.shape[0]

    def gather(j, carry):
        first = j * slots

        def body(g, inner):
            base = pl.multiple_of(first + g * UNROLL, UNROLL)
            for u in range(UNROLL):
                stage_ref[pl.ds(base + u, 1), :] = v_ref[pl.ds(idx_ref[base + u], 1), :]
            return inner

        return lax.fori_loop(0, (count_ref[j] + (UNROLL - 1)) // UNROLL, body, carry)

    lax.fori_loop(0, peers, gather, 0)
    half, quarter = slots // 2, slots // 4
    row = lax.broadcasted_iota(jnp.int32, (slots, LANES), 0)
    lane_a = lax.broadcasted_iota(jnp.int32, (half, LANES), 1)
    lane_b = lax.broadcasted_iota(jnp.int32, (quarter, LANES), 1) // 32

    def peer(j, carry):
        base = pl.multiple_of(j * slots, slots)
        taken = jnp.where(row < count_ref[j], stage_ref[pl.ds(base, slots), :], 0.0)
        if is_packed(slots, class_half):
            low, high = taken[:half], taken[half:]
            packed_ref[j, 0:half] = jnp.where(lane_a < 64, low, pltpu.roll(high, 64, 1)).astype(bf16)
            parts = (low[:quarter], low[quarter:], high[:quarter], high[quarter:])
            narrow = jnp.zeros((quarter, LANES), f32)
            for g in range(4):
                narrow = jnp.where(lane_b == g, pltpu.roll(parts[g], (g * 32 - 64) % LANES, 1), narrow)
            packed_ref[j, half : half + quarter] = narrow.astype(bf16)
        else:
            packed_ref[j] = taken.astype(bf16)
        pltpu.make_async_copy(packed_ref.at[j], out_ref.at[j], sems.at[j]).start()
        return carry

    lax.fori_loop(0, peers, peer, 0)


def wait_packed(packed_ref, out_ref, sems):
    def peer(j, carry):
        pltpu.make_async_copy(packed_ref.at[j], out_ref.at[j], sems.at[j]).wait()
        return carry

    lax.fori_loop(0, packed_ref.shape[0], peer, 0)


def unpack_rows(recv_ref, rows_ref, slots, class_half):
    peers = recv_ref.shape[0]
    if not is_packed(slots, class_half):

        def plain(j, carry):
            rows_ref[pl.ds(pl.multiple_of(j * slots, slots), slots), :] = recv_ref[j]
            return carry

        lax.fori_loop(0, peers, plain, 0)
        return
    half, quarter = slots // 2, slots // 4
    lane = lax.broadcasted_iota(jnp.int32, (quarter, LANES), 1)

    def body(j, carry):
        base = pl.multiple_of(j * slots, slots)
        wide = recv_ref[j, 0:half].astype(f32)
        narrow = recv_ref[j, half : half + quarter].astype(f32)
        turned = pltpu.roll(wide, 64, 1)
        fronts = (wide[:quarter], wide[quarter:], turned[:quarter], turned[quarter:])
        for g in range(4):
            back = pltpu.roll(narrow, (64 - g * 32) % LANES, 1)
            back = jnp.where(lane < 96, back, 0.0)
            rows_ref[pl.ds(base + g * quarter, quarter), :] = jnp.where(
                lane < 64, fronts[g], back
            ).astype(bf16)
        return carry

    lax.fori_loop(0, peers, body, 0)


def root_columns(degree_ref, function):
    blocks, block = degree_ref.shape
    values = function(degree_ref[...].astype(f32))
    return jnp.transpose(jnp.concatenate([values, jnp.zeros((block - blocks, block), f32)], 0))


def over_lanes(columns, b):
    return jnp.broadcast_to(columns[:, b : b + 1], columns.shape)


def first_kernel(slots, class_half, core_ref, count_ref, idx_ref, nodes_ref, labels_ref, logits_ref, degree_ref,
                 out_ref, value_ref, wide_ref, diff_ref, v_ref, stage_ref, packed_ref, value_v, sems, own_sems):
    classes, batch = logits_ref.shape
    blocks, block = degree_ref.shape
    core = core_ref[0]
    logits = logits_ref[...]
    shifted = jnp.exp(logits - jnp.max(logits, axis=0, keepdims=True))
    hot = lax.broadcasted_iota(jnp.int32, (classes, batch), 0) == labels_ref[...]
    probs = shifted / jnp.sum(shifted, axis=0, keepdims=True)
    wide_ref[...] = jnp.zeros_like(wide_ref)
    wide_ref[0:classes, :] = probs - jnp.where(hot, 1.0, 0.0)
    chosen = wide_ref[pl.ds(pl.multiple_of(core * class_half, 8), LANES), :]
    lane = lax.broadcasted_iota(jnp.int32, (batch, LANES), 1)
    diff_ref[...] = jnp.where(lane < class_half, jnp.transpose(chosen), 0.0)
    v_ref[...] = jnp.zeros_like(v_ref)

    def add_row(i, carry):
        at = pl.ds(nodes_ref[i], 1)
        v_ref[at, :] = v_ref[at, :] + diff_ref[pl.ds(i, 1), :]
        return carry

    lax.fori_loop(0, batch, add_row, 0, unroll=8)
    roots = root_columns(degree_ref, lax.rsqrt)
    for b in range(blocks):
        at = slice(b * block, (b + 1) * block)
        scaled = over_lanes(roots, b) * v_ref[at, :]
        value_v[at, :] = scaled.astype(bf16)
        v_ref[at, :] = scaled
    value_copy = pltpu.make_async_copy(value_v, value_ref, own_sems.at[0])
    value_copy.start()
    send_packed(v_ref, count_ref, idx_ref, stage_ref, packed_ref, out_ref, sems, slots, class_half)
    value_copy.wait()
    wait_packed(packed_ref, out_ref, sems)


def add_tiles(acc_ref, source_ref, tile_refs, meta_ref, target_base, source_base, stride):
    count, block = tile_refs[0].shape[0], tile_refs[0].shape[1]
    for which, tiles in enumerate(tile_refs):
        for t in range(count):
            target = meta_ref[which * stride + target_base + t]
            source = meta_ref[which * stride + source_base + t]
            product = jnp.dot(
                tiles[t],
                source_ref[pl.ds(pl.multiple_of(source * block, block), block), :],
                preferred_element_type=f32,
            )
            at = pl.ds(pl.multiple_of(target * block, block), block)
            acc_ref[at, :] = acc_ref[at, :] + product


def near_kernel(stride, last, meta_ref, degree_ref, own_ref, other_ref, *rest):
    count = own_ref.shape[0]
    values = 1 if not last else HOPS
    value_refs, rest = rest[:values], rest[values:]
    near_ref, value_vs, own_v, other_v, acc_ref, sems = rest
    copies = [pltpu.make_async_copy(value_refs[i], value_vs.at[i], sems.at[i]) for i in range(values)]
    copies.append(pltpu.make_async_copy(own_ref, own_v, sems.at[HOPS]))
    copies.append(pltpu.make_async_copy(other_ref, other_v, sems.at[HOPS + 1]))
    for copy in copies:
        copy.start()
    blocks, block = degree_ref.shape
    if not last:
        acc_ref[...] = jnp.zeros_like(acc_ref)
    for copy in copies:
        copy.wait()
    if last:
        columns = root_columns(degree_ref, lambda degree: (teleport / (1.0 - teleport)) * degree)
        for b in range(blocks):
            at = slice(b * block, (b + 1) * block)
            total = value_vs[0, at, :].astype(f32)
            for i in range(1, values):
                total = total + value_vs[i, at, :].astype(f32)
            acc_ref[at, :] = over_lanes(columns, b) * total
    add_tiles(acc_ref, value_vs.at[0], (own_v, other_v), meta_ref, 0, count, stride)
    out = pltpu.make_async_copy(acc_ref, near_ref, sems.at[HOPS + 2])
    out.start()
    out.wait()


def far_kernel(slots, class_half, base, stride, last, core_ref, meta_ref, count_ref, idx_ref, degree_ref, recv_ref,
               own_ref, other_ref, near_ref, *rest):
    if last:
        keep_ref, send_ref, recv_v, own_v, other_v, rows_ref, acc_ref, own_sems = rest
    else:
        (out_ref, value_ref, recv_v, own_v, other_v, rows_ref, acc_ref, stage_ref, packed_ref, value_v, sems,
         own_sems) = rest
    count, block = own_ref.shape[0], own_ref.shape[1]
    blocks = degree_ref.shape[0]
    copies = [
        pltpu.make_async_copy(recv_ref, recv_v, own_sems.at[0]),
        pltpu.make_async_copy(near_ref, acc_ref, own_sems.at[1]),
        pltpu.make_async_copy(own_ref, own_v, own_sems.at[2]),
        pltpu.make_async_copy(other_ref, other_v, own_sems.at[3]),
    ]
    for copy in copies:
        copy.start()
    roots = root_columns(degree_ref, lax.rsqrt)
    copies[0].wait()
    unpack_rows(recv_v, rows_ref, slots, class_half)
    for copy in copies[1:]:
        copy.wait()
    add_tiles(acc_ref, rows_ref, (own_v, other_v), meta_ref, base, base + count, stride)
    rate = 1.0 - teleport
    if last:
        half_blocks = blocks // 2
        core = core_ref[0]
        for b in range(half_blocks):
            to = slice(b * block, (b + 1) * block)
            outs = []
            for b_at in (b, half_blocks + b):
                at = slice(b_at * block, (b_at + 1) * block)
                outs.append((rate * over_lanes(roots, b_at) * acc_ref[at, :]).astype(bf16))
            keep_ref[to, :] = jnp.where(core == 0, outs[0], outs[1])
            send_ref[to, :] = jnp.where(core == 0, outs[1], outs[0])
        return
    for b in range(blocks):
        at = slice(b * block, (b + 1) * block)
        root = over_lanes(roots, b)
        scaled = (rate * root * root) * acc_ref[at, :]
        value_v[at, :] = scaled.astype(bf16)
        acc_ref[at, :] = scaled
    value_copy = pltpu.make_async_copy(value_v, value_ref, own_sems.at[4])
    value_copy.start()
    send_packed(acc_ref, count_ref, idx_ref, stage_ref, packed_ref, out_ref, sems, slots, class_half)
    value_copy.wait()
    wait_packed(packed_ref, out_ref, sems)


def forward_kernel(first_row, chunk, turn_depth, turn_hidden, core_ref, bias_ref, x_ref, weight_ref, *rest):
    hidden_ref, slope_ref, x_v, weight_v, hidden_v, slope_v, sems, out_sems = rest[-8:]
    core = core_ref[0]
    rows, depth = x_v.shape
    width = weight_v.shape[1]
    step = min(256, width // 2)
    copies = [pltpu.make_async_copy(x_ref.at[pl.ds(first_row, rows)], x_v, sems.at[0])]
    if turn_depth:
        half = depth // 2
        for i in range(2):
            source = pl.multiple_of((core ^ i) * half, half)
            copies.append(
                pltpu.make_async_copy(
                    weight_ref.at[pl.ds(source, half)], weight_v.at[pl.ds(i * half, half)], sems.at[1 + i]
                )
            )
    else:
        copies.append(pltpu.make_async_copy(weight_ref, weight_v, sems.at[1]))
    for copy in copies:
        copy.start()
    for copy in copies:
        copy.wait()
    outs = []
    for c in range(rows // chunk):
        here = slice(c * chunk, (c + 1) * chunk)

        def body(j, carry, here=here):
            start = pl.multiple_of(j * step, step)
            at = pl.ds(start, step)
            pre = jnp.dot(x_v[here, :], weight_v[:, at], preferred_element_type=f32) + bias_ref[:, at]
            hidden, slope = gelu_parts(pre)
            slope_v[here, at] = slope
            if turn_hidden:
                turned = lax.rem(start + core * (width // 2), width)
                hidden_v[here, pl.ds(pl.multiple_of(turned, step), step)] = hidden
            else:
                hidden_v[here, at] = hidden
            return carry

        lax.fori_loop(0, width // step, body, 0)
        to = pl.ds(first_row + c * chunk, chunk)
        for k, (source, target) in enumerate(((hidden_v, hidden_ref), (slope_v, slope_ref))):
            out = pltpu.make_async_copy(source.at[pl.ds(c * chunk, chunk)], target.at[to], out_sems.at[2 * c + k])
            out.start()
            outs.append(out)
    for out in outs:
        out.wait()


def forward_layer(core_arg, x, weight, bias, part, parts, turn_depth, turn_hidden, earlier, name):
    rows, depth = x.shape
    width = weight.shape[1]
    own = rows // parts
    chunk = 256 if own % 256 == 0 else own
    kind = jax.ShapeDtypeStruct((rows, width), bf16)
    return pl.pallas_call(
        functools.partial(forward_kernel, part * own, chunk, turn_depth, turn_hidden),
        out_shape=(kind, kind),
        in_specs=[smem(), vmem(), hbm(), hbm()] + [hbm()] * len(earlier),
        out_specs=(hbm(), hbm()),
        scratch_shapes=[
            pltpu.VMEM((own, depth), bf16),
            pltpu.VMEM((depth, width), bf16),
            pltpu.VMEM((own, width), bf16),
            pltpu.VMEM((own, width), bf16),
            pltpu.SemaphoreType.DMA((3,)),
            pltpu.SemaphoreType.DMA((2 * (own // chunk),)),
        ],
        input_output_aliases={4 + i: i for i in range(len(earlier))},
        compiler_params=params(),
        cost_estimate=pl.CostEstimate(
            flops=(2 * rows * depth * width + 20 * rows * width) // parts,
            bytes_accessed=8 * 2**20 // parts,
            transcendentals=rows * width // parts,
        ),
        name=name,
    )(core_arg, bias.reshape(1, width), x, weight, *earlier)


def finish_kernel(class_half, core_ref, mine_one, theirs_one, mine_two, theirs_two, first_ref, first_bias_ref,
                  second_ref, second_bias_ref, third_ref, mine_v, theirs_v, wide_v, sems, out_sems):
    one, two = mine_one.shape[0], mine_two.shape[0]
    hidden = second_ref.shape[0]
    feat = first_ref.shape[0]
    classes = third_ref.shape[0]
    half, feat_half = hidden // 2, feat // 2
    copies = []
    for i, (source, target) in enumerate(((mine_one, mine_v), (theirs_one, theirs_v))):
        copies.append(pltpu.make_async_copy(source, target.at[pl.ds(0, one)], sems.at[i]))
    for i, (source, target) in enumerate(((mine_two, mine_v), (theirs_two, theirs_v))):
        copies.append(pltpu.make_async_copy(source, target.at[pl.ds(one, two)], sems.at[2 + i]))
    for copy in copies:
        copy.start()
    is_first = core_ref[0] == 0

    def both(start, count):
        mine = mine_v[start : start + count, :].astype(f32)
        theirs = theirs_v[start : start + count, :].astype(f32)
        return jnp.where(is_first, mine, theirs), jnp.where(is_first, theirs, mine)

    step = math.gcd(one, half)
    outs = []
    for start in range(0, half, step):
        if start == 0:
            copies[0].wait()
            copies[1].wait()
        if start == one:
            copies[2].wait()
            copies[3].wait()
        low, high = both(start, step)
        for k, value in enumerate((low, high)):
            at = k * half + start
            wide_v[at : at + step, :] = value
            out = pltpu.make_async_copy(
                wide_v.at[pl.ds(at, step)], second_ref.at[pl.ds(at, step)], out_sems.at[2 * (start // step) + k]
            )
            out.start()
            outs.append(out)
    low, high = both(half, feat_half)
    first_ref[0:feat_half, :] = low
    first_ref[feat_half:feat, :] = high
    low, high = both(half + feat_half, class_half)
    third_ref[0:class_half, :] = low
    third_ref[class_half:classes, :] = high[: classes - class_half]
    low, high = both(half + feat_half + class_half, 8)
    first_bias_ref[...] = low[:1]
    second_bias_ref[...] = high[:1]
    for out in outs:
        out.wait()


def gelu_parts(x):
    k = math.sqrt(2.0 / math.pi)
    square = x * x
    t = jnp.tanh(x * (k + (k * 0.044715) * square))
    half_up = 0.5 + 0.5 * t
    slope = half_up + (0.5 * x) * (1.0 - t * t) * (k + (3.0 * k * 0.044715) * square)
    return (x * half_up).astype(bf16), slope.astype(bf16)


def swap_cores(x):
    return lax.ppermute(x, "col", [(0, 1), (1, 0)])


def exchange(x, first_step, second_step):
    domains, cores = lax.axis_size("dom"), lax.axis_size("col")
    steps = (first_step, second_step)
    pairs = [
        (d * cores + c, (d ^ steps[c]) * cores + c) for d in range(domains) for c in range(cores)
    ]
    return lax.ppermute(x, ("dom", "col"), pairs)


def halving_steps():
    domains = lax.axis_size("dom")
    bits = [1 << b for b in range(domains.bit_length() - 1)]
    other = list(bits)
    if len(bits) > 1:
        other[0], other[1] = other[1], other[0]
    return list(zip(bits, other))


def split(x, axis):
    half = x.shape[axis] // 2
    return lax.slice_in_dim(x, 0, half, axis=axis), lax.slice_in_dim(x, half, 2 * half, axis=axis)


def sum_over_domains(x):
    me, core = lax.axis_index("dom"), lax.axis_index("col")
    plan = []
    width, depth = x.shape[1], x.shape[0]
    for steps in halving_steps():
        if width > LANES:
            plan.append((steps, 1))
            width //= 2
        else:
            plan.append((steps, 0))
            depth //= 2
    current = x
    bits = []
    for (a, b), axis in plan:
        up = jnp.where(core == 0, me & a, me & b) != 0
        bits.append(up)
        low, high = split(current, axis)
        got = exchange(jnp.where(up, low, high), a, b)
        keep = jnp.where(up, high, low)
        current = (keep.astype(f32) + got.astype(f32)).astype(bf16)
    for ((a, b), axis), up in zip(plan[::-1], bits[::-1]):
        got = exchange(current, a, b)
        current = jnp.where(
            up,
            jnp.concatenate([got, current], axis),
            jnp.concatenate([current, got], axis),
        )
    return current


def shards(
    features,
    first_weight,
    first_bias,
    second_weight,
    second_bias,
    third_weight,
    local_tiles,
    local_target,
    local_source,
    halo_tiles,
    halo_target,
    halo_block,
    send_rows,
    send_count,
    degree,
    batch_nodes,
    labels,
    batch_logits,
):
    rows = degree.shape[0]
    classes = batch_logits.shape[-1]
    batch = batch_logits.shape[1]
    block = local_tiles.shape[-1]
    blocks = rows // block
    peers, slots = send_rows.shape[1], send_rows.shape[2]
    hidden = second_weight.shape[0]
    class_half = (classes // 2 + 7) // 8 * 8
    core = lax.axis_index("col").astype(jnp.int32)
    core_arg = core.reshape(1)
    packed = packed_rows(slots, class_half)
    local_count, halo_count = local_tiles.shape[2], halo_tiles.shape[2]

    meta_own = jnp.concatenate([local_target[0, 0], local_source[0, 0], halo_target[0, 0], halo_block[0, 0]])
    stride = meta_own.shape[0]
    meta = jnp.concatenate([meta_own, swap_cores(meta_own)])
    own_local, own_halo = local_tiles[0, 0], halo_tiles[0, 0]
    other_local, other_halo = swap_cores(own_local), swap_cores(own_halo)

    degree_blocks = degree.reshape(blocks, block)
    out_type = jax.ShapeDtypeStruct((peers, packed, LANES), bf16)
    value_type = jax.ShapeDtypeStruct((rows, LANES), bf16)
    half_type = jax.ShapeDtypeStruct((rows // 2, LANES), bf16)
    acc = pltpu.VMEM((rows, LANES), f32)
    sending = [
        pltpu.VMEM((peers * slots, LANES), f32),
        pltpu.VMEM((peers, packed, LANES), bf16),
        pltpu.VMEM((rows, LANES), bf16),
    ]
    peer_sems = pltpu.SemaphoreType.DMA((peers,))

    idx = send_rows[0].reshape(-1)
    counts = send_count[0]
    out, value = pl.pallas_call(
        functools.partial(first_kernel, slots, class_half),
        out_shape=(out_type, value_type),
        in_specs=[smem()] * 4 + [vmem()] * 3,
        out_specs=(hbm(), hbm()),
        scratch_shapes=[
            pltpu.VMEM((2 * LANES, batch), f32),
            pltpu.VMEM((batch, LANES), f32),
            acc,
            *sending,
            peer_sems,
            pltpu.SemaphoreType.DMA((1,)),
        ],
        compiler_params=params(),
        name="first",
    )(core_arg, counts, idx, batch_nodes[0], labels, batch_logits[0].T, degree_blocks)

    values = []
    for hop in range(HOPS):
        last = hop + 1 == HOPS
        values.insert(0, value)
        landed = lax.all_to_all(out, "dom", split_axis=0, concat_axis=0, tiled=True)
        near_values = values if last else values[:1]
        near = pl.pallas_call(
            functools.partial(near_kernel, stride, last),
            out_shape=jax.ShapeDtypeStruct((rows, LANES), f32),
            in_specs=[smem(), vmem(), hbm(), hbm()] + [hbm()] * len(near_values),
            out_specs=hbm(),
            scratch_shapes=[
                pltpu.VMEM((len(near_values), rows, LANES), bf16),
                pltpu.VMEM((local_count, block, block), bf16),
                pltpu.VMEM((local_count, block, block), bf16),
                pltpu.VMEM((rows, LANES), f32),
                pltpu.SemaphoreType.DMA((HOPS + 3,)),
            ],
            compiler_params=params(),
            cost_estimate=pl.CostEstimate(
                flops=4 * local_count * block**3, bytes_accessed=4 * 2**20, transcendentals=0
            ),
            name="near_last" if last else "near",
        )(meta, degree_blocks, own_local, other_local, *near_values)
        if hop == 0:
            x, _ = lax.optimization_barrier((features, value))
            hidden_first, slope_first = forward_layer(
                core_arg, x, first_weight, first_bias, 0, 1, False, True, (), "forward_one"
            )
            near, hidden_first, slope_first = lax.optimization_barrier((near, hidden_first, slope_first))
        if hop in (1, 2):
            tied, _ = lax.optimization_barrier((hidden_first, value))
            second = forward_layer(
                core_arg, tied, second_weight, second_bias, hop - 1, 2, True, False, () if hop == 1 else second,
                "forward_two",
            )
            near, *second = lax.optimization_barrier((near, *second))
        if last:
            tied, _ = lax.optimization_barrier((third_weight, value))
            low = jnp.pad(tied[:, :class_half], ((0, 0), (0, LANES - class_half)))
            high = jnp.pad(tied[:, class_half:], ((0, 0), (0, LANES - classes + class_half)))
            third = jnp.where(core == 0, jnp.concatenate([low, high], 1), jnp.concatenate([high, low], 1))
            near, third = lax.optimization_barrier((near, third))
        result = pl.pallas_call(
            functools.partial(far_kernel, slots, class_half, 2 * local_count, stride, last),
            out_shape=(half_type, half_type) if last else (out_type, value_type),
            in_specs=[smem()] * 4 + [vmem()] + [hbm()] * 4,
            out_specs=(vmem(), vmem()) if last else (hbm(), hbm()),
            scratch_shapes=[
                pltpu.VMEM((peers, packed, LANES), bf16),
                pltpu.VMEM((halo_count, block, block), bf16),
                pltpu.VMEM((halo_count, block, block), bf16),
                pltpu.VMEM((peers * slots, LANES), bf16),
                acc,
            ]
            + ([] if last else sending + [peer_sems])
            + [pltpu.SemaphoreType.DMA((5,))],
            compiler_params=params(),
            name="far_last" if last else "far",
        )(core_arg, meta, counts, idx, degree_blocks, landed, own_halo, other_halo, near)
        if last:
            keep, send = result
        else:
            out, value = result

    hidden_second, slope_second = second
    got = swap_cores(send)
    delta = jnp.concatenate([keep, got], axis=1)

    def contract(a, b):
        return lax.dot_general(a, b, (((0,), (0,)), ((), ())), preferred_element_type=f32).astype(bf16)

    half, feat = hidden // 2, x.shape[1]
    lead = half // 4 * 3
    back_second = lax.dot_general(delta, third, (((1,), (1,)), ((), ())), preferred_element_type=f32)
    second_delta = (slope_second.astype(f32) * back_second).astype(bf16)
    second_bias_grad = jnp.sum(second_delta.astype(f32), axis=0).astype(bf16)
    send_lead = contract(hidden_first[:, half : half + lead], second_delta)
    got_lead = swap_cores(send_lead)
    keep_lead = contract(hidden_first[:, :lead], second_delta)
    send_tail = contract(hidden_first[:, half + lead :], second_delta)
    keep_tail = contract(hidden_first[:, lead:half], second_delta)
    third_grad = contract(delta, hidden_second)
    back_first = lax.dot_general(
        second_delta, second_weight, (((1,), (1,)), ((), ())), preferred_element_type=f32
    )
    first_delta = (slope_first.astype(f32) * back_first).astype(bf16)
    first_grad = contract(x, first_delta)
    first_bias_grad = jnp.sum(first_delta.astype(f32), axis=0).astype(bf16)

    is_first = core == 0
    domains = lax.axis_size("dom")
    column_splits = (hidden // LANES).bit_length() - 1
    grain = 8 * max(1, domains >> column_splits)
    used = half - lead + feat // 2 + class_half
    tail_rows = -(-(used + 1) // grain) * grain
    low_first, high_first = first_grad[: feat // 2], first_grad[feat // 2 :]

    def bundle(tail, first_rows, third_rows, bias_row):
        bias = jnp.broadcast_to(bias_row[None], (tail_rows - used, hidden))
        return jnp.concatenate([tail, first_rows, third_rows[:class_half], bias], 0)

    keep_rest = bundle(
        keep_tail,
        jnp.where(is_first, low_first, high_first),
        third_grad[:LANES],
        jnp.where(is_first, first_bias_grad, second_bias_grad),
    )
    send_rest = bundle(
        send_tail,
        jnp.where(is_first, high_first, low_first),
        third_grad[LANES:],
        jnp.where(is_first, second_bias_grad, first_bias_grad),
    )
    got_rest = swap_cores(send_rest)
    mine_lead = sum_over_domains((keep_lead.astype(f32) + got_lead.astype(f32)).astype(bf16))
    mine_rest = sum_over_domains((keep_rest.astype(f32) + got_rest.astype(f32)).astype(bf16))
    theirs_lead, theirs_rest = swap_cores(mine_lead), swap_cores(mine_rest)
    rows_all = lead + tail_rows
    first_out, first_bias_out, second_out, second_bias_out, third_out = pl.pallas_call(
        functools.partial(finish_kernel, class_half),
        out_shape=(
            jax.ShapeDtypeStruct((feat, hidden), f32),
            jax.ShapeDtypeStruct((1, hidden), f32),
            jax.ShapeDtypeStruct((hidden, hidden), f32),
            jax.ShapeDtypeStruct((1, hidden), f32),
            jax.ShapeDtypeStruct((classes, hidden), f32),
        ),
        in_specs=[smem()] + [hbm()] * 4,
        out_specs=(vmem(), vmem(), hbm(), vmem(), vmem()),
        scratch_shapes=[
            pltpu.VMEM((rows_all, hidden), bf16),
            pltpu.VMEM((rows_all, hidden), bf16),
            pltpu.VMEM((hidden, hidden), f32),
            pltpu.SemaphoreType.DMA((4,)),
            pltpu.SemaphoreType.DMA((2 * (half // math.gcd(lead, half)),)),
        ],
        compiler_params=params(),
        name="finish",
    )(core_arg, mine_lead, theirs_lead, mine_rest, theirs_rest)
    return first_out, first_bias_out.reshape(hidden), second_out, second_bias_out.reshape(hidden), third_out.T


def solution(mesh):
    return jax.shard_map(
        shards,
        mesh=mesh,
        in_specs=(
            P(("grp", "dom", "col"), None),
            P(),
            P(),
            P(),
            P(),
            P(),
            P(("grp", "dom"), "col", None, None, None),
            P(("grp", "dom"), "col", None),
            P(("grp", "dom"), "col", None),
            P(("grp", "dom"), "col", None, None, None),
            P(("grp", "dom"), "col", None),
            P(("grp", "dom"), "col", None),
            P(("grp", "dom"), None, None),
            P(("grp", "dom"), None),
            P(("grp", "dom")),
            P(("grp", "dom"), None),
            P(("grp", "dom"), None),
            P(("grp", "dom"), None, None),
        ),
        out_specs=(P("grp", None), P("grp"), P("grp", None), P("grp"), P("grp", None)),
        check_vma=False,
    )
```

```python
import functools
import math

import jax
import jax.numpy as jnp
from jax import lax
from jax.experimental import pallas as pl
from jax.experimental.pallas import tpu as pltpu
from jax.sharding import PartitionSpec as P

HOPS = 4
teleport = 0.1
LANES = 128
UNROLL = 16
VMEM_LIMIT = 60 * 1024 * 1024

bf16 = jnp.bfloat16
f32 = jnp.float32


def vmem():
    return pl.BlockSpec(memory_space=pltpu.VMEM)


def smem():
    return pl.BlockSpec(memory_space=pltpu.SMEM)


def hbm():
    return pl.BlockSpec(memory_space=pltpu.HBM)


def params():
    return pltpu.CompilerParams(vmem_limit_bytes=VMEM_LIMIT)


def is_packed(slots, class_half):
    return slots % 64 == 0 and class_half <= 96


def packed_rows(slots, class_half):
    return slots * 3 // 4 if is_packed(slots, class_half) else slots


def send_packed(v_ref, count_ref, idx_ref, stage_ref, packed_ref, out_ref, sems, slots, class_half):
    peers = packed_ref.shape[0]

    def gather(j, carry):
        first = j * slots

        def body(g, inner):
            base = pl.multiple_of(first + g * UNROLL, UNROLL)
            for u in range(UNROLL):
                stage_ref[pl.ds(base + u, 1), :] = v_ref[pl.ds(idx_ref[base + u], 1), :]
            return inner

        return lax.fori_loop(0, (count_ref[j] + (UNROLL - 1)) // UNROLL, body, carry)

    lax.fori_loop(0, peers, gather, 0)
    half, quarter = slots // 2, slots // 4
    row = lax.broadcasted_iota(jnp.int32, (slots, LANES), 0)
    lane_a = lax.broadcasted_iota(jnp.int32, (half, LANES), 1)
    lane_b = lax.broadcasted_iota(jnp.int32, (quarter, LANES), 1) // 32

    def peer(j, carry):
        base = pl.multiple_of(j * slots, slots)
        taken = jnp.where(row < count_ref[j], stage_ref[pl.ds(base, slots), :], 0.0)
        if is_packed(slots, class_half):
            low, high = taken[:half], taken[half:]
            packed_ref[j, 0:half] = jnp.where(lane_a < 64, low, pltpu.roll(high, 64, 1)).astype(bf16)
            parts = (low[:quarter], low[quarter:], high[:quarter], high[quarter:])
            narrow = jnp.zeros((quarter, LANES), f32)
            for g in range(4):
                narrow = jnp.where(lane_b == g, pltpu.roll(parts[g], (g * 32 - 64) % LANES, 1), narrow)
            packed_ref[j, half : half + quarter] = narrow.astype(bf16)
        else:
            packed_ref[j] = taken.astype(bf16)
        pltpu.make_async_copy(packed_ref.at[j], out_ref.at[j], sems.at[j]).start()
        return carry

    lax.fori_loop(0, peers, peer, 0)


def wait_packed(packed_ref, out_ref, sems):
    def peer(j, carry):
        pltpu.make_async_copy(packed_ref.at[j], out_ref.at[j], sems.at[j]).wait()
        return carry

    lax.fori_loop(0, packed_ref.shape[0], peer, 0)


def unpack_rows(recv_ref, rows_ref, slots, class_half):
    peers = recv_ref.shape[0]
    if not is_packed(slots, class_half):

        def plain(j, carry):
            rows_ref[pl.ds(pl.multiple_of(j * slots, slots), slots), :] = recv_ref[j]
            return carry

        lax.fori_loop(0, peers, plain, 0)
        return
    half, quarter = slots // 2, slots // 4
    lane = lax.broadcasted_iota(jnp.int32, (quarter, LANES), 1)

    def body(j, carry):
        base = pl.multiple_of(j * slots, slots)
        wide = recv_ref[j, 0:half].astype(f32)
        narrow = recv_ref[j, half : half + quarter].astype(f32)
        turned = pltpu.roll(wide, 64, 1)
        fronts = (wide[:quarter], wide[quarter:], turned[:quarter], turned[quarter:])
        for g in range(4):
            back = pltpu.roll(narrow, (64 - g * 32) % LANES, 1)
            back = jnp.where(lane < 96, back, 0.0)
            rows_ref[pl.ds(base + g * quarter, quarter), :] = jnp.where(
                lane < 64, fronts[g], back
            ).astype(bf16)
        return carry

    lax.fori_loop(0, peers, body, 0)


def root_columns(degree_ref, function):
    blocks, block = degree_ref.shape
    values = function(degree_ref[...].astype(f32))
    return jnp.transpose(jnp.concatenate([values, jnp.zeros((block - blocks, block), f32)], 0))


def over_lanes(columns, b):
    return jnp.broadcast_to(columns[:, b : b + 1], columns.shape)


def first_kernel(class_half, core_ref, count_ref, nodes_ref, rows_ref, labels_ref, logits_ref, degree_ref,
                 out_ref, value_ref, wide_ref, diff_ref, v_ref, stage_ref, packed_ref, value_v, idx_ref, idx_sems,
                 sems, own_sems):
    classes, unused, batch = logits_ref.shape
    peers = packed_ref.shape[0]
    slots = stage_ref.shape[0] // peers
    flat = []
    if rows_ref.ndim == 1:
        idx_ref = rows_ref
    else:
        for j in range(peers):
            to = idx_ref.at[pl.ds(j * slots, slots)]
            flat.append(pltpu.make_async_copy(rows_ref.at[j], to, idx_sems.at[j]))
    for copy in flat:
        copy.start()
    blocks, block = degree_ref.shape
    core = core_ref[0]
    logits = logits_ref[...].reshape(classes, batch)
    shifted = jnp.exp(logits - jnp.max(logits, axis=0, keepdims=True))
    hot = lax.broadcasted_iota(jnp.int32, (classes, batch), 0) == labels_ref[...]
    probs = shifted / jnp.sum(shifted, axis=0, keepdims=True)
    wide_ref[...] = jnp.zeros_like(wide_ref)
    wide_ref[0:classes, :] = probs - jnp.where(hot, 1.0, 0.0)
    chosen = wide_ref[pl.ds(pl.multiple_of(core * class_half, 8), LANES), :]
    lane = lax.broadcasted_iota(jnp.int32, (batch, LANES), 1)
    diff_ref[...] = jnp.where(lane < class_half, jnp.transpose(chosen), 0.0)
    v_ref[...] = jnp.zeros_like(v_ref)

    def add_row(i, carry):
        at = pl.ds(nodes_ref[i], 1)
        v_ref[at, :] = v_ref[at, :] + diff_ref[pl.ds(i, 1), :]
        return carry

    lax.fori_loop(0, batch, add_row, 0, unroll=8)
    roots = root_columns(degree_ref, lax.rsqrt)
    for b in range(blocks):
        at = slice(b * block, (b + 1) * block)
        scaled = over_lanes(roots, b) * v_ref[at, :]
        value_v[at, :] = scaled.astype(bf16)
        v_ref[at, :] = scaled
    value_copy = pltpu.make_async_copy(value_v, value_ref, own_sems.at[0])
    value_copy.start()
    for copy in flat:
        copy.wait()
    send_packed(v_ref, count_ref, idx_ref, stage_ref, packed_ref, out_ref, sems, slots, class_half)
    value_copy.wait()
    wait_packed(packed_ref, out_ref, sems)


def add_tiles(acc_ref, source_ref, tile_refs, meta_ref, target_base, source_base, stride):
    count, block = tile_refs[0].shape[0], tile_refs[0].shape[1]
    for which, tiles in enumerate(tile_refs):
        for t in range(count):
            target = meta_ref[which * stride + target_base + t]
            source = meta_ref[which * stride + source_base + t]
            product = jnp.dot(
                tiles[t],
                source_ref[pl.ds(pl.multiple_of(source * block, block), block), :],
                preferred_element_type=f32,
            )
            at = pl.ds(pl.multiple_of(target * block, block), block)
            acc_ref[at, :] = acc_ref[at, :] + product


def near_kernel(stride, last, meta_ref, degree_ref, own_ref, other_ref, *rest):
    count = own_ref.shape[0]
    values = 1 if not last else HOPS
    value_refs, rest = rest[:values], rest[values:]
    near_ref, value_vs, own_v, other_v, acc_ref, sems = rest
    copies = [pltpu.make_async_copy(value_refs[i], value_vs.at[i], sems.at[i]) for i in range(values)]
    copies.append(pltpu.make_async_copy(own_ref, own_v, sems.at[HOPS]))
    copies.append(pltpu.make_async_copy(other_ref, other_v, sems.at[HOPS + 1]))
    for copy in copies:
        copy.start()
    blocks, block = degree_ref.shape
    if not last:
        acc_ref[...] = jnp.zeros_like(acc_ref)
    for copy in copies:
        copy.wait()
    if last:
        columns = root_columns(degree_ref, lambda degree: (teleport / (1.0 - teleport)) * degree)
        for b in range(blocks):
            at = slice(b * block, (b + 1) * block)
            total = value_vs[0, at, :].astype(f32)
            for i in range(1, values):
                total = total + value_vs[i, at, :].astype(f32)
            acc_ref[at, :] = over_lanes(columns, b) * total
    add_tiles(acc_ref, value_vs.at[0], (own_v, other_v), meta_ref, 0, count, stride)
    out = pltpu.make_async_copy(acc_ref, near_ref, sems.at[HOPS + 2])
    out.start()
    out.wait()


def far_kernel(slots, class_half, base, stride, last, core_ref, meta_ref, count_ref, idx_ref, degree_ref, recv_ref,
               own_ref, other_ref, near_ref, *rest):
    if last:
        keep_ref, send_ref, recv_v, own_v, other_v, rows_ref, acc_ref, own_sems = rest
    else:
        (out_ref, value_ref, recv_v, own_v, other_v, rows_ref, acc_ref, stage_ref, packed_ref, value_v, sems,
         own_sems) = rest
    count, block = own_ref.shape[0], own_ref.shape[1]
    blocks = degree_ref.shape[0]
    copies = [
        pltpu.make_async_copy(recv_ref, recv_v, own_sems.at[0]),
        pltpu.make_async_copy(near_ref, acc_ref, own_sems.at[1]),
        pltpu.make_async_copy(own_ref, own_v, own_sems.at[2]),
        pltpu.make_async_copy(other_ref, other_v, own_sems.at[3]),
    ]
    for copy in copies:
        copy.start()
    roots = root_columns(degree_ref, lax.rsqrt)
    copies[0].wait()
    unpack_rows(recv_v, rows_ref, slots, class_half)
    for copy in copies[1:]:
        copy.wait()
    add_tiles(acc_ref, rows_ref, (own_v, other_v), meta_ref, base, base + count, stride)
    rate = 1.0 - teleport
    if last:
        half_blocks = blocks // 2
        core = core_ref[0]
        for b in range(half_blocks):
            to = slice(b * block, (b + 1) * block)
            outs = []
            for b_at in (b, half_blocks + b):
                at = slice(b_at * block, (b_at + 1) * block)
                outs.append((rate * over_lanes(roots, b_at) * acc_ref[at, :]).astype(bf16))
            keep_ref[to, :] = jnp.where(core == 0, outs[0], outs[1])
            send_ref[to, :] = jnp.where(core == 0, outs[1], outs[0])
        return
    for b in range(blocks):
        at = slice(b * block, (b + 1) * block)
        root = over_lanes(roots, b)
        scaled = (rate * root * root) * acc_ref[at, :]
        value_v[at, :] = scaled.astype(bf16)
        acc_ref[at, :] = scaled
    value_copy = pltpu.make_async_copy(value_v, value_ref, own_sems.at[4])
    value_copy.start()
    send_packed(acc_ref, count_ref, idx_ref, stage_ref, packed_ref, out_ref, sems, slots, class_half)
    value_copy.wait()
    wait_packed(packed_ref, out_ref, sems)


def finish_kernel(class_half, core_ref, mine_one, theirs_one, mine_two, theirs_two, first_ref, first_bias_ref,
                  second_ref, second_bias_ref, third_ref, wide_v, out_sems):
    one = mine_one.shape[0]
    hidden = second_ref.shape[0]
    feat = first_ref.shape[0]
    classes = third_ref.shape[0]
    half, feat_half = hidden // 2, feat // 2
    is_first = core_ref[0] == 0

    def both(start, count):
        mine_ref, theirs_ref = (mine_one, theirs_one) if start < one else (mine_two, theirs_two)
        at = start if start < one else start - one
        mine = mine_ref[at : at + count, :].astype(f32)
        theirs = theirs_ref[at : at + count, :].astype(f32)
        return jnp.where(is_first, mine, theirs), jnp.where(is_first, theirs, mine)

    step = math.gcd(one, half)
    outs = []
    for start in range(0, half, step):
        for k, value in enumerate(both(start, step)):
            at = k * half + start
            wide_v[at : at + step, :] = value
            out = pltpu.make_async_copy(
                wide_v.at[pl.ds(at, step)], second_ref.at[pl.ds(at, step)], out_sems.at[2 * (start // step) + k]
            )
            out.start()
            outs.append(out)
    low, high = both(half + feat_half, class_half)
    third_ref[0:class_half, :] = low
    third_ref[class_half:classes, :] = high[: classes - class_half]
    firsts = both(half, feat_half)
    biases = both(half + feat_half + class_half, 8)
    for k in range(2):
        at = slice(k * half, (k + 1) * half)
        first_ref[0:feat_half, at] = firsts[k][:, :half]
        first_ref[feat_half:feat, at] = firsts[k][:, half:]
        first_bias_ref[:, at] = biases[k][:1, :half]
        second_bias_ref[:, at] = biases[k][:1, half:]
    for out in outs:
        out.wait()


def gelu_parts(x):
    k = math.sqrt(2.0 / math.pi)
    square = x * x
    t = jnp.tanh(x * (k + (k * 0.044715) * square))
    half_up = 0.5 + 0.5 * t
    slope = half_up + (0.5 * x) * (1.0 - t * t) * (k + (3.0 * k * 0.044715) * square)
    return (x * half_up).astype(bf16), slope.astype(bf16)


def swap_cores(x):
    return lax.ppermute(x, "col", [(0, 1), (1, 0)])


def exchange(x, first_step, second_step):
    domains, cores = lax.axis_size("dom"), lax.axis_size("col")
    steps = (first_step, second_step)
    pairs = [
        (d * cores + c, (d ^ steps[c]) * cores + c) for d in range(domains) for c in range(cores)
    ]
    return lax.ppermute(x, ("dom", "col"), pairs)


def halving_steps():
    domains = lax.axis_size("dom")
    bits = [1 << b for b in range(domains.bit_length() - 1)]
    other = list(bits)
    if len(bits) > 1:
        other[0], other[1] = other[1], other[0]
    return list(zip(bits, other))


def split(x, axis):
    half = x.shape[axis] // 2
    return lax.slice_in_dim(x, 0, half, axis=axis), lax.slice_in_dim(x, half, 2 * half, axis=axis)


def sum_over_domains(x):
    me, core = lax.axis_index("dom"), lax.axis_index("col")
    plan = []
    width, depth = x.shape[1], x.shape[0]
    for steps in halving_steps():
        if width > LANES:
            plan.append((steps, 1))
            width //= 2
        else:
            plan.append((steps, 0))
            depth //= 2
    current = x
    bits = []
    for (a, b), axis in plan:
        up = jnp.where(core == 0, me & a, me & b) != 0
        bits.append(up)
        low, high = split(current, axis)
        got = exchange(jnp.where(up, low, high), a, b)
        keep = jnp.where(up, high, low)
        current = (keep.astype(f32) + got.astype(f32)).astype(bf16)
    for ((a, b), axis), up in zip(plan[::-1], bits[::-1]):
        got = exchange(current, a, b)
        current = jnp.where(
            up,
            jnp.concatenate([got, current], axis),
            jnp.concatenate([current, got], axis),
        )
    return current


def shards(
    features,
    first_weight,
    first_bias,
    second_weight,
    second_bias,
    third_weight,
    local_tiles,
    local_target,
    local_source,
    halo_tiles,
    halo_target,
    halo_block,
    send_rows,
    send_count,
    degree,
    batch_nodes,
    labels,
    batch_logits,
):
    rows = degree.shape[0]
    classes = batch_logits.shape[-1]
    batch = batch_logits.shape[1]
    block = local_tiles.shape[-1]
    blocks = rows // block
    peers, slots = send_rows.shape[1], send_rows.shape[2]
    hidden = second_weight.shape[0]
    class_half = (classes // 2 + 7) // 8 * 8
    core = lax.axis_index("col").astype(jnp.int32)
    core_arg = core.reshape(1)
    packed = packed_rows(slots, class_half)
    local_count, halo_count = local_tiles.shape[2], halo_tiles.shape[2]

    meta_own = jnp.concatenate([local_target[0, 0], local_source[0, 0], halo_target[0, 0], halo_block[0, 0]])
    stride = meta_own.shape[0]
    meta = jnp.concatenate([meta_own, swap_cores(meta_own)])
    own_local, own_halo = local_tiles[0, 0], halo_tiles[0, 0]
    other_local, other_halo = swap_cores(own_local), swap_cores(own_halo)

    degree_blocks = degree.reshape(blocks, block)
    out_type = jax.ShapeDtypeStruct((peers, packed, LANES), bf16)
    value_type = jax.ShapeDtypeStruct((rows, LANES), bf16)
    half_type = jax.ShapeDtypeStruct((rows // 2, LANES), bf16)
    acc = pltpu.VMEM((rows, LANES), f32)
    sending = [
        pltpu.VMEM((peers * slots, LANES), f32),
        pltpu.VMEM((peers, packed, LANES), bf16),
        pltpu.VMEM((rows, LANES), bf16),
    ]
    peer_sems = pltpu.SemaphoreType.DMA((peers,))

    counts = send_count[0]
    whole_tiles = slots % LANES == 0
    first_rows = send_rows[0] if whole_tiles else send_rows[0].reshape(-1)
    out, value = pl.pallas_call(
        functools.partial(first_kernel, class_half),
        out_shape=(out_type, value_type),
        in_specs=[smem()] * 3 + [vmem() if whole_tiles else smem()] + [vmem()] * 3,
        out_specs=(hbm(), hbm()),
        scratch_shapes=[
            pltpu.VMEM((2 * LANES, batch), f32),
            pltpu.VMEM((batch, LANES), f32),
            acc,
            *sending,
            pltpu.SMEM((peers * slots,), jnp.int32),
            peer_sems,
            peer_sems,
            pltpu.SemaphoreType.DMA((1,)),
        ],
        compiler_params=params(),
        name="first",
    )(core_arg, counts, batch_nodes[0], first_rows, labels, jnp.transpose(batch_logits, (2, 0, 1)), degree_blocks)
    idx = lax.optimization_barrier((send_rows, value))[0].reshape(-1)

    def turn(array, axis):
        low, high = split(array, axis)
        return jnp.where(core == 0, array, jnp.concatenate([high, low], axis))

    values = []
    for hop in range(HOPS):
        last = hop + 1 == HOPS
        values.insert(0, value)
        landed = lax.all_to_all(out, "dom", split_axis=0, concat_axis=0, tiled=True)
        near_values = values if last else values[:1]
        near = pl.pallas_call(
            functools.partial(near_kernel, stride, last),
            out_shape=jax.ShapeDtypeStruct((rows, LANES), f32),
            in_specs=[smem(), vmem(), hbm(), hbm()] + [hbm()] * len(near_values),
            out_specs=hbm(),
            scratch_shapes=[
                pltpu.VMEM((len(near_values), rows, LANES), bf16),
                pltpu.VMEM((local_count, block, block), bf16),
                pltpu.VMEM((local_count, block, block), bf16),
                pltpu.VMEM((rows, LANES), f32),
                pltpu.SemaphoreType.DMA((HOPS + 3,)),
            ],
            compiler_params=params(),
            cost_estimate=pl.CostEstimate(
                flops=4 * local_count * block**3, bytes_accessed=4 * 2**20, transcendentals=0
            ),
            name="near_last" if last else "near",
        )(meta, degree_blocks, own_local, other_local, *near_values)
        if hop == 0:
            x, first_w, second_w, _ = lax.optimization_barrier((features, first_weight, second_weight, value))
            pre_first = jnp.dot(x, turn(first_w, 1), preferred_element_type=f32) + turn(first_bias, 0)
            hidden_first, slope_first = gelu_parts(pre_first)
            second_turned = turn(second_w, 0)
            near, hidden_first, slope_first, second_turned = lax.optimization_barrier(
                (near, hidden_first, slope_first, second_turned)
            )
        if hop == 1:
            tied, _ = lax.optimization_barrier((hidden_first, value))
            pre_second = jnp.dot(tied, second_turned, preferred_element_type=f32)
            near, pre_second = lax.optimization_barrier((near, pre_second))
        if hop == 2:
            tied, _ = lax.optimization_barrier((pre_second, value))
            hidden_second, slope_second = gelu_parts(tied + second_bias)
            near, hidden_second, slope_second = lax.optimization_barrier((near, hidden_second, slope_second))
        if last:
            tied, _ = lax.optimization_barrier((third_weight, value))
            low = jnp.pad(tied[:, :class_half], ((0, 0), (0, LANES - class_half)))
            high = jnp.pad(tied[:, class_half:], ((0, 0), (0, LANES - classes + class_half)))
            third = jnp.where(core == 0, jnp.concatenate([low, high], 1), jnp.concatenate([high, low], 1))
            near, third = lax.optimization_barrier((near, third))
        result = pl.pallas_call(
            functools.partial(far_kernel, slots, class_half, 2 * local_count, stride, last),
            out_shape=(half_type, half_type) if last else (out_type, value_type),
            in_specs=[smem()] * 4 + [vmem()] + [hbm()] * 4,
            out_specs=(vmem(), vmem()) if last else (hbm(), hbm()),
            scratch_shapes=[
                pltpu.VMEM((peers, packed, LANES), bf16),
                pltpu.VMEM((halo_count, block, block), bf16),
                pltpu.VMEM((halo_count, block, block), bf16),
                pltpu.VMEM((peers * slots, LANES), bf16),
                acc,
            ]
            + ([] if last else sending + [peer_sems])
            + [pltpu.SemaphoreType.DMA((5,))],
            compiler_params=params(),
            name="far_last" if last else "far",
        )(core_arg, meta, counts, idx, degree_blocks, landed, own_halo, other_halo, near)
        if last:
            keep, send = result
        else:
            out, value = result

    got = swap_cores(send)
    delta = jnp.concatenate([keep, got], axis=1)

    def contract(a, b):
        return lax.dot_general(a, b, (((0,), (0,)), ((), ())), preferred_element_type=f32).astype(bf16)

    half, feat = hidden // 2, x.shape[1]
    lead = half // 4 * 3
    back_second = lax.dot_general(delta, third, (((1,), (1,)), ((), ())), preferred_element_type=f32)
    second_delta = (slope_second.astype(f32) * back_second).astype(bf16)
    second_bias_grad = jnp.sum(second_delta.astype(f32), axis=0).astype(bf16)
    send_lead = contract(hidden_first[:, half : half + lead], second_delta)
    got_lead = swap_cores(send_lead)
    keep_lead = contract(hidden_first[:, :lead], second_delta)
    send_tail = contract(hidden_first[:, half + lead :], second_delta)
    keep_tail = contract(hidden_first[:, lead:half], second_delta)
    third_grad = contract(delta, hidden_second)
    back_first = lax.dot_general(
        second_delta, second_turned, (((1,), (1,)), ((), ())), preferred_element_type=f32
    )
    first_delta = (slope_first.astype(f32) * back_first).astype(bf16)
    first_grad = contract(x, first_delta)
    first_bias_grad = jnp.sum(first_delta.astype(f32), axis=0).astype(bf16)

    is_first = core == 0
    domains = lax.axis_size("dom")
    column_splits = (hidden // LANES).bit_length() - 1
    grain = 8 * max(1, domains >> column_splits)
    used = half - lead + feat // 2 + class_half
    tail_rows = -(-(used + 1) // grain) * grain

    def bundle(part, tail, third_rows, bias_half):
        at = slice(part * half, (part + 1) * half)
        first_rows = jnp.concatenate([first_grad[: feat // 2, at], first_grad[feat // 2 :, at]], 1)
        bias_row = jnp.concatenate([first_bias_grad[at], bias_half])
        bias = jnp.broadcast_to(bias_row[None], (tail_rows - used, hidden))
        return jnp.concatenate([tail, first_rows, third_rows[:class_half], bias], 0)

    low_bias, high_bias = split(second_bias_grad, 0)
    keep_rest = bundle(0, keep_tail, third_grad[:LANES], jnp.where(is_first, low_bias, high_bias))
    send_rest = bundle(1, send_tail, third_grad[LANES:], jnp.where(is_first, high_bias, low_bias))
    got_rest = swap_cores(send_rest)
    mine_lead = sum_over_domains((keep_lead.astype(f32) + got_lead.astype(f32)).astype(bf16))
    mine_rest = sum_over_domains((keep_rest.astype(f32) + got_rest.astype(f32)).astype(bf16))
    theirs_lead, theirs_rest = swap_cores(mine_lead), swap_cores(mine_rest)
    first_out, first_bias_out, second_out, second_bias_out, third_out = pl.pallas_call(
        functools.partial(finish_kernel, class_half),
        out_shape=(
            jax.ShapeDtypeStruct((feat, hidden), f32),
            jax.ShapeDtypeStruct((1, hidden), f32),
            jax.ShapeDtypeStruct((hidden, hidden), f32),
            jax.ShapeDtypeStruct((1, hidden), f32),
            jax.ShapeDtypeStruct((classes, hidden), f32),
        ),
        in_specs=[smem()] + [vmem()] * 4,
        out_specs=(vmem(), vmem(), hbm(), vmem(), vmem()),
        scratch_shapes=[
            pltpu.VMEM((hidden, hidden), f32),
            pltpu.SemaphoreType.DMA((2 * (half // math.gcd(lead, half)),)),
        ],
        compiler_params=pltpu.CompilerParams(vmem_limit_bytes=24 * 1024 * 1024),
        name="finish",
    )(core_arg, mine_lead, theirs_lead, mine_rest, theirs_rest)
    return first_out, first_bias_out.reshape(hidden), second_out, second_bias_out.reshape(hidden), third_out.T


def solution(mesh):
    return jax.shard_map(
        shards,
        mesh=mesh,
        in_specs=(
            P(("grp", "dom", "col"), None),
            P(),
            P(),
            P(),
            P(),
            P(),
            P(("grp", "dom"), "col", None, None, None),
            P(("grp", "dom"), "col", None),
            P(("grp", "dom"), "col", None),
            P(("grp", "dom"), "col", None, None, None),
            P(("grp", "dom"), "col", None),
            P(("grp", "dom"), "col", None),
            P(("grp", "dom"), None, None),
            P(("grp", "dom"), None),
            P(("grp", "dom")),
            P(("grp", "dom"), None),
            P(("grp", "dom"), None),
            P(("grp", "dom"), None, None),
        ),
        out_specs=(P("grp", None), P("grp"), P("grp", None), P("grp"), P("grp", None)),
        check_vma=False,
    )
```

```python
import functools
import math

import jax
import jax.numpy as jnp
from jax import lax
from jax.experimental import pallas as pl
from jax.experimental.pallas import tpu as pltpu
from jax.sharding import PartitionSpec as P

HOPS = 4
teleport = 0.1
LANES = 128
UNROLL = 16
VMEM_LIMIT = 60 * 1024 * 1024

bf16 = jnp.bfloat16
f32 = jnp.float32


def vmem():
    return pl.BlockSpec(memory_space=pltpu.VMEM)


def smem():
    return pl.BlockSpec(memory_space=pltpu.SMEM)


def hbm():
    return pl.BlockSpec(memory_space=pltpu.HBM)


def params():
    return pltpu.CompilerParams(vmem_limit_bytes=VMEM_LIMIT)


def is_packed(slots, class_half):
    return slots % 64 == 0 and class_half <= 96


def packed_rows(slots, class_half):
    return slots * 3 // 4 if is_packed(slots, class_half) else slots


def send_packed(v_ref, count_ref, idx_ref, stage_ref, packed_ref, out_ref, sems, slots, class_half):
    peers = packed_ref.shape[0]

    def gather(j, carry):
        first = j * slots

        def body(g, inner):
            base = pl.multiple_of(first + g * UNROLL, UNROLL)
            for u in range(UNROLL):
                stage_ref[pl.ds(base + u, 1), :] = v_ref[pl.ds(idx_ref[base + u], 1), :]
            return inner

        return lax.fori_loop(0, (count_ref[j] + (UNROLL - 1)) // UNROLL, body, carry)

    lax.fori_loop(0, peers, gather, 0)
    half, quarter = slots // 2, slots // 4
    row = lax.broadcasted_iota(jnp.int32, (slots, LANES), 0)
    lane_a = lax.broadcasted_iota(jnp.int32, (half, LANES), 1)
    lane_b = lax.broadcasted_iota(jnp.int32, (quarter, LANES), 1) // 32

    def peer(j, carry):
        base = pl.multiple_of(j * slots, slots)
        taken = jnp.where(row < count_ref[j], stage_ref[pl.ds(base, slots), :], 0.0)
        if is_packed(slots, class_half):
            low, high = taken[:half], taken[half:]
            packed_ref[j, 0:half] = jnp.where(lane_a < 64, low, pltpu.roll(high, 64, 1)).astype(bf16)
            parts = (low[:quarter], low[quarter:], high[:quarter], high[quarter:])
            narrow = jnp.zeros((quarter, LANES), f32)
            for g in range(4):
                narrow = jnp.where(lane_b == g, pltpu.roll(parts[g], (g * 32 - 64) % LANES, 1), narrow)
            packed_ref[j, half : half + quarter] = narrow.astype(bf16)
        else:
            packed_ref[j] = taken.astype(bf16)
        pltpu.make_async_copy(packed_ref.at[j], out_ref.at[j], sems.at[j]).start()
        return carry

    lax.fori_loop(0, peers, peer, 0)


def wait_packed(packed_ref, out_ref, sems):
    def peer(j, carry):
        pltpu.make_async_copy(packed_ref.at[j], out_ref.at[j], sems.at[j]).wait()
        return carry

    lax.fori_loop(0, packed_ref.shape[0], peer, 0)


def unpack_rows(recv_ref, rows_ref, slots, class_half):
    peers = recv_ref.shape[0]
    if not is_packed(slots, class_half):

        def plain(j, carry):
            rows_ref[pl.ds(pl.multiple_of(j * slots, slots), slots), :] = recv_ref[j]
            return carry

        lax.fori_loop(0, peers, plain, 0)
        return
    half, quarter = slots // 2, slots // 4
    lane = lax.broadcasted_iota(jnp.int32, (quarter, LANES), 1)

    def body(j, carry):
        base = pl.multiple_of(j * slots, slots)
        wide = recv_ref[j, 0:half].astype(f32)
        narrow = recv_ref[j, half : half + quarter].astype(f32)
        turned = pltpu.roll(wide, 64, 1)
        fronts = (wide[:quarter], wide[quarter:], turned[:quarter], turned[quarter:])
        for g in range(4):
            back = pltpu.roll(narrow, (64 - g * 32) % LANES, 1)
            back = jnp.where(lane < 96, back, 0.0)
            rows_ref[pl.ds(base + g * quarter, quarter), :] = jnp.where(
                lane < 64, fronts[g], back
            ).astype(bf16)
        return carry

    lax.fori_loop(0, peers, body, 0)


def root_columns(degree_ref, function):
    blocks, block = degree_ref.shape
    values = function(degree_ref[...].astype(f32))
    return jnp.transpose(jnp.concatenate([values, jnp.zeros((block - blocks, block), f32)], 0))


def over_lanes(columns, b):
    return jnp.broadcast_to(columns[:, b : b + 1], columns.shape)


def first_kernel(class_half, core_ref, count_ref, nodes_ref, rows_ref, labels_ref, logits_ref, degree_ref,
                 out_ref, value_ref, wide_ref, diff_ref, v_ref, stage_ref, packed_ref, value_v, idx_ref, idx_sems,
                 sems, own_sems):
    classes, unused, batch = logits_ref.shape
    peers = packed_ref.shape[0]
    slots = stage_ref.shape[0] // peers
    flat = []
    if rows_ref.ndim == 1:
        idx_ref = rows_ref
    else:
        for j in range(peers):
            to = idx_ref.at[pl.ds(j * slots, slots)]
            flat.append(pltpu.make_async_copy(rows_ref.at[j], to, idx_sems.at[j]))
    for copy in flat:
        copy.start()
    blocks, block = degree_ref.shape
    core = core_ref[0]
    logits = logits_ref[...].reshape(classes, batch)
    shifted = jnp.exp(logits - jnp.max(logits, axis=0, keepdims=True))
    hot = lax.broadcasted_iota(jnp.int32, (classes, batch), 0) == labels_ref[...]
    probs = shifted / jnp.sum(shifted, axis=0, keepdims=True)
    wide_ref[...] = jnp.zeros_like(wide_ref)
    wide_ref[0:classes, :] = probs - jnp.where(hot, 1.0, 0.0)
    chosen = wide_ref[pl.ds(pl.multiple_of(core * class_half, 8), LANES), :]
    lane = lax.broadcasted_iota(jnp.int32, (batch, LANES), 1)
    diff_ref[...] = jnp.where(lane < class_half, jnp.transpose(chosen), 0.0)
    v_ref[...] = jnp.zeros_like(v_ref)

    def add_row(i, carry):
        at = pl.ds(nodes_ref[i], 1)
        v_ref[at, :] = v_ref[at, :] + diff_ref[pl.ds(i, 1), :]
        return carry

    lax.fori_loop(0, batch, add_row, 0, unroll=8)
    roots = root_columns(degree_ref, lax.rsqrt)
    for b in range(blocks):
        at = slice(b * block, (b + 1) * block)
        scaled = over_lanes(roots, b) * v_ref[at, :]
        value_v[at, :] = scaled.astype(bf16)
        v_ref[at, :] = scaled
    value_copy = pltpu.make_async_copy(value_v, value_ref, own_sems.at[0])
    value_copy.start()
    for copy in flat:
        copy.wait()
    send_packed(v_ref, count_ref, idx_ref, stage_ref, packed_ref, out_ref, sems, slots, class_half)
    value_copy.wait()
    wait_packed(packed_ref, out_ref, sems)


def add_tiles(acc_ref, source_ref, tile_refs, meta_ref, target_base, source_base, stride):
    count, block = tile_refs[0].shape[0], tile_refs[0].shape[1]
    for which, tiles in enumerate(tile_refs):
        for t in range(count):
            target = meta_ref[which * stride + target_base + t]
            source = meta_ref[which * stride + source_base + t]
            product = jnp.dot(
                tiles[t],
                source_ref[pl.ds(pl.multiple_of(source * block, block), block), :],
                preferred_element_type=f32,
            )
            at = pl.ds(pl.multiple_of(target * block, block), block)
            acc_ref[at, :] = acc_ref[at, :] + product


def near_kernel(stride, last, meta_ref, degree_ref, own_ref, other_ref, *rest):
    count = own_ref.shape[0]
    values = 1 if not last else HOPS
    value_refs, rest = rest[:values], rest[values:]
    near_ref, value_vs, own_v, other_v, acc_ref, near_v, sems = rest
    copies = [pltpu.make_async_copy(value_refs[i], value_vs.at[i], sems.at[i]) for i in range(values)]
    copies.append(pltpu.make_async_copy(own_ref, own_v, sems.at[HOPS]))
    copies.append(pltpu.make_async_copy(other_ref, other_v, sems.at[HOPS + 1]))
    for copy in copies:
        copy.start()
    blocks, block = degree_ref.shape
    acc_ref[...] = jnp.zeros_like(acc_ref)
    for copy in copies:
        copy.wait()
    add_tiles(acc_ref, value_vs.at[0], (own_v, other_v), meta_ref, 0, count, stride)
    columns = root_columns(degree_ref, lambda degree: (teleport / (1.0 - teleport)) * degree) if last else None
    outs = []
    parts = 4 if blocks % 4 == 0 else 1
    for b in range(blocks):
        at = slice(b * block, (b + 1) * block)
        near = acc_ref[at, :]
        if last:
            total = value_vs[0, at, :].astype(f32)
            for i in range(1, values):
                total = total + value_vs[i, at, :].astype(f32)
            near = near + over_lanes(columns, b) * total
        near_v[at, :] = near.astype(bf16)
        if (b + 1) % (blocks // parts) == 0:
            part = (b + 1) // (blocks // parts) - 1
            span = blocks // parts * block
            here = pl.ds(part * span, span)
            outs.append(pltpu.make_async_copy(near_v.at[here], near_ref.at[here], sems.at[HOPS + 2 + part]))
            outs[-1].start()
    for out in outs:
        out.wait()


def far_kernel(slots, class_half, base, stride, last, core_ref, meta_ref, count_ref, idx_ref, degree_ref, recv_ref,
               own_ref, other_ref, near_ref, *rest):
    if last:
        keep_ref, send_ref, recv_v, own_v, other_v, near_v, rows_ref, acc_ref, own_sems = rest
    else:
        (out_ref, value_ref, recv_v, own_v, other_v, near_v, rows_ref, acc_ref, stage_ref, packed_ref, value_v, sems,
         own_sems) = rest
    count, block = own_ref.shape[0], own_ref.shape[1]
    blocks = degree_ref.shape[0]
    copies = [
        pltpu.make_async_copy(recv_ref, recv_v, own_sems.at[0]),
        pltpu.make_async_copy(own_ref, own_v, own_sems.at[1]),
        pltpu.make_async_copy(other_ref, other_v, own_sems.at[2]),
        pltpu.make_async_copy(near_ref, near_v, own_sems.at[3]),
    ]
    for copy in copies:
        copy.start()
    roots = root_columns(degree_ref, lax.rsqrt)
    acc_ref[...] = jnp.zeros_like(acc_ref)
    copies[0].wait()
    unpack_rows(recv_v, rows_ref, slots, class_half)
    for copy in copies[1:]:
        copy.wait()
    add_tiles(acc_ref, rows_ref, (own_v, other_v), meta_ref, base, base + count, stride)
    rate = 1.0 - teleport
    if last:
        half_blocks = blocks // 2
        core = core_ref[0]
        for b in range(half_blocks):
            to = slice(b * block, (b + 1) * block)
            outs = []
            for b_at in (b, half_blocks + b):
                at = slice(b_at * block, (b_at + 1) * block)
                outs.append((rate * over_lanes(roots, b_at) * (acc_ref[at, :] + near_v[at, :].astype(f32))).astype(bf16))
            keep_ref[to, :] = jnp.where(core == 0, outs[0], outs[1])
            send_ref[to, :] = jnp.where(core == 0, outs[1], outs[0])
        return
    for b in range(blocks):
        at = slice(b * block, (b + 1) * block)
        root = over_lanes(roots, b)
        scaled = (rate * root * root) * (acc_ref[at, :] + near_v[at, :].astype(f32))
        value_v[at, :] = scaled.astype(bf16)
        acc_ref[at, :] = scaled
    value_copy = pltpu.make_async_copy(value_v, value_ref, own_sems.at[4])
    value_copy.start()
    send_packed(acc_ref, count_ref, idx_ref, stage_ref, packed_ref, out_ref, sems, slots, class_half)
    value_copy.wait()
    wait_packed(packed_ref, out_ref, sems)


def finish_kernel(class_half, core_ref, mine_one, theirs_one, mine_two, theirs_two, first_ref, first_bias_ref,
                  second_ref, second_bias_ref, third_ref, wide_v, out_sems):
    one = mine_one.shape[0]
    hidden = second_ref.shape[0]
    feat = first_ref.shape[0]
    classes = third_ref.shape[0]
    half, feat_half = hidden // 2, feat // 2
    is_first = core_ref[0] == 0

    def both(start, count):
        mine_ref, theirs_ref = (mine_one, theirs_one) if start < one else (mine_two, theirs_two)
        at = start if start < one else start - one
        mine = mine_ref[at : at + count, :].astype(f32)
        theirs = theirs_ref[at : at + count, :].astype(f32)
        return jnp.where(is_first, mine, theirs), jnp.where(is_first, theirs, mine)

    step = math.gcd(one, half)
    outs = []
    for start in range(0, half, step):
        for k, value in enumerate(both(start, step)):
            at = k * half + start
            wide_v[at : at + step, :] = value
            out = pltpu.make_async_copy(
                wide_v.at[pl.ds(at, step)], second_ref.at[pl.ds(at, step)], out_sems.at[2 * (start // step) + k]
            )
            out.start()
            outs.append(out)
    low, high = both(half + feat_half, class_half)
    third_ref[0:class_half, :] = low
    third_ref[class_half:classes, :] = high[: classes - class_half]
    firsts = both(half, feat_half)
    biases = both(half + feat_half + class_half, 8)
    for k in range(2):
        at = slice(k * half, (k + 1) * half)
        first_ref[0:feat_half, at] = firsts[k][:, :half]
        first_ref[feat_half:feat, at] = firsts[k][:, half:]
        first_bias_ref[:, at] = biases[k][:1, :half]
        second_bias_ref[:, at] = biases[k][:1, half:]
    for out in outs:
        out.wait()


def gelu_parts(x):
    k = math.sqrt(2.0 / math.pi)
    square = x * x
    t = jnp.tanh(x * (k + (k * 0.044715) * square))
    half_up = 0.5 + 0.5 * t
    slope = half_up + (0.5 * x) * (1.0 - t * t) * (k + (3.0 * k * 0.044715) * square)
    return (x * half_up).astype(bf16), slope.astype(bf16)


def swap_cores(x):
    return lax.ppermute(x, "col", [(0, 1), (1, 0)])


def exchange(x, first_step, second_step):
    domains, cores = lax.axis_size("dom"), lax.axis_size("col")
    steps = (first_step, second_step)
    pairs = [
        (d * cores + c, (d ^ steps[c]) * cores + c) for d in range(domains) for c in range(cores)
    ]
    return lax.ppermute(x, ("dom", "col"), pairs)


def halving_steps():
    domains = lax.axis_size("dom")
    bits = [1 << b for b in range(domains.bit_length() - 1)]
    other = list(bits)
    if len(bits) > 1:
        other[0], other[1] = other[1], other[0]
    return list(zip(bits, other))


def split(x, axis):
    half = x.shape[axis] // 2
    return lax.slice_in_dim(x, 0, half, axis=axis), lax.slice_in_dim(x, half, 2 * half, axis=axis)


def halving_plan(shape):
    me, core = lax.axis_index("dom"), lax.axis_index("col")
    plan, width = [], shape[1]
    for a, b in halving_steps():
        plan.append((a, b, 1 if width > LANES else 0, jnp.where(core == 0, me & a, me & b) != 0))
        width = width // 2 if width > LANES else width
    return plan


def halves_of(x, step):
    low, high = split(x, step[2])
    return jnp.where(step[3], high, low), jnp.where(step[3], low, high)


def sum_over_domains(keep, send, plan):
    for i, (a, b, axis, up) in enumerate(plan):
        got = exchange(send, a, b)
        current = (keep.astype(f32) + got.astype(f32)).astype(bf16)
        if i + 1 < len(plan):
            keep, send = halves_of(current, plan[i + 1])
    for a, b, axis, up in plan[::-1]:
        got = exchange(current, a, b)
        current = jnp.where(
            up,
            jnp.concatenate([got, current], axis),
            jnp.concatenate([current, got], axis),
        )
    return current


def shards(
    features,
    first_weight,
    first_bias,
    second_weight,
    second_bias,
    third_weight,
    local_tiles,
    local_target,
    local_source,
    halo_tiles,
    halo_target,
    halo_block,
    send_rows,
    send_count,
    degree,
    batch_nodes,
    labels,
    batch_logits,
):
    rows = degree.shape[0]
    classes = batch_logits.shape[-1]
    batch = batch_logits.shape[1]
    block = local_tiles.shape[-1]
    blocks = rows // block
    peers, slots = send_rows.shape[1], send_rows.shape[2]
    hidden = second_weight.shape[0]
    class_half = (classes // 2 + 7) // 8 * 8
    core = lax.axis_index("col").astype(jnp.int32)
    core_arg = core.reshape(1)
    packed = packed_rows(slots, class_half)
    local_count, halo_count = local_tiles.shape[2], halo_tiles.shape[2]

    stride = 2 * (local_count + halo_count)
    degree_blocks = degree.reshape(blocks, block)
    out_type = jax.ShapeDtypeStruct((peers, packed, LANES), bf16)
    value_type = jax.ShapeDtypeStruct((rows, LANES), bf16)
    half_type = jax.ShapeDtypeStruct((rows // 2, LANES), bf16)
    acc = pltpu.VMEM((rows, LANES), f32)
    sending = [
        pltpu.VMEM((peers * slots, LANES), f32),
        pltpu.VMEM((peers, packed, LANES), bf16),
        pltpu.VMEM((rows, LANES), bf16),
    ]
    peer_sems = pltpu.SemaphoreType.DMA((peers,))

    counts = send_count[0]
    whole_tiles = slots % LANES == 0
    first_rows = send_rows[0] if whole_tiles else send_rows[0].reshape(-1)
    out, value = pl.pallas_call(
        functools.partial(first_kernel, class_half),
        out_shape=(out_type, value_type),
        in_specs=[smem()] * 3 + [vmem() if whole_tiles else smem()] + [vmem()] * 3,
        out_specs=(hbm(), hbm()),
        scratch_shapes=[
            pltpu.VMEM((2 * LANES, batch), f32),
            pltpu.VMEM((batch, LANES), f32),
            acc,
            *sending,
            pltpu.SMEM((peers * slots,), jnp.int32),
            peer_sems,
            peer_sems,
            pltpu.SemaphoreType.DMA((1,)),
        ],
        compiler_params=params(),
        name="first",
    )(core_arg, counts, batch_nodes[0], first_rows, labels, jnp.transpose(batch_logits, (2, 0, 1)), degree_blocks)
    tied_rows, *lists, _ = lax.optimization_barrier(
        (send_rows, local_target, local_source, halo_target, halo_block, value)
    )
    idx = tied_rows.reshape(-1)
    meta_own = jnp.concatenate([part[0, 0] for part in lists])
    meta = jnp.concatenate([meta_own, swap_cores(meta_own)])
    own_local, own_halo = local_tiles[0, 0], halo_tiles[0, 0]
    other_local, other_halo = swap_cores(own_local), swap_cores(own_halo)

    def turn(array, axis):
        low, high = split(array, axis)
        return jnp.where(core == 0, array, jnp.concatenate([high, low], axis))

    values = []
    for hop in range(HOPS):
        last = hop + 1 == HOPS
        values.insert(0, value)
        landed = lax.all_to_all(out, "dom", split_axis=0, concat_axis=0, tiled=True)
        near_values = values if last else values[:1]
        near = pl.pallas_call(
            functools.partial(near_kernel, stride, last),
            out_shape=value_type,
            in_specs=[smem(), vmem(), hbm(), hbm()] + [hbm()] * len(near_values),
            out_specs=hbm(),
            scratch_shapes=[
                pltpu.VMEM((len(near_values), rows, LANES), bf16),
                pltpu.VMEM((local_count, block, block), bf16),
                pltpu.VMEM((local_count, block, block), bf16),
                pltpu.VMEM((rows, LANES), f32),
                pltpu.VMEM((rows, LANES), bf16),
                pltpu.SemaphoreType.DMA((HOPS + 6,)),
            ],
            compiler_params=params(),
            cost_estimate=pl.CostEstimate(
                flops=4 * local_count * block**3, bytes_accessed=4 * 2**20, transcendentals=0
            ),
            name="near_last" if last else "near",
        )(meta, degree_blocks, own_local, other_local, *near_values)
        if hop == 0:
            first_w, first_b, second_w, _ = lax.optimization_barrier(
                (first_weight, first_bias, second_weight, value)
            )
            first_turned, bias_turned, second_turned = turn(first_w, 1), turn(first_b, 0), turn(second_w, 0)
            near, first_turned, bias_turned, second_turned = lax.optimization_barrier(
                (near, first_turned, bias_turned, second_turned)
            )
        if hop == 1:
            x, _ = lax.optimization_barrier((features, value))
            pre_first = jnp.dot(x, first_turned, preferred_element_type=f32) + bias_turned
            hidden_first, slope_first = gelu_parts(pre_first)
            near, hidden_first, slope_first = lax.optimization_barrier((near, hidden_first, slope_first))
        if hop == 2:
            tied, _ = lax.optimization_barrier((hidden_first, value))
            pre_second = jnp.dot(tied, second_turned, preferred_element_type=f32) + second_bias
            hidden_second, slope_second = gelu_parts(pre_second)
            near, hidden_second, slope_second = lax.optimization_barrier((near, hidden_second, slope_second))
        if last:
            tied, _ = lax.optimization_barrier((third_weight, value))
            low = jnp.pad(tied[:, :class_half], ((0, 0), (0, LANES - class_half)))
            high = jnp.pad(tied[:, class_half:], ((0, 0), (0, LANES - classes + class_half)))
            third = jnp.where(core == 0, jnp.concatenate([low, high], 1), jnp.concatenate([high, low], 1))
            near, third = lax.optimization_barrier((near, third))
        result = pl.pallas_call(
            functools.partial(far_kernel, slots, class_half, 2 * local_count, stride, last),
            out_shape=(half_type, half_type) if last else (out_type, value_type),
            in_specs=[smem()] * 4 + [vmem()] + [hbm()] * 4,
            out_specs=(vmem(), vmem()) if last else (hbm(), hbm()),
            scratch_shapes=[
                pltpu.VMEM((peers, packed, LANES), bf16),
                pltpu.VMEM((halo_count, block, block), bf16),
                pltpu.VMEM((halo_count, block, block), bf16),
                pltpu.VMEM((rows, LANES), bf16),
                pltpu.VMEM((peers * slots, LANES), bf16),
                acc,
            ]
            + ([] if last else sending + [peer_sems])
            + [pltpu.SemaphoreType.DMA((5,))],
            compiler_params=params(),
            name="far_last" if last else "far",
        )(core_arg, meta, counts, idx, degree_blocks, landed, own_halo, other_halo, near)
        if last:
            keep, send = result
        else:
            out, value = result

    got = swap_cores(send)
    delta = jnp.concatenate([keep, got], axis=1)

    def contract(a, b):
        return lax.dot_general(a, b, (((0,), (0,)), ((), ())), preferred_element_type=f32).astype(bf16)

    half, feat = hidden // 2, x.shape[1]
    lead = half // 4 * 3
    back_second = lax.dot_general(delta, third, (((1,), (1,)), ((), ())), preferred_element_type=f32)
    second_delta = (slope_second.astype(f32) * back_second).astype(bf16)
    second_bias_grad = jnp.sum(second_delta.astype(f32), axis=0).astype(bf16)
    send_lead = contract(hidden_first[:, half : half + lead], second_delta)
    got_lead = swap_cores(send_lead)
    keep_lead = contract(hidden_first[:, :lead], second_delta)
    lead_plan = halving_plan(keep_lead.shape)
    lead_keep, lead_send = halves_of((keep_lead.astype(f32) + got_lead.astype(f32)).astype(bf16), lead_plan[0])
    lead_send, lead_keep, second_delta, delta = lax.optimization_barrier((lead_send, lead_keep, second_delta, delta))
    send_tail = contract(hidden_first[:, half + lead :], second_delta)
    keep_tail = contract(hidden_first[:, lead:half], second_delta)
    third_grad = contract(delta, hidden_second)
    back_first = lax.dot_general(
        second_delta, second_turned, (((1,), (1,)), ((), ())), preferred_element_type=f32
    )
    first_delta = (slope_first.astype(f32) * back_first).astype(bf16)
    first_grad = contract(x, first_delta)
    first_bias_grad = jnp.sum(first_delta.astype(f32), axis=0).astype(bf16)

    is_first = core == 0
    domains = lax.axis_size("dom")
    column_splits = (hidden // LANES).bit_length() - 1
    grain = 8 * max(1, domains >> column_splits)
    used = half - lead + feat // 2 + class_half
    tail_rows = -(-(used + 1) // grain) * grain

    def bundle(part, tail, third_rows, bias_half):
        at = slice(part * half, (part + 1) * half)
        first_rows = jnp.concatenate([first_grad[: feat // 2, at], first_grad[feat // 2 :, at]], 1)
        bias_row = jnp.concatenate([first_bias_grad[at], bias_half])
        bias = jnp.broadcast_to(bias_row[None], (tail_rows - used, hidden))
        return jnp.concatenate([tail, first_rows, third_rows[:class_half], bias], 0)

    low_bias, high_bias = split(second_bias_grad, 0)
    keep_rest = bundle(0, keep_tail, third_grad[:LANES], jnp.where(is_first, low_bias, high_bias))
    send_rest = bundle(1, send_tail, third_grad[LANES:], jnp.where(is_first, high_bias, low_bias))
    got_rest = swap_cores(send_rest)
    mine_lead = sum_over_domains(lead_keep, lead_send, lead_plan)
    rest_plan = halving_plan(keep_rest.shape)
    rest = (keep_rest.astype(f32) + got_rest.astype(f32)).astype(bf16)
    mine_rest = sum_over_domains(*halves_of(rest, rest_plan[0]), rest_plan)
    theirs_lead, theirs_rest = swap_cores(mine_lead), swap_cores(mine_rest)
    first_out, first_bias_out, second_out, second_bias_out, third_out = pl.pallas_call(
        functools.partial(finish_kernel, class_half),
        out_shape=(
            jax.ShapeDtypeStruct((feat, hidden), f32),
            jax.ShapeDtypeStruct((1, hidden), f32),
            jax.ShapeDtypeStruct((hidden, hidden), f32),
            jax.ShapeDtypeStruct((1, hidden), f32),
            jax.ShapeDtypeStruct((classes, hidden), f32),
        ),
        in_specs=[smem()] + [vmem()] * 4,
        out_specs=(vmem(), vmem(), hbm(), vmem(), vmem()),
        scratch_shapes=[
            pltpu.VMEM((hidden, hidden), f32),
            pltpu.SemaphoreType.DMA((2 * (half // math.gcd(lead, half)),)),
        ],
        compiler_params=pltpu.CompilerParams(vmem_limit_bytes=24 * 1024 * 1024),
        name="finish",
    )(core_arg, mine_lead, theirs_lead, mine_rest, theirs_rest)
    return first_out, first_bias_out.reshape(hidden), second_out, second_bias_out.reshape(hidden), third_out.T


def solution(mesh):
    return jax.shard_map(
        shards,
        mesh=mesh,
        in_specs=(
            P(("grp", "dom", "col"), None),
            P(),
            P(),
            P(),
            P(),
            P(),
            P(("grp", "dom"), "col", None, None, None),
            P(("grp", "dom"), "col", None),
            P(("grp", "dom"), "col", None),
            P(("grp", "dom"), "col", None, None, None),
            P(("grp", "dom"), "col", None),
            P(("grp", "dom"), "col", None),
            P(("grp", "dom"), None, None),
            P(("grp", "dom"), None),
            P(("grp", "dom")),
            P(("grp", "dom"), None),
            P(("grp", "dom"), None),
            P(("grp", "dom"), None, None),
        ),
        out_specs=(P("grp", None), P("grp"), P("grp", None), P("grp"), P("grp", None)),
        check_vma=False,
    )
```

```python
import functools
import math

import jax
import jax.numpy as jnp
from jax import lax
from jax.experimental import pallas as pl
from jax.experimental.pallas import tpu as pltpu
from jax.sharding import PartitionSpec as P

HOPS = 4
teleport = 0.1
LANES = 128
UNROLL = 16
VMEM_LIMIT = 60 * 1024 * 1024

bf16 = jnp.bfloat16
f32 = jnp.float32


def vmem():
    return pl.BlockSpec(memory_space=pltpu.VMEM)


def smem():
    return pl.BlockSpec(memory_space=pltpu.SMEM)


def hbm():
    return pl.BlockSpec(memory_space=pltpu.HBM)


def params():
    return pltpu.CompilerParams(vmem_limit_bytes=VMEM_LIMIT)


def is_packed(slots, class_half):
    return slots % 64 == 0 and class_half <= 96


def packed_rows(slots, class_half):
    return slots * 3 // 4 if is_packed(slots, class_half) else slots


def send_packed(v_ref, count_ref, idx_ref, stage_ref, packed_ref, out_ref, sems, slots, class_half):
    peers = packed_ref.shape[0]

    def gather(j, carry):
        first = j * slots

        def body(g, inner):
            base = pl.multiple_of(first + g * UNROLL, UNROLL)
            for u in range(UNROLL):
                stage_ref[pl.ds(base + u, 1), :] = v_ref[pl.ds(idx_ref[base + u], 1), :]
            return inner

        return lax.fori_loop(0, (count_ref[j] + (UNROLL - 1)) // UNROLL, body, carry)

    lax.fori_loop(0, peers, gather, 0)
    half, quarter = slots // 2, slots // 4
    row = lax.broadcasted_iota(jnp.int32, (slots, LANES), 0)
    lane_a = lax.broadcasted_iota(jnp.int32, (half, LANES), 1)
    lane_b = lax.broadcasted_iota(jnp.int32, (quarter, LANES), 1) // 32

    def peer(j, carry):
        base = pl.multiple_of(j * slots, slots)
        taken = jnp.where(row < count_ref[j], stage_ref[pl.ds(base, slots), :], 0.0)
        if is_packed(slots, class_half):
            low, high = taken[:half], taken[half:]
            packed_ref[j, 0:half] = jnp.where(lane_a < 64, low, pltpu.roll(high, 64, 1)).astype(bf16)
            parts = (low[:quarter], low[quarter:], high[:quarter], high[quarter:])
            narrow = jnp.zeros((quarter, LANES), f32)
            for g in range(4):
                narrow = jnp.where(lane_b == g, pltpu.roll(parts[g], (g * 32 - 64) % LANES, 1), narrow)
            packed_ref[j, half : half + quarter] = narrow.astype(bf16)
        else:
            packed_ref[j] = taken.astype(bf16)
        pltpu.make_async_copy(packed_ref.at[j], out_ref.at[j], sems.at[j]).start()
        return carry

    lax.fori_loop(0, peers, peer, 0)


def wait_packed(packed_ref, out_ref, sems):
    def peer(j, carry):
        pltpu.make_async_copy(packed_ref.at[j], out_ref.at[j], sems.at[j]).wait()
        return carry

    lax.fori_loop(0, packed_ref.shape[0], peer, 0)


def unpack_rows(recv_ref, rows_ref, slots, class_half):
    peers = recv_ref.shape[0]
    if not is_packed(slots, class_half):

        def plain(j, carry):
            rows_ref[pl.ds(pl.multiple_of(j * slots, slots), slots), :] = recv_ref[j]
            return carry

        lax.fori_loop(0, peers, plain, 0)
        return
    half, quarter = slots // 2, slots // 4
    lane = lax.broadcasted_iota(jnp.int32, (quarter, LANES), 1)

    def body(j, carry):
        base = pl.multiple_of(j * slots, slots)
        wide = recv_ref[j, 0:half].astype(f32)
        narrow = recv_ref[j, half : half + quarter].astype(f32)
        turned = pltpu.roll(wide, 64, 1)
        fronts = (wide[:quarter], wide[quarter:], turned[:quarter], turned[quarter:])
        for g in range(4):
            back = pltpu.roll(narrow, (64 - g * 32) % LANES, 1)
            back = jnp.where(lane < 96, back, 0.0)
            rows_ref[pl.ds(base + g * quarter, quarter), :] = jnp.where(
                lane < 64, fronts[g], back
            ).astype(bf16)
        return carry

    lax.fori_loop(0, peers, body, 0)


def root_columns(degree_ref, function):
    blocks, block = degree_ref.shape
    values = function(degree_ref[...].astype(f32))
    return jnp.transpose(jnp.concatenate([values, jnp.zeros((block - blocks, block), f32)], 0))


def over_lanes(columns, b):
    return jnp.broadcast_to(columns[:, b : b + 1], columns.shape)


def first_kernel(class_half, core_ref, count_ref, nodes_ref, rows_ref, labels_ref, logits_ref, degree_ref,
                 out_ref, value_ref, wide_ref, diff_ref, v_ref, stage_ref, packed_ref, value_v, idx_ref, idx_sems,
                 sems, own_sems):
    classes, unused, batch = logits_ref.shape
    peers = packed_ref.shape[0]
    slots = stage_ref.shape[0] // peers
    flat = []
    if rows_ref.ndim == 1:
        idx_ref = rows_ref
    else:
        for j in range(peers):
            to = idx_ref.at[pl.ds(j * slots, slots)]
            flat.append(pltpu.make_async_copy(rows_ref.at[j], to, idx_sems.at[j]))
    for copy in flat:
        copy.start()
    blocks, block = degree_ref.shape
    core = core_ref[0]
    logits = logits_ref[...].reshape(classes, batch)
    shifted = jnp.exp(logits - jnp.max(logits, axis=0, keepdims=True))
    hot = lax.broadcasted_iota(jnp.int32, (classes, batch), 0) == labels_ref[...]
    probs = shifted / jnp.sum(shifted, axis=0, keepdims=True)
    wide_ref[...] = jnp.zeros_like(wide_ref)
    wide_ref[0:classes, :] = probs - jnp.where(hot, 1.0, 0.0)
    chosen = wide_ref[pl.ds(pl.multiple_of(core * class_half, 8), LANES), :]
    lane = lax.broadcasted_iota(jnp.int32, (batch, LANES), 1)
    diff_ref[...] = jnp.where(lane < class_half, jnp.transpose(chosen), 0.0)
    v_ref[...] = jnp.zeros_like(v_ref)

    def add_row(i, carry):
        at = pl.ds(nodes_ref[i], 1)
        v_ref[at, :] = v_ref[at, :] + diff_ref[pl.ds(i, 1), :]
        return carry

    lax.fori_loop(0, batch, add_row, 0, unroll=8)
    roots = root_columns(degree_ref, lax.rsqrt)
    for b in range(blocks):
        at = slice(b * block, (b + 1) * block)
        scaled = over_lanes(roots, b) * v_ref[at, :]
        value_v[at, :] = scaled.astype(bf16)
        v_ref[at, :] = scaled
    value_copy = pltpu.make_async_copy(value_v, value_ref, own_sems.at[0])
    value_copy.start()
    for copy in flat:
        copy.wait()
    send_packed(v_ref, count_ref, idx_ref, stage_ref, packed_ref, out_ref, sems, slots, class_half)
    value_copy.wait()
    wait_packed(packed_ref, out_ref, sems)


def add_tiles(acc_ref, source_ref, tile_refs, meta_ref, target_base, source_base, stride):
    count, block = tile_refs[0].shape[0], tile_refs[0].shape[1]
    for which, tiles in enumerate(tile_refs):
        for t in range(count):
            target = meta_ref[which * stride + target_base + t]
            source = meta_ref[which * stride + source_base + t]
            product = jnp.dot(
                tiles[t],
                source_ref[pl.ds(pl.multiple_of(source * block, block), block), :],
                preferred_element_type=f32,
            )
            at = pl.ds(pl.multiple_of(target * block, block), block)
            acc_ref[at, :] = acc_ref[at, :] + product


def far_kernel(slots, class_half, stride, last, core_ref, meta_ref, count_ref, idx_ref, degree_ref, recv_ref,
               own_halo_ref, other_halo_ref, value_in_ref, own_local_ref, other_local_ref, *rest):
    if last:
        total_ref, keep_ref, send_ref, recv_v, tiles_v, value_in_v, rows_ref, acc_ref, total_v, own_sems = rest
    else:
        (out_ref, value_ref, recv_v, tiles_v, value_in_v, rows_ref, acc_ref, stage_ref, packed_ref, value_v, sems,
         own_sems) = rest
    local_count, block = own_local_ref.shape[0], own_local_ref.shape[1]
    halo_count = own_halo_ref.shape[0]
    blocks = degree_ref.shape[0]
    tiles = []
    start = 0
    for ref in (own_local_ref, other_local_ref, own_halo_ref, other_halo_ref):
        tiles.append(tiles_v.at[pl.ds(start, ref.shape[0])])
        start += ref.shape[0]
    copies = [
        pltpu.make_async_copy(value_in_ref, value_in_v, own_sems.at[0]),
        pltpu.make_async_copy(own_local_ref, tiles[0], own_sems.at[1]),
        pltpu.make_async_copy(other_local_ref, tiles[1], own_sems.at[2]),
        pltpu.make_async_copy(recv_ref, recv_v, own_sems.at[3]),
        pltpu.make_async_copy(own_halo_ref, tiles[2], own_sems.at[4]),
        pltpu.make_async_copy(other_halo_ref, tiles[3], own_sems.at[5]),
    ]
    for copy in copies:
        copy.start()
    if last:
        total_copy = pltpu.make_async_copy(total_ref, total_v, own_sems.at[6])
        total_copy.start()
    roots = root_columns(degree_ref, lax.rsqrt)
    if last:
        columns = root_columns(degree_ref, lambda degree: (teleport / (1.0 - teleport)) * degree)
        total_copy.wait()
        copies[0].wait()
        for b in range(blocks):
            at = slice(b * block, (b + 1) * block)
            total = total_v[at, :].astype(f32) + value_in_v[at, :].astype(f32)
            acc_ref[at, :] = over_lanes(columns, b) * total
    else:
        acc_ref[...] = jnp.zeros_like(acc_ref)
        copies[0].wait()
    for copy in copies[1:3]:
        copy.wait()
    add_tiles(acc_ref, value_in_v, (tiles[0], tiles[1]), meta_ref, 0, local_count, stride)
    copies[3].wait()
    unpack_rows(recv_v, rows_ref, slots, class_half)
    for copy in copies[4:]:
        copy.wait()
    base = 2 * local_count
    add_tiles(acc_ref, rows_ref, (tiles[2], tiles[3]), meta_ref, base, base + halo_count, stride)
    rate = 1.0 - teleport
    if last:
        half_blocks = blocks // 2
        core = core_ref[0]
        for b in range(half_blocks):
            to = slice(b * block, (b + 1) * block)
            outs = []
            for b_at in (b, half_blocks + b):
                at = slice(b_at * block, (b_at + 1) * block)
                outs.append((rate * over_lanes(roots, b_at) * acc_ref[at, :]).astype(bf16))
            keep_ref[to, :] = jnp.where(core == 0, outs[0], outs[1])
            send_ref[to, :] = jnp.where(core == 0, outs[1], outs[0])
        return
    for b in range(blocks):
        at = slice(b * block, (b + 1) * block)
        root = over_lanes(roots, b)
        scaled = (rate * root * root) * acc_ref[at, :]
        value_v[at, :] = scaled.astype(bf16)
        acc_ref[at, :] = scaled
    value_copy = pltpu.make_async_copy(value_v, value_ref, own_sems.at[6])
    value_copy.start()
    send_packed(acc_ref, count_ref, idx_ref, stage_ref, packed_ref, out_ref, sems, slots, class_half)
    value_copy.wait()
    wait_packed(packed_ref, out_ref, sems)


def finish_kernel(class_half, core_ref, mine_one, theirs_one, mine_two, theirs_two, first_ref, first_bias_ref,
                  second_ref, second_bias_ref, third_ref, wide_v, out_sems):
    one = mine_one.shape[0]
    hidden = second_ref.shape[0]
    feat = first_ref.shape[0]
    classes = third_ref.shape[0]
    half, feat_half = hidden // 2, feat // 2
    is_first = core_ref[0] == 0

    def both(start, count):
        mine_ref, theirs_ref = (mine_one, theirs_one) if start < one else (mine_two, theirs_two)
        at = start if start < one else start - one
        mine = mine_ref[at : at + count, :].astype(f32)
        theirs = theirs_ref[at : at + count, :].astype(f32)
        return jnp.where(is_first, mine, theirs), jnp.where(is_first, theirs, mine)

    step = math.gcd(one, half)
    outs = []
    for start in range(0, half, step):
        for k, value in enumerate(both(start, step)):
            at = k * half + start
            wide_v[at : at + step, :] = value
            out = pltpu.make_async_copy(
                wide_v.at[pl.ds(at, step)], second_ref.at[pl.ds(at, step)], out_sems.at[2 * (start // step) + k]
            )
            out.start()
            outs.append(out)
    low, high = both(half + feat_half, class_half)
    third_ref[0:class_half, :] = low
    third_ref[class_half:classes, :] = high[: classes - class_half]
    firsts = both(half, feat_half)
    biases = both(half + feat_half + class_half, 8)
    for k in range(2):
        at = slice(k * half, (k + 1) * half)
        first_ref[0:feat_half, at] = firsts[k][:, :half]
        first_ref[feat_half:feat, at] = firsts[k][:, half:]
        first_bias_ref[:, at] = biases[k][:1, :half]
        second_bias_ref[:, at] = biases[k][:1, half:]
    for out in outs:
        out.wait()


def gelu_parts(x):
    k = math.sqrt(2.0 / math.pi)
    square = x * x
    t = jnp.tanh(x * (k + (k * 0.044715) * square))
    half_up = 0.5 + 0.5 * t
    slope = half_up + (0.5 * x) * (1.0 - t * t) * (k + (3.0 * k * 0.044715) * square)
    return (x * half_up).astype(bf16), slope.astype(bf16)


def swap_cores(x):
    return lax.ppermute(x, "col", [(0, 1), (1, 0)])


def exchange(x, first_step, second_step):
    domains, cores = lax.axis_size("dom"), lax.axis_size("col")
    steps = (first_step, second_step)
    pairs = [
        (d * cores + c, (d ^ steps[c]) * cores + c) for d in range(domains) for c in range(cores)
    ]
    return lax.ppermute(x, ("dom", "col"), pairs)


def halving_steps():
    domains = lax.axis_size("dom")
    bits = [1 << b for b in range(domains.bit_length() - 1)]
    other = list(bits)
    if len(bits) > 1:
        other[0], other[1] = other[1], other[0]
    return list(zip(bits, other))


def split(x, axis):
    half = x.shape[axis] // 2
    return lax.slice_in_dim(x, 0, half, axis=axis), lax.slice_in_dim(x, half, 2 * half, axis=axis)


def sum_over_domains(x):
    me, core = lax.axis_index("dom"), lax.axis_index("col")
    plan = []
    width, depth = x.shape[1], x.shape[0]
    for steps in halving_steps():
        if width > LANES:
            plan.append((steps, 1))
            width //= 2
        else:
            plan.append((steps, 0))
            depth //= 2
    current = x
    bits = []
    for (a, b), axis in plan:
        up = jnp.where(core == 0, me & a, me & b) != 0
        bits.append(up)
        low, high = split(current, axis)
        got = exchange(jnp.where(up, low, high), a, b)
        keep = jnp.where(up, high, low)
        current = (keep.astype(f32) + got.astype(f32)).astype(bf16)
    for ((a, b), axis), up in zip(plan[::-1], bits[::-1]):
        got = exchange(current, a, b)
        current = jnp.where(
            up,
            jnp.concatenate([got, current], axis),
            jnp.concatenate([current, got], axis),
        )
    return current


def shards(
    features,
    first_weight,
    first_bias,
    second_weight,
    second_bias,
    third_weight,
    local_tiles,
    local_target,
    local_source,
    halo_tiles,
    halo_target,
    halo_block,
    send_rows,
    send_count,
    degree,
    batch_nodes,
    labels,
    batch_logits,
):
    rows = degree.shape[0]
    classes = batch_logits.shape[-1]
    batch = batch_logits.shape[1]
    block = local_tiles.shape[-1]
    blocks = rows // block
    peers, slots = send_rows.shape[1], send_rows.shape[2]
    hidden = second_weight.shape[0]
    class_half = (classes // 2 + 7) // 8 * 8
    core = lax.axis_index("col").astype(jnp.int32)
    core_arg = core.reshape(1)
    packed = packed_rows(slots, class_half)
    local_count, halo_count = local_tiles.shape[2], halo_tiles.shape[2]

    stride = 2 * (local_count + halo_count)
    degree_blocks = degree.reshape(blocks, block)
    out_type = jax.ShapeDtypeStruct((peers, packed, LANES), bf16)
    value_type = jax.ShapeDtypeStruct((rows, LANES), bf16)
    half_type = jax.ShapeDtypeStruct((rows // 2, LANES), bf16)
    acc = pltpu.VMEM((rows, LANES), f32)
    sending = [
        pltpu.VMEM((peers * slots, LANES), f32),
        pltpu.VMEM((peers, packed, LANES), bf16),
        pltpu.VMEM((rows, LANES), bf16),
    ]
    peer_sems = pltpu.SemaphoreType.DMA((peers,))

    counts = send_count[0]
    whole_tiles = slots % LANES == 0
    first_rows = send_rows[0] if whole_tiles else send_rows[0].reshape(-1)
    out, value = pl.pallas_call(
        functools.partial(first_kernel, class_half),
        out_shape=(out_type, value_type),
        in_specs=[smem()] * 3 + [vmem() if whole_tiles else smem()] + [vmem()] * 3,
        out_specs=(hbm(), hbm()),
        scratch_shapes=[
            pltpu.VMEM((2 * LANES, batch), f32),
            pltpu.VMEM((batch, LANES), f32),
            acc,
            *sending,
            pltpu.SMEM((peers * slots,), jnp.int32),
            peer_sems,
            peer_sems,
            pltpu.SemaphoreType.DMA((1,)),
        ],
        compiler_params=params(),
        name="first",
    )(core_arg, counts, batch_nodes[0], first_rows, labels, jnp.transpose(batch_logits, (2, 0, 1)), degree_blocks)
    tied_rows, *lists, _ = lax.optimization_barrier(
        (send_rows, local_target, local_source, halo_target, halo_block, value)
    )
    idx = tied_rows.reshape(-1)
    meta_own = jnp.concatenate([part[0, 0] for part in lists])
    meta = jnp.concatenate([meta_own, swap_cores(meta_own)])
    own_local, own_halo = local_tiles[0, 0], halo_tiles[0, 0]
    other_local, other_halo = swap_cores(own_local), swap_cores(own_halo)

    def turn(array, axis):
        low, high = split(array, axis)
        return jnp.where(core == 0, array, jnp.concatenate([high, low], axis))

    values = []
    for hop in range(HOPS):
        last = hop + 1 == HOPS
        values.insert(0, value)
        landed = lax.all_to_all(out, "dom", split_axis=0, concat_axis=0, tiled=True)
        extra = []
        if hop == 0:
            first_w, first_b, second_w, _ = lax.optimization_barrier(
                (first_weight, first_bias, second_weight, value)
            )
            held = (turn(first_w, 1), turn(first_b, 0), turn(second_w, 0))
            value, first_turned, bias_turned, second_turned = lax.optimization_barrier((value, *held))
        if hop == 1:
            x, third_w, _ = lax.optimization_barrier((features, third_weight, value))
            pre_first = jnp.dot(x, first_turned, preferred_element_type=f32) + bias_turned
            low = jnp.pad(third_w[:, :class_half], ((0, 0), (0, LANES - class_half)))
            high = jnp.pad(third_w[:, class_half:], ((0, 0), (0, LANES - classes + class_half)))
            third = jnp.where(core == 0, jnp.concatenate([low, high], 1), jnp.concatenate([high, low], 1))
            value, hidden_first, slope_first, third = lax.optimization_barrier((value, *gelu_parts(pre_first), third))
        if hop == 2:
            tied, _ = lax.optimization_barrier((hidden_first, value))
            pre_second = jnp.dot(tied, second_turned, preferred_element_type=f32)
            value, pre_second = lax.optimization_barrier((value, pre_second))
        if last:
            tied, *earlier, _ = lax.optimization_barrier((pre_second, *values[1:], value))
            total = sum(part.astype(f32) for part in earlier).astype(bf16)
            value, hidden_second, slope_second, total = lax.optimization_barrier(
                (value, *gelu_parts(tied + second_bias), total)
            )
            extra = [total]
        result = pl.pallas_call(
            functools.partial(far_kernel, slots, class_half, stride, last),
            out_shape=(half_type, half_type) if last else (out_type, value_type),
            in_specs=[smem()] * 4 + [vmem()] + [hbm()] * (6 + len(extra)),
            out_specs=(vmem(), vmem()) if last else (hbm(), hbm()),
            scratch_shapes=[
                pltpu.VMEM((peers, packed, LANES), bf16),
                pltpu.VMEM((2 * (local_count + halo_count), block, block), bf16),
                pltpu.VMEM((rows, LANES), bf16),
                pltpu.VMEM((peers * slots, LANES), bf16),
                acc,
            ]
            + ([pltpu.VMEM((rows, LANES), bf16)] if last else sending + [peer_sems])
            + [pltpu.SemaphoreType.DMA((7,))],
            compiler_params=params(),
            name="far_last" if last else "far",
        )(core_arg, meta, counts, idx, degree_blocks, landed, own_halo, other_halo, value, own_local, other_local, *extra)
        if last:
            keep, send = result
        else:
            out, value = result

    got = swap_cores(send)
    delta = jnp.concatenate([keep, got], axis=1)

    def contract(a, b):
        return lax.dot_general(a, b, (((0,), (0,)), ((), ())), preferred_element_type=f32).astype(bf16)

    half, feat = hidden // 2, x.shape[1]
    lead = half // 4 * 3
    back_second = lax.dot_general(delta, third, (((1,), (1,)), ((), ())), preferred_element_type=f32)
    second_delta = (slope_second.astype(f32) * back_second).astype(bf16)
    second_bias_grad = jnp.sum(second_delta.astype(f32), axis=0).astype(bf16)
    send_lead = contract(hidden_first[:, half : half + lead], second_delta)
    got_lead = swap_cores(send_lead)
    keep_lead = contract(hidden_first[:, :lead], second_delta)
    send_tail = contract(hidden_first[:, half + lead :], second_delta)
    keep_tail = contract(hidden_first[:, lead:half], second_delta)
    third_grad = contract(delta, hidden_second)
    back_first = lax.dot_general(
        second_delta, second_turned, (((1,), (1,)), ((), ())), preferred_element_type=f32
    )
    first_delta = (slope_first.astype(f32) * back_first).astype(bf16)
    first_grad = contract(x, first_delta)
    first_bias_grad = jnp.sum(first_delta.astype(f32), axis=0).astype(bf16)

    is_first = core == 0
    domains = lax.axis_size("dom")
    column_splits = (hidden // LANES).bit_length() - 1
    grain = 8 * max(1, domains >> column_splits)
    used = half - lead + feat // 2 + class_half
    tail_rows = -(-(used + 1) // grain) * grain

    def bundle(part, tail, third_rows, bias_half):
        at = slice(part * half, (part + 1) * half)
        first_rows = jnp.concatenate([first_grad[: feat // 2, at], first_grad[feat // 2 :, at]], 1)
        bias_row = jnp.concatenate([first_bias_grad[at], bias_half])
        bias = jnp.broadcast_to(bias_row[None], (tail_rows - used, hidden))
        return jnp.concatenate([tail, first_rows, third_rows[:class_half], bias], 0)

    low_bias, high_bias = split(second_bias_grad, 0)
    keep_rest = bundle(0, keep_tail, third_grad[:LANES], jnp.where(is_first, low_bias, high_bias))
    send_rest = bundle(1, send_tail, third_grad[LANES:], jnp.where(is_first, high_bias, low_bias))
    got_rest = swap_cores(send_rest)
    mine_lead = sum_over_domains((keep_lead.astype(f32) + got_lead.astype(f32)).astype(bf16))
    mine_rest = sum_over_domains((keep_rest.astype(f32) + got_rest.astype(f32)).astype(bf16))
    theirs_lead, theirs_rest = swap_cores(mine_lead), swap_cores(mine_rest)
    first_out, first_bias_out, second_out, second_bias_out, third_out = pl.pallas_call(
        functools.partial(finish_kernel, class_half),
        out_shape=(
            jax.ShapeDtypeStruct((feat, hidden), f32),
            jax.ShapeDtypeStruct((1, hidden), f32),
            jax.ShapeDtypeStruct((hidden, hidden), f32),
            jax.ShapeDtypeStruct((1, hidden), f32),
            jax.ShapeDtypeStruct((classes, hidden), f32),
        ),
        in_specs=[smem()] + [vmem()] * 4,
        out_specs=(vmem(), vmem(), hbm(), vmem(), vmem()),
        scratch_shapes=[
            pltpu.VMEM((hidden, hidden), f32),
            pltpu.SemaphoreType.DMA((2 * (half // math.gcd(lead, half)),)),
        ],
        compiler_params=pltpu.CompilerParams(vmem_limit_bytes=24 * 1024 * 1024),
        name="finish",
    )(core_arg, mine_lead, theirs_lead, mine_rest, theirs_rest)
    return first_out, first_bias_out.reshape(hidden), second_out, second_bias_out.reshape(hidden), third_out.T


def solution(mesh):
    return jax.shard_map(
        shards,
        mesh=mesh,
        in_specs=(
            P(("grp", "dom", "col"), None),
            P(),
            P(),
            P(),
            P(),
            P(),
            P(("grp", "dom"), "col", None, None, None),
            P(("grp", "dom"), "col", None),
            P(("grp", "dom"), "col", None),
            P(("grp", "dom"), "col", None, None, None),
            P(("grp", "dom"), "col", None),
            P(("grp", "dom"), "col", None),
            P(("grp", "dom"), None, None),
            P(("grp", "dom"), None),
            P(("grp", "dom")),
            P(("grp", "dom"), None),
            P(("grp", "dom"), None),
            P(("grp", "dom"), None, None),
        ),
        out_specs=(P("grp", None), P("grp"), P("grp", None), P("grp"), P("grp", None)),
        check_vma=False,
    )
```

```python
import functools
import math

import jax
import jax.numpy as jnp
from jax import lax
from jax.experimental import pallas as pl
from jax.experimental.pallas import tpu as pltpu
from jax.sharding import PartitionSpec as P

HOPS = 4
teleport = 0.1
LANES = 128
UNROLL = 16
VMEM_LIMIT = 60 * 1024 * 1024

bf16 = jnp.bfloat16
f32 = jnp.float32


def vmem():
    return pl.BlockSpec(memory_space=pltpu.VMEM)


def smem():
    return pl.BlockSpec(memory_space=pltpu.SMEM)


def hbm():
    return pl.BlockSpec(memory_space=pltpu.HBM)


def params():
    return pltpu.CompilerParams(vmem_limit_bytes=VMEM_LIMIT)


def is_packed(slots, class_half):
    return slots % 64 == 0 and class_half <= 96


def packed_rows(slots, class_half):
    return slots * 3 // 4 if is_packed(slots, class_half) else slots


def send_packed(v_ref, count_ref, idx_ref, stage_ref, packed_ref, out_ref, sems, slots, class_half):
    peers = packed_ref.shape[0]

    def gather(j, carry):
        first = j * slots

        def body(g, inner):
            base = pl.multiple_of(first + g * UNROLL, UNROLL)
            for u in range(UNROLL):
                stage_ref[pl.ds(base + u, 1), :] = v_ref[pl.ds(idx_ref[base + u], 1), :]
            return inner

        return lax.fori_loop(0, (count_ref[j] + (UNROLL - 1)) // UNROLL, body, carry)

    lax.fori_loop(0, peers, gather, 0)
    half, quarter = slots // 2, slots // 4
    row = lax.broadcasted_iota(jnp.int32, (slots, LANES), 0)
    lane_a = lax.broadcasted_iota(jnp.int32, (half, LANES), 1)
    lane_b = lax.broadcasted_iota(jnp.int32, (quarter, LANES), 1) // 32

    def peer(j, carry):
        base = pl.multiple_of(j * slots, slots)
        taken = jnp.where(row < count_ref[j], stage_ref[pl.ds(base, slots), :], 0.0)
        if is_packed(slots, class_half):
            low, high = taken[:half], taken[half:]
            packed_ref[j, 0:half] = jnp.where(lane_a < 64, low, pltpu.roll(high, 64, 1)).astype(bf16)
            parts = (low[:quarter], low[quarter:], high[:quarter], high[quarter:])
            narrow = jnp.zeros((quarter, LANES), f32)
            for g in range(4):
                narrow = jnp.where(lane_b == g, pltpu.roll(parts[g], (g * 32 - 64) % LANES, 1), narrow)
            packed_ref[j, half : half + quarter] = narrow.astype(bf16)
        else:
            packed_ref[j] = taken.astype(bf16)
        pltpu.make_async_copy(packed_ref.at[j], out_ref.at[j], sems.at[j]).start()
        return carry

    lax.fori_loop(0, peers, peer, 0)


def wait_packed(packed_ref, out_ref, sems):
    def peer(j, carry):
        pltpu.make_async_copy(packed_ref.at[j], out_ref.at[j], sems.at[j]).wait()
        return carry

    lax.fori_loop(0, packed_ref.shape[0], peer, 0)


def unpack_rows(recv_ref, rows_ref, slots, class_half):
    peers = recv_ref.shape[0]
    if not is_packed(slots, class_half):

        def plain(j, carry):
            rows_ref[pl.ds(pl.multiple_of(j * slots, slots), slots), :] = recv_ref[j]
            return carry

        lax.fori_loop(0, peers, plain, 0)
        return
    half, quarter = slots // 2, slots // 4
    lane = lax.broadcasted_iota(jnp.int32, (quarter, LANES), 1)

    def body(j, carry):
        base = pl.multiple_of(j * slots, slots)
        wide = recv_ref[j, 0:half].astype(f32)
        narrow = recv_ref[j, half : half + quarter].astype(f32)
        turned = pltpu.roll(wide, 64, 1)
        fronts = (wide[:quarter], wide[quarter:], turned[:quarter], turned[quarter:])
        for g in range(4):
            back = pltpu.roll(narrow, (64 - g * 32) % LANES, 1)
            back = jnp.where(lane < 96, back, 0.0)
            rows_ref[pl.ds(base + g * quarter, quarter), :] = jnp.where(
                lane < 64, fronts[g], back
            ).astype(bf16)
        return carry

    lax.fori_loop(0, peers, body, 0)


def root_columns(degree_ref, function):
    blocks, block = degree_ref.shape
    values = function(degree_ref[...].astype(f32))
    return jnp.transpose(jnp.concatenate([values, jnp.zeros((block - blocks, block), f32)], 0))


def over_lanes(columns, b):
    return jnp.broadcast_to(columns[:, b : b + 1], columns.shape)


def first_kernel(class_half, core_ref, count_ref, nodes_ref, rows_ref, labels_ref, logits_ref, degree_ref,
                 out_ref, value_ref, wide_ref, diff_ref, v_ref, stage_ref, packed_ref, value_v, idx_ref, idx_sems,
                 sems, own_sems):
    classes, unused, batch = logits_ref.shape
    peers = packed_ref.shape[0]
    slots = stage_ref.shape[0] // peers
    flat = []
    if rows_ref.ndim == 1:
        idx_ref = rows_ref
    else:
        for j in range(peers):
            to = idx_ref.at[pl.ds(j * slots, slots)]
            flat.append(pltpu.make_async_copy(rows_ref.at[j], to, idx_sems.at[j]))
    for copy in flat:
        copy.start()
    blocks, block = degree_ref.shape
    core = core_ref[0]
    logits = logits_ref[...].reshape(classes, batch)
    shifted = jnp.exp(logits - jnp.max(logits, axis=0, keepdims=True))
    hot = lax.broadcasted_iota(jnp.int32, (classes, batch), 0) == labels_ref[...]
    probs = shifted / jnp.sum(shifted, axis=0, keepdims=True)
    wide_ref[...] = jnp.zeros_like(wide_ref)
    wide_ref[0:classes, :] = probs - jnp.where(hot, 1.0, 0.0)
    chosen = wide_ref[pl.ds(pl.multiple_of(core * class_half, 8), LANES), :]
    lane = lax.broadcasted_iota(jnp.int32, (batch, LANES), 1)
    diff_ref[...] = jnp.where(lane < class_half, jnp.transpose(chosen), 0.0)
    v_ref[...] = jnp.zeros_like(v_ref)

    def add_row(i, carry):
        at = pl.ds(nodes_ref[i], 1)
        v_ref[at, :] = v_ref[at, :] + diff_ref[pl.ds(i, 1), :]
        return carry

    lax.fori_loop(0, batch, add_row, 0, unroll=8)
    roots = root_columns(degree_ref, lax.rsqrt)
    for b in range(blocks):
        at = slice(b * block, (b + 1) * block)
        scaled = over_lanes(roots, b) * v_ref[at, :]
        value_v[at, :] = scaled.astype(bf16)
        v_ref[at, :] = scaled
    value_copy = pltpu.make_async_copy(value_v, value_ref, own_sems.at[0])
    value_copy.start()
    for copy in flat:
        copy.wait()
    send_packed(v_ref, count_ref, idx_ref, stage_ref, packed_ref, out_ref, sems, slots, class_half)
    value_copy.wait()
    wait_packed(packed_ref, out_ref, sems)


def add_tiles(acc_ref, source_ref, tile_refs, meta_ref, target_base, source_base, stride):
    count, block = tile_refs[0].shape[0], tile_refs[0].shape[1]
    for which, tiles in enumerate(tile_refs):
        for t in range(count):
            target = meta_ref[which * stride + target_base + t]
            source = meta_ref[which * stride + source_base + t]
            product = jnp.dot(
                tiles[t],
                source_ref[pl.ds(pl.multiple_of(source * block, block), block), :],
                preferred_element_type=f32,
            )
            at = pl.ds(pl.multiple_of(target * block, block), block)
            acc_ref[at, :] = acc_ref[at, :] + product


class Part:
    def __init__(self, ref, offset):
        self.ref, self.offset = ref, offset

    def __getitem__(self, i):
        return self.ref[self.offset + i]


def turn_kernel(core_ref, first_ref, bias_ref, second_ref, first_out, bias_out, second_out, sems):
    core = core_ref[0]
    half = second_ref.shape[0] // 2
    copies = []
    for i in range(2):
        source = pl.ds(pl.multiple_of((core ^ i) * half, half), half)
        to = pl.ds(i * half, half)
        copies += [
            pltpu.make_async_copy(second_ref.at[source], second_out.at[to], sems.at[3 * i]),
            pltpu.make_async_copy(first_ref.at[:, source], first_out.at[:, to], sems.at[3 * i + 1]),
            pltpu.make_async_copy(bias_ref.at[:, source], bias_out.at[:, to], sems.at[3 * i + 2]),
        ]
    for copy in copies:
        copy.start()
    for copy in copies:
        copy.wait()


def far_kernel(slots, class_half, stride, last, ints_ref, degree_in_ref, recv_ref,
               own_halo_ref, other_halo_ref, value_in_ref, own_local_ref, other_local_ref, *rest):
    if last:
        (total_ref, keep_ref, send_ref, ints, degree_ref, recv_v, tiles_v, value_in_v, rows_ref, acc_ref, total_v,
         own_sems) = rest
    else:
        (out_ref, value_ref, ints, degree_ref, recv_v, tiles_v, value_in_v, rows_ref, acc_ref, stage_ref, packed_ref,
         value_v, sems, own_sems) = rest
    core_ref, count_ref = Part(ints, 0), Part(ints, 1)
    meta_ref, idx_ref = Part(ints, LANES), Part(ints, LANES + 2 * stride)
    degree_copy = pltpu.make_async_copy(degree_in_ref, degree_ref, own_sems.at[7])
    degree_copy.start()
    ints_copy = pltpu.make_async_copy(ints_ref, ints, own_sems.at[8])
    ints_copy.start()
    local_count, block = own_local_ref.shape[0], own_local_ref.shape[1]
    halo_count = own_halo_ref.shape[0]
    blocks = degree_ref.shape[0]
    tiles = []
    start = 0
    for ref in (own_local_ref, other_local_ref, own_halo_ref, other_halo_ref):
        tiles.append(tiles_v.at[pl.ds(start, ref.shape[0])])
        start += ref.shape[0]
    copies = [
        pltpu.make_async_copy(value_in_ref, value_in_v, own_sems.at[0]),
        pltpu.make_async_copy(own_local_ref, tiles[0], own_sems.at[1]),
        pltpu.make_async_copy(other_local_ref, tiles[1], own_sems.at[2]),
        pltpu.make_async_copy(recv_ref, recv_v, own_sems.at[3]),
        pltpu.make_async_copy(own_halo_ref, tiles[2], own_sems.at[4]),
        pltpu.make_async_copy(other_halo_ref, tiles[3], own_sems.at[5]),
    ]
    for copy in copies:
        copy.start()
    if last:
        total_copy = pltpu.make_async_copy(total_ref, total_v, own_sems.at[6])
        total_copy.start()
    degree_copy.wait()
    roots = root_columns(degree_ref, lax.rsqrt)
    if last:
        columns = root_columns(degree_ref, lambda degree: (teleport / (1.0 - teleport)) * degree)
        total_copy.wait()
        copies[0].wait()
        for b in range(blocks):
            at = slice(b * block, (b + 1) * block)
            total = total_v[at, :].astype(f32) + value_in_v[at, :].astype(f32)
            acc_ref[at, :] = over_lanes(columns, b) * total
    else:
        acc_ref[...] = jnp.zeros_like(acc_ref)
        copies[0].wait()
    for copy in copies[1:3]:
        copy.wait()
    ints_copy.wait()
    add_tiles(acc_ref, value_in_v, (tiles[0], tiles[1]), meta_ref, 0, local_count, stride)
    copies[3].wait()
    unpack_rows(recv_v, rows_ref, slots, class_half)
    for copy in copies[4:]:
        copy.wait()
    base = 2 * local_count
    add_tiles(acc_ref, rows_ref, (tiles[2], tiles[3]), meta_ref, base, base + halo_count, stride)
    rate = 1.0 - teleport
    if last:
        half_blocks = blocks // 2
        core = core_ref[0]
        for b in range(half_blocks):
            to = slice(b * block, (b + 1) * block)
            outs = []
            for b_at in (b, half_blocks + b):
                at = slice(b_at * block, (b_at + 1) * block)
                outs.append((rate * over_lanes(roots, b_at) * acc_ref[at, :]).astype(bf16))
            keep_ref[to, :] = jnp.where(core == 0, outs[0], outs[1])
            send_ref[to, :] = jnp.where(core == 0, outs[1], outs[0])
        return
    for b in range(blocks):
        at = slice(b * block, (b + 1) * block)
        root = over_lanes(roots, b)
        scaled = (rate * root * root) * acc_ref[at, :]
        value_v[at, :] = scaled.astype(bf16)
        acc_ref[at, :] = scaled
    value_copy = pltpu.make_async_copy(value_v, value_ref, own_sems.at[6])
    value_copy.start()
    send_packed(acc_ref, count_ref, idx_ref, stage_ref, packed_ref, out_ref, sems, slots, class_half)
    value_copy.wait()
    wait_packed(packed_ref, out_ref, sems)


def finish_kernel(class_half, core_ref, mine_one, theirs_one, mine_two, theirs_two, first_ref, first_bias_ref,
                  second_ref, second_bias_ref, third_ref, wide_v, out_sems):
    one = mine_one.shape[0]
    hidden = second_ref.shape[0]
    feat = first_ref.shape[0]
    classes = third_ref.shape[0]
    half, feat_half = hidden // 2, feat // 2
    is_first = core_ref[0] == 0

    def both(start, count):
        mine_ref, theirs_ref = (mine_one, theirs_one) if start < one else (mine_two, theirs_two)
        at = start if start < one else start - one
        mine = mine_ref[at : at + count, :].astype(f32)
        theirs = theirs_ref[at : at + count, :].astype(f32)
        return jnp.where(is_first, mine, theirs), jnp.where(is_first, theirs, mine)

    step = math.gcd(one, half)
    outs = []
    for start in range(0, half, step):
        for k, value in enumerate(both(start, step)):
            at = k * half + start
            wide_v[at : at + step, :] = value
            out = pltpu.make_async_copy(
                wide_v.at[pl.ds(at, step)], second_ref.at[pl.ds(at, step)], out_sems.at[2 * (start // step) + k]
            )
            out.start()
            outs.append(out)
    low, high = both(half + feat_half, class_half)
    third_ref[0:class_half, :] = low
    third_ref[class_half:classes, :] = high[: classes - class_half]
    firsts = both(half, feat_half)
    biases = both(half + feat_half + class_half, 8)
    for k in range(2):
        at = slice(k * half, (k + 1) * half)
        first_ref[0:feat_half, at] = firsts[k][:, :half]
        first_ref[feat_half:feat, at] = firsts[k][:, half:]
        first_bias_ref[:, at] = biases[k][:1, :half]
        second_bias_ref[:, at] = biases[k][:1, half:]
    for out in outs:
        out.wait()


def gelu_parts(x):
    k = math.sqrt(2.0 / math.pi)
    square = x * x
    t = jnp.tanh(x * (k + (k * 0.044715) * square))
    half_up = 0.5 + 0.5 * t
    slope = half_up + (0.5 * x) * (1.0 - t * t) * (k + (3.0 * k * 0.044715) * square)
    return (x * half_up).astype(bf16), slope.astype(bf16)


def swap_cores(x):
    return lax.ppermute(x, "col", [(0, 1), (1, 0)])


def exchange(x, first_step, second_step):
    domains, cores = lax.axis_size("dom"), lax.axis_size("col")
    steps = (first_step, second_step)
    pairs = [
        (d * cores + c, (d ^ steps[c]) * cores + c) for d in range(domains) for c in range(cores)
    ]
    return lax.ppermute(x, ("dom", "col"), pairs)


def halving_steps():
    domains = lax.axis_size("dom")
    bits = [1 << b for b in range(domains.bit_length() - 1)]
    other = list(bits)
    if len(bits) > 1:
        other[0], other[1] = other[1], other[0]
    return list(zip(bits, other))


def split(x, axis):
    half = x.shape[axis] // 2
    return lax.slice_in_dim(x, 0, half, axis=axis), lax.slice_in_dim(x, half, 2 * half, axis=axis)


def sum_over_domains(x):
    me, core = lax.axis_index("dom"), lax.axis_index("col")
    plan = []
    width, depth = x.shape[1], x.shape[0]
    for steps in halving_steps():
        if width > LANES:
            plan.append((steps, 1))
            width //= 2
        else:
            plan.append((steps, 0))
            depth //= 2
    current = x
    bits = []
    for (a, b), axis in plan:
        up = jnp.where(core == 0, me & a, me & b) != 0
        bits.append(up)
        low, high = split(current, axis)
        got = exchange(jnp.where(up, low, high), a, b)
        keep = jnp.where(up, high, low)
        current = (keep.astype(f32) + got.astype(f32)).astype(bf16)
    for ((a, b), axis), up in zip(plan[::-1], bits[::-1]):
        got = exchange(current, a, b)
        current = jnp.where(
            up,
            jnp.concatenate([got, current], axis),
            jnp.concatenate([current, got], axis),
        )
    return current


def shards(
    features,
    first_weight,
    first_bias,
    second_weight,
    second_bias,
    third_weight,
    local_tiles,
    local_target,
    local_source,
    halo_tiles,
    halo_target,
    halo_block,
    send_rows,
    send_count,
    degree,
    batch_nodes,
    labels,
    batch_logits,
):
    rows = degree.shape[0]
    classes = batch_logits.shape[-1]
    batch = batch_logits.shape[1]
    block = local_tiles.shape[-1]
    blocks = rows // block
    peers, slots = send_rows.shape[1], send_rows.shape[2]
    hidden = second_weight.shape[0]
    class_half = (classes // 2 + 7) // 8 * 8
    core = lax.axis_index("col").astype(jnp.int32)
    core_arg = core.reshape(1)
    packed = packed_rows(slots, class_half)
    local_count, halo_count = local_tiles.shape[2], halo_tiles.shape[2]

    stride = 2 * (local_count + halo_count)
    degree_blocks = degree.reshape(blocks, block)
    out_type = jax.ShapeDtypeStruct((peers, packed, LANES), bf16)
    value_type = jax.ShapeDtypeStruct((rows, LANES), bf16)
    half_type = jax.ShapeDtypeStruct((rows // 2, LANES), bf16)
    acc = pltpu.VMEM((rows, LANES), f32)
    sending = [
        pltpu.VMEM((peers * slots, LANES), f32),
        pltpu.VMEM((peers, packed, LANES), bf16),
        pltpu.VMEM((rows, LANES), bf16),
    ]
    peer_sems = pltpu.SemaphoreType.DMA((peers,))

    counts = send_count[0]
    whole_tiles = slots % LANES == 0
    first_rows = send_rows[0] if whole_tiles else send_rows[0].reshape(-1)
    out, value = pl.pallas_call(
        functools.partial(first_kernel, class_half),
        out_shape=(out_type, value_type),
        in_specs=[smem()] * 3 + [vmem() if whole_tiles else smem()] + [vmem()] * 3,
        out_specs=(hbm(), hbm()),
        scratch_shapes=[
            pltpu.VMEM((2 * LANES, batch), f32),
            pltpu.VMEM((batch, LANES), f32),
            acc,
            *sending,
            pltpu.SMEM((peers * slots,), jnp.int32),
            peer_sems,
            peer_sems,
            pltpu.SemaphoreType.DMA((1,)),
        ],
        compiler_params=params(),
        name="first",
    )(core_arg, counts, batch_nodes[0], first_rows, labels, jnp.transpose(batch_logits, (2, 0, 1)), degree_blocks)
    first_w, first_b, second_w, _ = lax.optimization_barrier((first_weight, first_bias, second_weight, value))
    first_turned, bias_turned, second_turned = pl.pallas_call(
        turn_kernel,
        out_shape=(
            jax.ShapeDtypeStruct(first_w.shape, bf16),
            jax.ShapeDtypeStruct((1, hidden), f32),
            jax.ShapeDtypeStruct(second_w.shape, bf16),
        ),
        in_specs=[smem(), hbm(), hbm(), hbm()],
        out_specs=(hbm(), hbm(), hbm()),
        scratch_shapes=[pltpu.SemaphoreType.DMA((6,))],
        compiler_params=params(),
        name="turn",
    )(core_arg, first_w, first_b.reshape(1, hidden), second_w)
    tied_rows, *lists, first_turned = lax.optimization_barrier(
        (send_rows, local_target, local_source, halo_target, halo_block, first_turned)
    )
    meta_own = jnp.concatenate([part[0, 0] for part in lists])
    total_ints = LANES + 2 * stride + peers * slots
    ints = jnp.concatenate(
        [
            core_arg,
            counts,
            jnp.zeros((LANES - 1 - peers,), jnp.int32),
            meta_own,
            swap_cores(meta_own),
            tied_rows.reshape(-1),
            jnp.zeros((-total_ints % 1024,), jnp.int32),
        ]
    )
    own_local, own_halo = local_tiles[0, 0], halo_tiles[0, 0]
    other_local, other_halo = swap_cores(own_local), swap_cores(own_halo)

    values = []
    for hop in range(HOPS):
        last = hop + 1 == HOPS
        values.insert(0, value)
        landed = lax.all_to_all(out, "dom", split_axis=0, concat_axis=0, tiled=True)
        extra = []
        if hop == 0:
            value, first_turned, bias_turned, second_turned = lax.optimization_barrier(
                (value, first_turned, bias_turned, second_turned)
            )
        if hop == 1:
            x, third_w, _ = lax.optimization_barrier((features, third_weight, value))
            pre_first = jnp.dot(x, first_turned, preferred_element_type=f32) + bias_turned
            low = jnp.pad(third_w[:, :class_half], ((0, 0), (0, LANES - class_half)))
            high = jnp.pad(third_w[:, class_half:], ((0, 0), (0, LANES - classes + class_half)))
            third = jnp.where(core == 0, jnp.concatenate([low, high], 1), jnp.concatenate([high, low], 1))
            value, hidden_first, slope_first, third = lax.optimization_barrier((value, *gelu_parts(pre_first), third))
        if hop == 2:
            tied, _ = lax.optimization_barrier((hidden_first, value))
            pre_second = jnp.dot(tied, second_turned, preferred_element_type=f32)
            value, pre_second = lax.optimization_barrier((value, pre_second))
        if last:
            tied, *earlier, _ = lax.optimization_barrier((pre_second, *values[1:], value))
            total = sum(part.astype(f32) for part in earlier).astype(bf16)
            value, hidden_second, slope_second, total = lax.optimization_barrier(
                (value, *gelu_parts(tied + second_bias), total)
            )
            extra = [total]
        result = pl.pallas_call(
            functools.partial(far_kernel, slots, class_half, stride, last),
            out_shape=(half_type, half_type) if last else (out_type, value_type),
            in_specs=[hbm()] * (8 + len(extra)),
            out_specs=(vmem(), vmem()) if last else (hbm(), hbm()),
            scratch_shapes=[
                pltpu.SMEM(ints.shape, jnp.int32),
                pltpu.VMEM((blocks, block), jnp.int32),
                pltpu.VMEM((peers, packed, LANES), bf16),
                pltpu.VMEM((2 * (local_count + halo_count), block, block), bf16),
                pltpu.VMEM((rows, LANES), bf16),
                pltpu.VMEM((peers * slots, LANES), bf16),
                acc,
            ]
            + ([pltpu.VMEM((rows, LANES), bf16)] if last else sending + [peer_sems])
            + [pltpu.SemaphoreType.DMA((9,))],
            compiler_params=params(),
            name="far_last" if last else "far",
        )(ints, degree_blocks, landed, own_halo, other_halo, value, own_local, other_local, *extra)
        if last:
            keep, send = result
        else:
            out, value = result

    got = swap_cores(send)
    delta = jnp.concatenate([keep, got], axis=1)

    def contract(a, b):
        return lax.dot_general(a, b, (((0,), (0,)), ((), ())), preferred_element_type=f32).astype(bf16)

    half, feat = hidden // 2, x.shape[1]
    lead = half // 4 * 3
    back_second = lax.dot_general(delta, third, (((1,), (1,)), ((), ())), preferred_element_type=f32)
    second_delta = (slope_second.astype(f32) * back_second).astype(bf16)
    second_bias_grad = jnp.sum(second_delta.astype(f32), axis=0).astype(bf16)
    send_lead = contract(hidden_first[:, half : half + lead], second_delta)
    got_lead = swap_cores(send_lead)
    keep_lead = contract(hidden_first[:, :lead], second_delta)
    send_tail = contract(hidden_first[:, half + lead :], second_delta)
    keep_tail = contract(hidden_first[:, lead:half], second_delta)
    third_grad = contract(delta, hidden_second)
    back_first = lax.dot_general(
        second_delta, second_turned, (((1,), (1,)), ((), ())), preferred_element_type=f32
    )
    first_delta = (slope_first.astype(f32) * back_first).astype(bf16)
    first_grad = contract(x, first_delta)
    first_bias_grad = jnp.sum(first_delta.astype(f32), axis=0).astype(bf16)

    is_first = core == 0
    domains = lax.axis_size("dom")
    column_splits = (hidden // LANES).bit_length() - 1
    grain = 8 * max(1, domains >> column_splits)
    used = half - lead + feat // 2 + class_half
    tail_rows = -(-(used + 1) // grain) * grain

    def bundle(part, tail, third_rows, bias_half):
        at = slice(part * half, (part + 1) * half)
        first_rows = jnp.concatenate([first_grad[: feat // 2, at], first_grad[feat // 2 :, at]], 1)
        bias_row = jnp.concatenate([first_bias_grad[at], bias_half])
        bias = jnp.broadcast_to(bias_row[None], (tail_rows - used, hidden))
        return jnp.concatenate([tail, first_rows, third_rows[:class_half], bias], 0)

    low_bias, high_bias = split(second_bias_grad, 0)
    keep_rest = bundle(0, keep_tail, third_grad[:LANES], jnp.where(is_first, low_bias, high_bias))
    send_rest = bundle(1, send_tail, third_grad[LANES:], jnp.where(is_first, high_bias, low_bias))
    got_rest = swap_cores(send_rest)
    mine_lead = sum_over_domains((keep_lead.astype(f32) + got_lead.astype(f32)).astype(bf16))
    mine_rest = sum_over_domains((keep_rest.astype(f32) + got_rest.astype(f32)).astype(bf16))
    theirs_lead, theirs_rest = swap_cores(mine_lead), swap_cores(mine_rest)
    first_out, first_bias_out, second_out, second_bias_out, third_out = pl.pallas_call(
        functools.partial(finish_kernel, class_half),
        out_shape=(
            jax.ShapeDtypeStruct((feat, hidden), f32),
            jax.ShapeDtypeStruct((1, hidden), f32),
            jax.ShapeDtypeStruct((hidden, hidden), f32),
            jax.ShapeDtypeStruct((1, hidden), f32),
            jax.ShapeDtypeStruct((classes, hidden), f32),
        ),
        in_specs=[smem()] + [vmem()] * 4,
        out_specs=(vmem(), vmem(), hbm(), vmem(), vmem()),
        scratch_shapes=[
            pltpu.VMEM((hidden, hidden), f32),
            pltpu.SemaphoreType.DMA((2 * (half // math.gcd(lead, half)),)),
        ],
        compiler_params=pltpu.CompilerParams(vmem_limit_bytes=24 * 1024 * 1024),
        name="finish",
    )(core_arg, mine_lead, theirs_lead, mine_rest, theirs_rest)
    return first_out, first_bias_out.reshape(hidden), second_out, second_bias_out.reshape(hidden), third_out.T


def solution(mesh):
    return jax.shard_map(
        shards,
        mesh=mesh,
        in_specs=(
            P(("grp", "dom", "col"), None),
            P(),
            P(),
            P(),
            P(),
            P(),
            P(("grp", "dom"), "col", None, None, None),
            P(("grp", "dom"), "col", None),
            P(("grp", "dom"), "col", None),
            P(("grp", "dom"), "col", None, None, None),
            P(("grp", "dom"), "col", None),
            P(("grp", "dom"), "col", None),
            P(("grp", "dom"), None, None),
            P(("grp", "dom"), None),
            P(("grp", "dom")),
            P(("grp", "dom"), None),
            P(("grp", "dom"), None),
            P(("grp", "dom"), None, None),
        ),
        out_specs=(P("grp", None), P("grp"), P("grp", None), P("grp"), P("grp", None)),
        check_vma=False,
    )
```

```python
import functools
import math

import jax
import jax.numpy as jnp
from jax import lax
from jax.experimental import pallas as pl
from jax.experimental.pallas import tpu as pltpu
from jax.sharding import PartitionSpec as P

HOPS = 4
teleport = 0.1
LANES = 128
UNROLL = 16
VMEM_LIMIT = 60 * 1024 * 1024

bf16 = jnp.bfloat16
f32 = jnp.float32


def vmem():
    return pl.BlockSpec(memory_space=pltpu.VMEM)


def smem():
    return pl.BlockSpec(memory_space=pltpu.SMEM)


def hbm():
    return pl.BlockSpec(memory_space=pltpu.HBM)


def params():
    return pltpu.CompilerParams(vmem_limit_bytes=VMEM_LIMIT)


def is_packed(slots, class_half):
    return slots % 64 == 0 and class_half <= 96


def packed_rows(slots, class_half):
    return slots * 3 // 4 if is_packed(slots, class_half) else slots


def send_packed(v_ref, count_ref, idx_ref, stage_ref, packed_ref, out_ref, sems, slots, class_half):
    peers = packed_ref.shape[0]

    def gather(j, carry):
        first = j * slots

        def body(g, inner):
            base = pl.multiple_of(first + g * UNROLL, UNROLL)
            for u in range(UNROLL):
                stage_ref[pl.ds(base + u, 1), :] = v_ref[pl.ds(idx_ref[base + u], 1), :]
            return inner

        return lax.fori_loop(0, (count_ref[j] + (UNROLL - 1)) // UNROLL, body, carry)

    lax.fori_loop(0, peers, gather, 0)
    half, quarter = slots // 2, slots // 4
    row = lax.broadcasted_iota(jnp.int32, (slots, LANES), 0)
    lane_a = lax.broadcasted_iota(jnp.int32, (half, LANES), 1)
    lane_b = lax.broadcasted_iota(jnp.int32, (quarter, LANES), 1) // 32

    def peer(j, carry):
        base = pl.multiple_of(j * slots, slots)
        taken = jnp.where(row < count_ref[j], stage_ref[pl.ds(base, slots), :], 0.0)
        if is_packed(slots, class_half):
            low, high = taken[:half], taken[half:]
            packed_ref[j, 0:half] = jnp.where(lane_a < 64, low, pltpu.roll(high, 64, 1)).astype(bf16)
            parts = (low[:quarter], low[quarter:], high[:quarter], high[quarter:])
            narrow = jnp.zeros((quarter, LANES), f32)
            for g in range(4):
                narrow = jnp.where(lane_b == g, pltpu.roll(parts[g], (g * 32 - 64) % LANES, 1), narrow)
            packed_ref[j, half : half + quarter] = narrow.astype(bf16)
        else:
            packed_ref[j] = taken.astype(bf16)
        pltpu.make_async_copy(packed_ref.at[j], out_ref.at[j], sems.at[j]).start()
        return carry

    lax.fori_loop(0, peers, peer, 0)


def wait_packed(packed_ref, out_ref, sems):
    def peer(j, carry):
        pltpu.make_async_copy(packed_ref.at[j], out_ref.at[j], sems.at[j]).wait()
        return carry

    lax.fori_loop(0, packed_ref.shape[0], peer, 0)


def unpack_rows(recv_ref, rows_ref, slots, class_half):
    peers = recv_ref.shape[0]
    if not is_packed(slots, class_half):

        def plain(j, carry):
            rows_ref[pl.ds(pl.multiple_of(j * slots, slots), slots), :] = recv_ref[j]
            return carry

        lax.fori_loop(0, peers, plain, 0)
        return
    half, quarter = slots // 2, slots // 4
    lane = lax.broadcasted_iota(jnp.int32, (quarter, LANES), 1)

    def body(j, carry):
        base = pl.multiple_of(j * slots, slots)
        wide = recv_ref[j, 0:half].astype(f32)
        narrow = recv_ref[j, half : half + quarter].astype(f32)
        turned = pltpu.roll(wide, 64, 1)
        fronts = (wide[:quarter], wide[quarter:], turned[:quarter], turned[quarter:])
        for g in range(4):
            back = pltpu.roll(narrow, (64 - g * 32) % LANES, 1)
            back = jnp.where(lane < 96, back, 0.0)
            rows_ref[pl.ds(base + g * quarter, quarter), :] = jnp.where(
                lane < 64, fronts[g], back
            ).astype(bf16)
        return carry

    lax.fori_loop(0, peers, body, 0)


def root_columns(degree_ref, function):
    blocks, block = degree_ref.shape
    values = function(degree_ref[...].astype(f32))
    return jnp.transpose(jnp.concatenate([values, jnp.zeros((block - blocks, block), f32)], 0))


def over_lanes(columns, b):
    return jnp.broadcast_to(columns[:, b : b + 1], columns.shape)


def first_kernel(class_half, core_ref, count_ref, nodes_ref, rows_ref, labels_ref, logits_ref, degree_ref,
                 out_ref, value_ref, wide_ref, diff_ref, v_ref, stage_ref, packed_ref, value_v, idx_ref, idx_sems,
                 sems, own_sems):
    classes, unused, batch = logits_ref.shape
    peers = packed_ref.shape[0]
    slots = stage_ref.shape[0] // peers
    flat = []
    if rows_ref.ndim == 1:
        idx_ref = rows_ref
    else:
        for j in range(peers):
            to = idx_ref.at[pl.ds(j * slots, slots)]
            flat.append(pltpu.make_async_copy(rows_ref.at[j], to, idx_sems.at[j]))
    for copy in flat:
        copy.start()
    blocks, block = degree_ref.shape
    core = core_ref[0]
    logits = logits_ref[...].reshape(classes, batch)
    shifted = jnp.exp(logits - jnp.max(logits, axis=0, keepdims=True))
    hot = lax.broadcasted_iota(jnp.int32, (classes, batch), 0) == labels_ref[...]
    probs = shifted / jnp.sum(shifted, axis=0, keepdims=True)
    wide_ref[...] = jnp.zeros_like(wide_ref)
    wide_ref[0:classes, :] = probs - jnp.where(hot, 1.0, 0.0)
    chosen = wide_ref[pl.ds(pl.multiple_of(core * class_half, 8), LANES), :]
    lane = lax.broadcasted_iota(jnp.int32, (batch, LANES), 1)
    diff_ref[...] = jnp.where(lane < class_half, jnp.transpose(chosen), 0.0)
    v_ref[...] = jnp.zeros_like(v_ref)

    def add_row(i, carry):
        at = pl.ds(nodes_ref[i], 1)
        v_ref[at, :] = v_ref[at, :] + diff_ref[pl.ds(i, 1), :]
        return carry

    lax.fori_loop(0, batch, add_row, 0, unroll=8)
    roots = root_columns(degree_ref, lax.rsqrt)
    for b in range(blocks):
        at = slice(b * block, (b + 1) * block)
        scaled = over_lanes(roots, b) * v_ref[at, :]
        value_v[at, :] = scaled.astype(bf16)
        v_ref[at, :] = scaled
    value_copy = pltpu.make_async_copy(value_v, value_ref, own_sems.at[0])
    value_copy.start()
    for copy in flat:
        copy.wait()
    send_packed(v_ref, count_ref, idx_ref, stage_ref, packed_ref, out_ref, sems, slots, class_half)
    value_copy.wait()
    wait_packed(packed_ref, out_ref, sems)


def add_tiles(acc_ref, source_ref, tile_refs, meta_ref, target_base, source_base, stride):
    count, block = tile_refs[0].shape[0], tile_refs[0].shape[1]
    for which, tiles in enumerate(tile_refs):
        for t in range(count):
            target = meta_ref[which * stride + target_base + t]
            source = meta_ref[which * stride + source_base + t]
            product = jnp.dot(
                tiles[t],
                source_ref[pl.ds(pl.multiple_of(source * block, block), block), :],
                preferred_element_type=f32,
            )
            at = pl.ds(pl.multiple_of(target * block, block), block)
            acc_ref[at, :] = acc_ref[at, :] + product


class Part:
    def __init__(self, ref, offset):
        self.ref, self.offset = ref, offset

    def __getitem__(self, i):
        return self.ref[self.offset + i]


def turn_kernel(core_ref, first_ref, bias_ref, second_ref, first_out, bias_out, second_out, first_v, bias_v, second_v,
                in_sems, out_sems):
    core = core_ref[0]
    half = second_ref.shape[0] // 2
    steps = []
    for i in range(2):
        source = pl.ds(pl.multiple_of((core ^ i) * half, half), half)
        to = pl.ds(i * half, half)
        for k, (array, held, out) in enumerate(
            (
                (second_ref.at[source], second_v.at[to], second_out.at[to]),
                (first_ref.at[:, source], first_v.at[:, to], first_out.at[:, to]),
                (bias_ref.at[:, source], bias_v.at[:, to], bias_out.at[:, to]),
            )
        ):
            steps.append(
                (
                    pltpu.make_async_copy(array, held, in_sems.at[3 * i + k]),
                    pltpu.make_async_copy(held, out, out_sems.at[3 * i + k]),
                )
            )
    for copy_in, unused in steps:
        copy_in.start()
    for copy_in, copy_out in steps:
        copy_in.wait()
        copy_out.start()
    for unused, copy_out in steps:
        copy_out.wait()


def far_kernel(slots, class_half, stride, last, ints_ref, degree_in_ref, recv_ref,
               own_halo_ref, other_halo_ref, value_in_ref, own_local_ref, other_local_ref, *rest):
    if last:
        (total_ref, keep_ref, send_ref, ints, degree_ref, recv_v, tiles_v, value_in_v, rows_ref, acc_ref, total_v,
         own_sems) = rest
    else:
        (out_ref, value_ref, ints, degree_ref, recv_v, tiles_v, value_in_v, rows_ref, acc_ref, stage_ref, packed_ref,
         value_v, sems, own_sems) = rest
    core_ref, count_ref = Part(ints, 0), Part(ints, 1)
    meta_ref, idx_ref = Part(ints, LANES), Part(ints, LANES + 2 * stride)
    degree_copy = pltpu.make_async_copy(degree_in_ref, degree_ref, own_sems.at[7])
    degree_copy.start()
    ints_copy = pltpu.make_async_copy(ints_ref, ints, own_sems.at[8])
    ints_copy.start()
    local_count, block = own_local_ref.shape[0], own_local_ref.shape[1]
    halo_count = own_halo_ref.shape[0]
    blocks = degree_ref.shape[0]
    tiles = []
    start = 0
    for ref in (own_local_ref, other_local_ref, own_halo_ref, other_halo_ref):
        tiles.append(tiles_v.at[pl.ds(start, ref.shape[0])])
        start += ref.shape[0]
    copies = [
        pltpu.make_async_copy(value_in_ref, value_in_v, own_sems.at[0]),
        pltpu.make_async_copy(own_local_ref, tiles[0], own_sems.at[1]),
        pltpu.make_async_copy(other_local_ref, tiles[1], own_sems.at[2]),
        pltpu.make_async_copy(recv_ref, recv_v, own_sems.at[3]),
        pltpu.make_async_copy(own_halo_ref, tiles[2], own_sems.at[4]),
        pltpu.make_async_copy(other_halo_ref, tiles[3], own_sems.at[5]),
    ]
    for copy in copies:
        copy.start()
    if last:
        total_copy = pltpu.make_async_copy(total_ref, total_v, own_sems.at[6])
        total_copy.start()
    degree_copy.wait()
    roots = root_columns(degree_ref, lax.rsqrt)
    if last:
        columns = root_columns(degree_ref, lambda degree: (teleport / (1.0 - teleport)) * degree)
        total_copy.wait()
        copies[0].wait()
        for b in range(blocks):
            at = slice(b * block, (b + 1) * block)
            total = total_v[at, :].astype(f32) + value_in_v[at, :].astype(f32)
            acc_ref[at, :] = over_lanes(columns, b) * total
    else:
        acc_ref[...] = jnp.zeros_like(acc_ref)
        copies[0].wait()
    for copy in copies[1:3]:
        copy.wait()
    ints_copy.wait()
    add_tiles(acc_ref, value_in_v, (tiles[0], tiles[1]), meta_ref, 0, local_count, stride)
    copies[3].wait()
    unpack_rows(recv_v, rows_ref, slots, class_half)
    for copy in copies[4:]:
        copy.wait()
    base = 2 * local_count
    add_tiles(acc_ref, rows_ref, (tiles[2], tiles[3]), meta_ref, base, base + halo_count, stride)
    rate = 1.0 - teleport
    if last:
        half_blocks = blocks // 2
        core = core_ref[0]
        for b in range(half_blocks):
            to = slice(b * block, (b + 1) * block)
            outs = []
            for b_at in (b, half_blocks + b):
                at = slice(b_at * block, (b_at + 1) * block)
                outs.append((rate * over_lanes(roots, b_at) * acc_ref[at, :]).astype(bf16))
            keep_ref[to, :] = jnp.where(core == 0, outs[0], outs[1])
            send_ref[to, :] = jnp.where(core == 0, outs[1], outs[0])
        return
    for b in range(blocks):
        at = slice(b * block, (b + 1) * block)
        root = over_lanes(roots, b)
        scaled = (rate * root * root) * acc_ref[at, :]
        value_v[at, :] = scaled.astype(bf16)
        acc_ref[at, :] = scaled
    value_copy = pltpu.make_async_copy(value_v, value_ref, own_sems.at[6])
    value_copy.start()
    send_packed(acc_ref, count_ref, idx_ref, stage_ref, packed_ref, out_ref, sems, slots, class_half)
    value_copy.wait()
    wait_packed(packed_ref, out_ref, sems)


def finish_kernel(class_half, core_ref, mine_one, theirs_one, mine_two, theirs_two, first_ref, first_bias_ref,
                  second_ref, second_bias_ref, third_ref, wide_v, out_sems):
    one = mine_one.shape[0]
    hidden = second_ref.shape[0]
    feat = first_ref.shape[0]
    classes = third_ref.shape[0]
    half, feat_half = hidden // 2, feat // 2
    is_first = core_ref[0] == 0

    def both(start, count):
        mine_ref, theirs_ref = (mine_one, theirs_one) if start < one else (mine_two, theirs_two)
        at = start if start < one else start - one
        mine = mine_ref[at : at + count, :].astype(f32)
        theirs = theirs_ref[at : at + count, :].astype(f32)
        return jnp.where(is_first, mine, theirs), jnp.where(is_first, theirs, mine)

    step = math.gcd(one, half)
    outs = []
    for start in range(0, half, step):
        for k, value in enumerate(both(start, step)):
            at = k * half + start
            wide_v[at : at + step, :] = value
            out = pltpu.make_async_copy(
                wide_v.at[pl.ds(at, step)], second_ref.at[pl.ds(at, step)], out_sems.at[2 * (start // step) + k]
            )
            out.start()
            outs.append(out)
    low, high = both(half + feat_half, class_half)
    third_ref[0:class_half, :] = low
    third_ref[class_half:classes, :] = high[: classes - class_half]
    firsts = both(half, feat_half)
    biases = both(half + feat_half + class_half, 8)
    for k in range(2):
        at = slice(k * half, (k + 1) * half)
        first_ref[0:feat_half, at] = firsts[k][:, :half]
        first_ref[feat_half:feat, at] = firsts[k][:, half:]
        first_bias_ref[:, at] = biases[k][:1, :half]
        second_bias_ref[:, at] = biases[k][:1, half:]
    for out in outs:
        out.wait()


def gelu_parts(x):
    k = math.sqrt(2.0 / math.pi)
    square = x * x
    t = jnp.tanh(x * (k + (k * 0.044715) * square))
    half_up = 0.5 + 0.5 * t
    slope = half_up + (0.5 * x) * (1.0 - t * t) * (k + (3.0 * k * 0.044715) * square)
    return (x * half_up).astype(bf16), slope.astype(bf16)


def swap_cores(x):
    return lax.ppermute(x, "col", [(0, 1), (1, 0)])


def exchange(x, first_step, second_step):
    domains, cores = lax.axis_size("dom"), lax.axis_size("col")
    steps = (first_step, second_step)
    pairs = [
        (d * cores + c, (d ^ steps[c]) * cores + c) for d in range(domains) for c in range(cores)
    ]
    return lax.ppermute(x, ("dom", "col"), pairs)


def halving_steps():
    domains = lax.axis_size("dom")
    bits = [1 << b for b in range(domains.bit_length() - 1)]
    other = list(bits)
    if len(bits) > 1:
        other[0], other[1] = other[1], other[0]
    return list(zip(bits, other))


def split(x, axis):
    half = x.shape[axis] // 2
    return lax.slice_in_dim(x, 0, half, axis=axis), lax.slice_in_dim(x, half, 2 * half, axis=axis)


def sum_over_domains(x):
    me, core = lax.axis_index("dom"), lax.axis_index("col")
    plan = []
    width, depth = x.shape[1], x.shape[0]
    for steps in halving_steps():
        if width > LANES:
            plan.append((steps, 1))
            width //= 2
        else:
            plan.append((steps, 0))
            depth //= 2
    current = x
    bits = []
    for (a, b), axis in plan:
        up = jnp.where(core == 0, me & a, me & b) != 0
        bits.append(up)
        low, high = split(current, axis)
        got = exchange(jnp.where(up, low, high), a, b)
        keep = jnp.where(up, high, low)
        current = (keep.astype(f32) + got.astype(f32)).astype(bf16)
    for ((a, b), axis), up in zip(plan[::-1], bits[::-1]):
        got = exchange(current, a, b)
        current = jnp.where(
            up,
            jnp.concatenate([got, current], axis),
            jnp.concatenate([current, got], axis),
        )
    return current


def shards(
    features,
    first_weight,
    first_bias,
    second_weight,
    second_bias,
    third_weight,
    local_tiles,
    local_target,
    local_source,
    halo_tiles,
    halo_target,
    halo_block,
    send_rows,
    send_count,
    degree,
    batch_nodes,
    labels,
    batch_logits,
):
    rows = degree.shape[0]
    classes = batch_logits.shape[-1]
    batch = batch_logits.shape[1]
    block = local_tiles.shape[-1]
    blocks = rows // block
    peers, slots = send_rows.shape[1], send_rows.shape[2]
    hidden = second_weight.shape[0]
    class_half = (classes // 2 + 7) // 8 * 8
    core = lax.axis_index("col").astype(jnp.int32)
    core_arg = core.reshape(1)
    packed = packed_rows(slots, class_half)
    local_count, halo_count = local_tiles.shape[2], halo_tiles.shape[2]

    stride = 2 * (local_count + halo_count)
    degree_blocks = degree.reshape(blocks, block)
    out_type = jax.ShapeDtypeStruct((peers, packed, LANES), bf16)
    value_type = jax.ShapeDtypeStruct((rows, LANES), bf16)
    half_type = jax.ShapeDtypeStruct((rows // 2, LANES), bf16)
    acc = pltpu.VMEM((rows, LANES), f32)
    sending = [
        pltpu.VMEM((peers * slots, LANES), f32),
        pltpu.VMEM((peers, packed, LANES), bf16),
        pltpu.VMEM((rows, LANES), bf16),
    ]
    peer_sems = pltpu.SemaphoreType.DMA((peers,))

    counts = send_count[0]
    whole_tiles = slots % LANES == 0
    first_rows = send_rows[0] if whole_tiles else send_rows[0].reshape(-1)
    out, value = pl.pallas_call(
        functools.partial(first_kernel, class_half),
        out_shape=(out_type, value_type),
        in_specs=[smem()] * 3 + [vmem() if whole_tiles else smem()] + [vmem()] * 3,
        out_specs=(hbm(), hbm()),
        scratch_shapes=[
            pltpu.VMEM((2 * LANES, batch), f32),
            pltpu.VMEM((batch, LANES), f32),
            acc,
            *sending,
            pltpu.SMEM((peers * slots,), jnp.int32),
            peer_sems,
            peer_sems,
            pltpu.SemaphoreType.DMA((1,)),
        ],
        compiler_params=params(),
        name="first",
    )(core_arg, counts, batch_nodes[0], first_rows, labels, jnp.transpose(batch_logits, (2, 0, 1)), degree_blocks)
    first_w, first_b, second_w, _ = lax.optimization_barrier((first_weight, first_bias, second_weight, value))
    first_turned, bias_turned, second_turned = pl.pallas_call(
        turn_kernel,
        out_shape=(
            jax.ShapeDtypeStruct(first_w.shape, bf16),
            jax.ShapeDtypeStruct((1, hidden), f32),
            jax.ShapeDtypeStruct(second_w.shape, bf16),
        ),
        in_specs=[smem(), hbm(), hbm(), hbm()],
        out_specs=(hbm(), hbm(), hbm()),
        scratch_shapes=[
            pltpu.VMEM(first_w.shape, bf16),
            pltpu.VMEM((1, hidden), f32),
            pltpu.VMEM(second_w.shape, bf16),
            pltpu.SemaphoreType.DMA((6,)),
            pltpu.SemaphoreType.DMA((6,)),
        ],
        compiler_params=params(),
        name="turn",
    )(core_arg, first_w, first_b.reshape(1, hidden), second_w)
    tied_rows, *lists, first_turned = lax.optimization_barrier(
        (send_rows, local_target, local_source, halo_target, halo_block, first_turned)
    )
    meta_own = jnp.concatenate([part[0, 0] for part in lists])
    total_ints = LANES + 2 * stride + peers * slots
    ints = jnp.concatenate(
        [
            core_arg,
            counts,
            jnp.zeros((LANES - 1 - peers,), jnp.int32),
            meta_own,
            swap_cores(meta_own),
            tied_rows.reshape(-1),
            jnp.zeros((-total_ints % 1024,), jnp.int32),
        ]
    )
    own_local, own_halo = local_tiles[0, 0], halo_tiles[0, 0]
    other_local, other_halo = swap_cores(own_local), swap_cores(own_halo)

    values = []
    for hop in range(HOPS):
        last = hop + 1 == HOPS
        values.insert(0, value)
        landed = lax.all_to_all(out, "dom", split_axis=0, concat_axis=0, tiled=True)
        extra = []
        if hop == 0:
            value, first_turned, bias_turned, second_turned = lax.optimization_barrier(
                (value, first_turned, bias_turned, second_turned)
            )
        if hop == 1:
            x, third_w, _ = lax.optimization_barrier((features, third_weight, value))
            pre_first = jnp.dot(x, first_turned, preferred_element_type=f32) + bias_turned
            low = jnp.pad(third_w[:, :class_half], ((0, 0), (0, LANES - class_half)))
            high = jnp.pad(third_w[:, class_half:], ((0, 0), (0, LANES - classes + class_half)))
            third = jnp.where(core == 0, jnp.concatenate([low, high], 1), jnp.concatenate([high, low], 1))
            value, hidden_first, slope_first, third = lax.optimization_barrier((value, *gelu_parts(pre_first), third))
        if hop == 2:
            tied, _ = lax.optimization_barrier((hidden_first, value))
            pre_second = jnp.dot(tied, second_turned, preferred_element_type=f32)
            value, pre_second = lax.optimization_barrier((value, pre_second))
        if last:
            tied, *earlier, _ = lax.optimization_barrier((pre_second, *values[1:], value))
            total = sum(part.astype(f32) for part in earlier).astype(bf16)
            value, hidden_second, slope_second, total = lax.optimization_barrier(
                (value, *gelu_parts(tied + second_bias), total)
            )
            extra = [total]
        result = pl.pallas_call(
            functools.partial(far_kernel, slots, class_half, stride, last),
            out_shape=(half_type, half_type) if last else (out_type, value_type),
            in_specs=[hbm()] * (8 + len(extra)),
            out_specs=(vmem(), vmem()) if last else (hbm(), hbm()),
            scratch_shapes=[
                pltpu.SMEM(ints.shape, jnp.int32),
                pltpu.VMEM((blocks, block), jnp.int32),
                pltpu.VMEM((peers, packed, LANES), bf16),
                pltpu.VMEM((2 * (local_count + halo_count), block, block), bf16),
                pltpu.VMEM((rows, LANES), bf16),
                pltpu.VMEM((peers * slots, LANES), bf16),
                acc,
            ]
            + ([pltpu.VMEM((rows, LANES), bf16)] if last else sending + [peer_sems])
            + [pltpu.SemaphoreType.DMA((9,))],
            compiler_params=params(),
            name="far_last" if last else "far",
        )(ints, degree_blocks, landed, own_halo, other_halo, value, own_local, other_local, *extra)
        if last:
            keep, send = result
        else:
            out, value = result

    got = swap_cores(send)
    delta = jnp.concatenate([keep, got], axis=1)

    def contract(a, b):
        return lax.dot_general(a, b, (((0,), (0,)), ((), ())), preferred_element_type=f32).astype(bf16)

    half, feat = hidden // 2, x.shape[1]
    lead = half // 4 * 3
    back_second = lax.dot_general(delta, third, (((1,), (1,)), ((), ())), preferred_element_type=f32)
    second_delta = (slope_second.astype(f32) * back_second).astype(bf16)
    second_bias_grad = jnp.sum(second_delta.astype(f32), axis=0).astype(bf16)
    send_lead = contract(hidden_first[:, half : half + lead], second_delta)
    got_lead = swap_cores(send_lead)
    keep_lead = contract(hidden_first[:, :lead], second_delta)
    send_tail = contract(hidden_first[:, half + lead :], second_delta)
    keep_tail = contract(hidden_first[:, lead:half], second_delta)
    third_grad = contract(delta, hidden_second)
    back_first = lax.dot_general(
        second_delta, second_turned, (((1,), (1,)), ((), ())), preferred_element_type=f32
    )
    first_delta = (slope_first.astype(f32) * back_first).astype(bf16)
    first_grad = contract(x, first_delta)
    first_bias_grad = jnp.sum(first_delta.astype(f32), axis=0).astype(bf16)

    is_first = core == 0
    domains = lax.axis_size("dom")
    column_splits = (hidden // LANES).bit_length() - 1
    grain = 8 * max(1, domains >> column_splits)
    used = half - lead + feat // 2 + class_half
    tail_rows = -(-(used + 1) // grain) * grain

    def bundle(part, tail, third_rows, bias_half):
        at = slice(part * half, (part + 1) * half)
        first_rows = jnp.concatenate([first_grad[: feat // 2, at], first_grad[feat // 2 :, at]], 1)
        bias_row = jnp.concatenate([first_bias_grad[at], bias_half])
        bias = jnp.broadcast_to(bias_row[None], (tail_rows - used, hidden))
        return jnp.concatenate([tail, first_rows, third_rows[:class_half], bias], 0)

    low_bias, high_bias = split(second_bias_grad, 0)
    keep_rest = bundle(0, keep_tail, third_grad[:LANES], jnp.where(is_first, low_bias, high_bias))
    send_rest = bundle(1, send_tail, third_grad[LANES:], jnp.where(is_first, high_bias, low_bias))
    got_rest = swap_cores(send_rest)
    mine_lead = sum_over_domains((keep_lead.astype(f32) + got_lead.astype(f32)).astype(bf16))
    mine_rest = sum_over_domains((keep_rest.astype(f32) + got_rest.astype(f32)).astype(bf16))
    theirs_lead, theirs_rest = swap_cores(mine_lead), swap_cores(mine_rest)
    first_out, first_bias_out, second_out, second_bias_out, third_out = pl.pallas_call(
        functools.partial(finish_kernel, class_half),
        out_shape=(
            jax.ShapeDtypeStruct((feat, hidden), f32),
            jax.ShapeDtypeStruct((1, hidden), f32),
            jax.ShapeDtypeStruct((hidden, hidden), f32),
            jax.ShapeDtypeStruct((1, hidden), f32),
            jax.ShapeDtypeStruct((classes, hidden), f32),
        ),
        in_specs=[smem()] + [vmem()] * 4,
        out_specs=(vmem(), vmem(), hbm(), vmem(), vmem()),
        scratch_shapes=[
            pltpu.VMEM((hidden, hidden), f32),
            pltpu.SemaphoreType.DMA((2 * (half // math.gcd(lead, half)),)),
        ],
        compiler_params=pltpu.CompilerParams(vmem_limit_bytes=24 * 1024 * 1024),
        name="finish",
    )(core_arg, mine_lead, theirs_lead, mine_rest, theirs_rest)
    return first_out, first_bias_out.reshape(hidden), second_out, second_bias_out.reshape(hidden), third_out.T


def solution(mesh):
    return jax.shard_map(
        shards,
        mesh=mesh,
        in_specs=(
            P(("grp", "dom", "col"), None),
            P(),
            P(),
            P(),
            P(),
            P(),
            P(("grp", "dom"), "col", None, None, None),
            P(("grp", "dom"), "col", None),
            P(("grp", "dom"), "col", None),
            P(("grp", "dom"), "col", None, None, None),
            P(("grp", "dom"), "col", None),
            P(("grp", "dom"), "col", None),
            P(("grp", "dom"), None, None),
            P(("grp", "dom"), None),
            P(("grp", "dom")),
            P(("grp", "dom"), None),
            P(("grp", "dom"), None),
            P(("grp", "dom"), None, None),
        ),
        out_specs=(P("grp", None), P("grp"), P("grp", None), P("grp"), P("grp", None)),
        check_vma=False,
    )
```

```python
import functools
import math

import jax
import jax.numpy as jnp
from jax import lax
from jax.experimental import pallas as pl
from jax.experimental.pallas import tpu as pltpu
from jax.sharding import PartitionSpec as P

HOPS = 4
teleport = 0.1
LANES = 128
UNROLL = 16
VMEM_LIMIT = 60 * 1024 * 1024

bf16 = jnp.bfloat16
f32 = jnp.float32


def vmem():
    return pl.BlockSpec(memory_space=pltpu.VMEM)


def smem():
    return pl.BlockSpec(memory_space=pltpu.SMEM)


def hbm():
    return pl.BlockSpec(memory_space=pltpu.HBM)


def params():
    return pltpu.CompilerParams(vmem_limit_bytes=VMEM_LIMIT)


def is_packed(slots, class_half):
    return slots % 64 == 0 and class_half <= 96


def packed_rows(slots, class_half):
    return slots * 3 // 4 if is_packed(slots, class_half) else slots


def send_packed(v_ref, count_ref, idx_ref, stage_ref, packed_ref, out_ref, sems, slots, class_half):
    peers = packed_ref.shape[0]

    def gather(j, carry):
        first = j * slots

        def body(g, inner):
            base = pl.multiple_of(first + g * UNROLL, UNROLL)
            for u in range(UNROLL):
                stage_ref[pl.ds(base + u, 1), :] = v_ref[pl.ds(idx_ref[base + u], 1), :]
            return inner

        return lax.fori_loop(0, (count_ref[j] + (UNROLL - 1)) // UNROLL, body, carry)

    lax.fori_loop(0, peers, gather, 0)
    half, quarter = slots // 2, slots // 4
    row = lax.broadcasted_iota(jnp.int32, (slots, LANES), 0)
    lane_a = lax.broadcasted_iota(jnp.int32, (half, LANES), 1)
    lane_b = lax.broadcasted_iota(jnp.int32, (quarter, LANES), 1) // 32

    def peer(j, carry):
        base = pl.multiple_of(j * slots, slots)
        taken = jnp.where(row < count_ref[j], stage_ref[pl.ds(base, slots), :], 0.0)
        if is_packed(slots, class_half):
            low, high = taken[:half], taken[half:]
            packed_ref[j, 0:half] = jnp.where(lane_a < 64, low, pltpu.roll(high, 64, 1)).astype(bf16)
            parts = (low[:quarter], low[quarter:], high[:quarter], high[quarter:])
            narrow = jnp.zeros((quarter, LANES), f32)
            for g in range(4):
                narrow = jnp.where(lane_b == g, pltpu.roll(parts[g], (g * 32 - 64) % LANES, 1), narrow)
            packed_ref[j, half : half + quarter] = narrow.astype(bf16)
        else:
            packed_ref[j] = taken.astype(bf16)
        pltpu.make_async_copy(packed_ref.at[j], out_ref.at[j], sems.at[j]).start()
        return carry

    lax.fori_loop(0, peers, peer, 0)


def wait_packed(packed_ref, out_ref, sems):
    def peer(j, carry):
        pltpu.make_async_copy(packed_ref.at[j], out_ref.at[j], sems.at[j]).wait()
        return carry

    lax.fori_loop(0, packed_ref.shape[0], peer, 0)


def unpack_rows(recv_ref, rows_ref, slots, class_half):
    peers = recv_ref.shape[0]
    if not is_packed(slots, class_half):

        def plain(j, carry):
            rows_ref[pl.ds(pl.multiple_of(j * slots, slots), slots), :] = recv_ref[j]
            return carry

        lax.fori_loop(0, peers, plain, 0)
        return
    half, quarter = slots // 2, slots // 4
    lane = lax.broadcasted_iota(jnp.int32, (quarter, LANES), 1)

    def body(j, carry):
        base = pl.multiple_of(j * slots, slots)
        wide = recv_ref[j, 0:half].astype(f32)
        narrow = recv_ref[j, half : half + quarter].astype(f32)
        turned = pltpu.roll(wide, 64, 1)
        fronts = (wide[:quarter], wide[quarter:], turned[:quarter], turned[quarter:])
        for g in range(4):
            back = pltpu.roll(narrow, (64 - g * 32) % LANES, 1)
            back = jnp.where(lane < 96, back, 0.0)
            rows_ref[pl.ds(base + g * quarter, quarter), :] = jnp.where(
                lane < 64, fronts[g], back
            ).astype(bf16)
        return carry

    lax.fori_loop(0, peers, body, 0)


def root_columns(degree_ref, function):
    blocks, block = degree_ref.shape
    values = function(degree_ref[...].astype(f32))
    return jnp.transpose(jnp.concatenate([values, jnp.zeros((block - blocks, block), f32)], 0))


def over_lanes(columns, b):
    return jnp.broadcast_to(columns[:, b : b + 1], columns.shape)


def first_kernel(class_half, core_ref, count_ref, nodes_ref, rows_ref, labels_in_ref, logits_in_ref, degree_in_ref,
                 out_ref, value_ref, labels_ref, logits_ref, degree_ref, wide_ref, diff_ref, v_ref, stage_ref,
                 packed_ref, value_v, idx_ref, idx_sems, sems, own_sems):
    classes, unused, batch = logits_ref.shape
    entries = [
        pltpu.make_async_copy(source, target, own_sems.at[1 + i])
        for i, (source, target) in enumerate(
            ((logits_in_ref, logits_ref), (labels_in_ref, labels_ref), (degree_in_ref, degree_ref))
        )
    ]
    for copy in entries:
        copy.start()
    peers = packed_ref.shape[0]
    slots = stage_ref.shape[0] // peers
    flat = []
    if rows_ref.ndim == 1:
        idx_ref = rows_ref
    else:
        for j in range(peers):
            to = idx_ref.at[pl.ds(j * slots, slots)]
            flat.append(pltpu.make_async_copy(rows_ref.at[j], to, idx_sems.at[j]))
    for copy in flat:
        copy.start()
    blocks, block = degree_ref.shape
    core = core_ref[0]
    v_ref[...] = jnp.zeros_like(v_ref)
    wide_ref[...] = jnp.zeros_like(wide_ref)
    for copy in entries:
        copy.wait()
    logits = logits_ref[...].reshape(classes, batch)
    shifted = jnp.exp(logits - jnp.max(logits, axis=0, keepdims=True))
    hot = lax.broadcasted_iota(jnp.int32, (classes, batch), 0) == labels_ref[...]
    probs = shifted / jnp.sum(shifted, axis=0, keepdims=True)
    wide_ref[0:classes, :] = probs - jnp.where(hot, 1.0, 0.0)
    chosen = wide_ref[pl.ds(pl.multiple_of(core * class_half, 8), LANES), :]
    lane = lax.broadcasted_iota(jnp.int32, (batch, LANES), 1)
    diff_ref[...] = jnp.where(lane < class_half, jnp.transpose(chosen), 0.0)

    def add_row(i, carry):
        at = pl.ds(nodes_ref[i], 1)
        v_ref[at, :] = v_ref[at, :] + diff_ref[pl.ds(i, 1), :]
        return carry

    lax.fori_loop(0, batch, add_row, 0, unroll=8)
    roots = root_columns(degree_ref, lax.rsqrt)
    for b in range(blocks):
        at = slice(b * block, (b + 1) * block)
        scaled = over_lanes(roots, b) * v_ref[at, :]
        value_v[at, :] = scaled.astype(bf16)
        v_ref[at, :] = scaled
    value_copy = pltpu.make_async_copy(value_v, value_ref, own_sems.at[0])
    value_copy.start()
    for copy in flat:
        copy.wait()
    send_packed(v_ref, count_ref, idx_ref, stage_ref, packed_ref, out_ref, sems, slots, class_half)
    value_copy.wait()
    wait_packed(packed_ref, out_ref, sems)


def add_tiles(acc_ref, source_ref, tile_refs, meta_ref, target_base, source_base, stride):
    count, block = tile_refs[0].shape[0], tile_refs[0].shape[1]
    for which, tiles in enumerate(tile_refs):
        for t in range(count):
            target = meta_ref[which * stride + target_base + t]
            source = meta_ref[which * stride + source_base + t]
            product = jnp.dot(
                tiles[t],
                source_ref[pl.ds(pl.multiple_of(source * block, block), block), :],
                preferred_element_type=f32,
            )
            at = pl.ds(pl.multiple_of(target * block, block), block)
            acc_ref[at, :] = acc_ref[at, :] + product


class Part:
    def __init__(self, ref, offset):
        self.ref, self.offset = ref, offset

    def __getitem__(self, i):
        return self.ref[self.offset + i]


def turn_kernel(core_ref, first_ref, bias_ref, second_ref, first_out, bias_out, second_out, first_v, bias_v, second_v,
                in_sems, out_sems):
    core = core_ref[0]
    half = second_ref.shape[0] // 2
    steps = []
    for i in range(2):
        source = pl.ds(pl.multiple_of((core ^ i) * half, half), half)
        to = pl.ds(i * half, half)
        for k, (array, held, out) in enumerate(
            (
                (second_ref.at[source], second_v.at[to], second_out.at[to]),
                (first_ref.at[:, source], first_v.at[:, to], first_out.at[:, to]),
                (bias_ref.at[:, source], bias_v.at[:, to], bias_out.at[:, to]),
            )
        ):
            steps.append(
                (
                    pltpu.make_async_copy(array, held, in_sems.at[3 * i + k]),
                    pltpu.make_async_copy(held, out, out_sems.at[3 * i + k]),
                )
            )
    for copy_in, unused in steps:
        copy_in.start()
    for copy_in, copy_out in steps:
        copy_in.wait()
        copy_out.start()
    for unused, copy_out in steps:
        copy_out.wait()


def far_kernel(slots, class_half, stride, last, ints_ref, degree_in_ref, recv_ref,
               own_halo_ref, other_halo_ref, value_in_ref, own_local_ref, other_local_ref, *rest):
    if last:
        (total_ref, keep_ref, send_ref, ints, degree_ref, recv_v, tiles_v, value_in_v, rows_ref, acc_ref, total_v,
         own_sems) = rest
    else:
        (out_ref, value_ref, ints, degree_ref, recv_v, tiles_v, value_in_v, rows_ref, acc_ref, stage_ref, packed_ref,
         value_v, sems, own_sems) = rest
    core_ref, count_ref = Part(ints, 0), Part(ints, 1)
    meta_ref, idx_ref = Part(ints, LANES), Part(ints, LANES + 2 * stride)
    degree_copy = pltpu.make_async_copy(degree_in_ref, degree_ref, own_sems.at[7])
    degree_copy.start()
    ints_copy = pltpu.make_async_copy(ints_ref, ints, own_sems.at[8])
    ints_copy.start()
    local_count, block = own_local_ref.shape[0], own_local_ref.shape[1]
    halo_count = own_halo_ref.shape[0]
    blocks = degree_ref.shape[0]
    tiles = []
    start = 0
    for ref in (own_local_ref, other_local_ref, own_halo_ref, other_halo_ref):
        tiles.append(tiles_v.at[pl.ds(start, ref.shape[0])])
        start += ref.shape[0]
    copies = [
        pltpu.make_async_copy(value_in_ref, value_in_v, own_sems.at[0]),
        pltpu.make_async_copy(own_local_ref, tiles[0], own_sems.at[1]),
        pltpu.make_async_copy(other_local_ref, tiles[1], own_sems.at[2]),
        pltpu.make_async_copy(recv_ref, recv_v, own_sems.at[3]),
        pltpu.make_async_copy(own_halo_ref, tiles[2], own_sems.at[4]),
        pltpu.make_async_copy(other_halo_ref, tiles[3], own_sems.at[5]),
    ]
    for copy in copies:
        copy.start()
    if last:
        total_copy = pltpu.make_async_copy(total_ref, total_v, own_sems.at[6])
        total_copy.start()
    degree_copy.wait()
    roots = root_columns(degree_ref, lax.rsqrt)
    if last:
        columns = root_columns(degree_ref, lambda degree: (teleport / (1.0 - teleport)) * degree)
        total_copy.wait()
        copies[0].wait()
        for b in range(blocks):
            at = slice(b * block, (b + 1) * block)
            total = total_v[at, :].astype(f32) + value_in_v[at, :].astype(f32)
            acc_ref[at, :] = over_lanes(columns, b) * total
    else:
        acc_ref[...] = jnp.zeros_like(acc_ref)
        copies[0].wait()
    for copy in copies[1:3]:
        copy.wait()
    ints_copy.wait()
    add_tiles(acc_ref, value_in_v, (tiles[0], tiles[1]), meta_ref, 0, local_count, stride)
    copies[3].wait()
    unpack_rows(recv_v, rows_ref, slots, class_half)
    for copy in copies[4:]:
        copy.wait()
    base = 2 * local_count
    add_tiles(acc_ref, rows_ref, (tiles[2], tiles[3]), meta_ref, base, base + halo_count, stride)
    rate = 1.0 - teleport
    if last:
        half_blocks = blocks // 2
        core = core_ref[0]
        for b in range(half_blocks):
            to = slice(b * block, (b + 1) * block)
            outs = []
            for b_at in (b, half_blocks + b):
                at = slice(b_at * block, (b_at + 1) * block)
                outs.append((rate * over_lanes(roots, b_at) * acc_ref[at, :]).astype(bf16))
            keep_ref[to, :] = jnp.where(core == 0, outs[0], outs[1])
            send_ref[to, :] = jnp.where(core == 0, outs[1], outs[0])
        return
    for b in range(blocks):
        at = slice(b * block, (b + 1) * block)
        root = over_lanes(roots, b)
        scaled = (rate * root * root) * acc_ref[at, :]
        value_v[at, :] = scaled.astype(bf16)
        acc_ref[at, :] = scaled
    value_copy = pltpu.make_async_copy(value_v, value_ref, own_sems.at[6])
    value_copy.start()
    send_packed(acc_ref, count_ref, idx_ref, stage_ref, packed_ref, out_ref, sems, slots, class_half)
    value_copy.wait()
    wait_packed(packed_ref, out_ref, sems)


def finish_kernel(class_half, core_ref, mine_one, theirs_one, mine_two, theirs_two, first_ref, first_bias_ref,
                  second_ref, second_bias_ref, third_ref, wide_v, out_sems):
    one = mine_one.shape[0]
    hidden = second_ref.shape[0]
    feat = first_ref.shape[0]
    classes = third_ref.shape[0]
    half, feat_half = hidden // 2, feat // 2
    is_first = core_ref[0] == 0

    def both(start, count):
        mine_ref, theirs_ref = (mine_one, theirs_one) if start < one else (mine_two, theirs_two)
        at = start if start < one else start - one
        mine = mine_ref[at : at + count, :].astype(f32)
        theirs = theirs_ref[at : at + count, :].astype(f32)
        return jnp.where(is_first, mine, theirs), jnp.where(is_first, theirs, mine)

    step = math.gcd(one, half)
    outs = []
    for start in range(0, half, step):
        for k, value in enumerate(both(start, step)):
            at = k * half + start
            wide_v[at : at + step, :] = value
            out = pltpu.make_async_copy(
                wide_v.at[pl.ds(at, step)], second_ref.at[pl.ds(at, step)], out_sems.at[2 * (start // step) + k]
            )
            out.start()
            outs.append(out)
    low, high = both(half + feat_half, class_half)
    third_ref[0:class_half, :] = low
    third_ref[class_half:classes, :] = high[: classes - class_half]
    firsts = both(half, feat_half)
    biases = both(half + feat_half + class_half, 8)
    for k in range(2):
        at = slice(k * half, (k + 1) * half)
        first_ref[0:feat_half, at] = firsts[k][:, :half]
        first_ref[feat_half:feat, at] = firsts[k][:, half:]
        first_bias_ref[:, at] = biases[k][:1, :half]
        second_bias_ref[:, at] = biases[k][:1, half:]
    for out in outs:
        out.wait()


def gelu_parts(x):
    k = math.sqrt(2.0 / math.pi)
    square = x * x
    t = jnp.tanh(x * (k + (k * 0.044715) * square))
    half_up = 0.5 + 0.5 * t
    slope = half_up + (0.5 * x) * (1.0 - t * t) * (k + (3.0 * k * 0.044715) * square)
    return (x * half_up).astype(bf16), slope.astype(bf16)


def swap_cores(x):
    return lax.ppermute(x, "col", [(0, 1), (1, 0)])


def exchange(x, first_step, second_step):
    domains, cores = lax.axis_size("dom"), lax.axis_size("col")
    steps = (first_step, second_step)
    pairs = [
        (d * cores + c, (d ^ steps[c]) * cores + c) for d in range(domains) for c in range(cores)
    ]
    return lax.ppermute(x, ("dom", "col"), pairs)


def halving_steps():
    domains = lax.axis_size("dom")
    bits = [1 << b for b in range(domains.bit_length() - 1)]
    other = list(bits)
    if len(bits) > 1:
        other[0], other[1] = other[1], other[0]
    return list(zip(bits, other))


def split(x, axis):
    half = x.shape[axis] // 2
    return lax.slice_in_dim(x, 0, half, axis=axis), lax.slice_in_dim(x, half, 2 * half, axis=axis)


def sum_over_domains(x):
    me, core = lax.axis_index("dom"), lax.axis_index("col")
    plan = []
    width, depth = x.shape[1], x.shape[0]
    for steps in halving_steps():
        if width > LANES:
            plan.append((steps, 1))
            width //= 2
        else:
            plan.append((steps, 0))
            depth //= 2
    current = x
    bits = []
    for (a, b), axis in plan:
        up = jnp.where(core == 0, me & a, me & b) != 0
        bits.append(up)
        low, high = split(current, axis)
        got = exchange(jnp.where(up, low, high), a, b)
        keep = jnp.where(up, high, low)
        current = (keep.astype(f32) + got.astype(f32)).astype(bf16)
    for ((a, b), axis), up in zip(plan[::-1], bits[::-1]):
        got = exchange(current, a, b)
        current = jnp.where(
            up,
            jnp.concatenate([got, current], axis),
            jnp.concatenate([current, got], axis),
        )
    return current


def shards(
    features,
    first_weight,
    first_bias,
    second_weight,
    second_bias,
    third_weight,
    local_tiles,
    local_target,
    local_source,
    halo_tiles,
    halo_target,
    halo_block,
    send_rows,
    send_count,
    degree,
    batch_nodes,
    labels,
    batch_logits,
):
    rows = degree.shape[0]
    classes = batch_logits.shape[-1]
    batch = batch_logits.shape[1]
    block = local_tiles.shape[-1]
    blocks = rows // block
    peers, slots = send_rows.shape[1], send_rows.shape[2]
    hidden = second_weight.shape[0]
    class_half = (classes // 2 + 7) // 8 * 8
    core = lax.axis_index("col").astype(jnp.int32)
    core_arg = core.reshape(1)
    packed = packed_rows(slots, class_half)
    local_count, halo_count = local_tiles.shape[2], halo_tiles.shape[2]

    stride = 2 * (local_count + halo_count)
    degree_blocks = degree.reshape(blocks, block)
    out_type = jax.ShapeDtypeStruct((peers, packed, LANES), bf16)
    value_type = jax.ShapeDtypeStruct((rows, LANES), bf16)
    half_type = jax.ShapeDtypeStruct((rows // 2, LANES), bf16)
    acc = pltpu.VMEM((rows, LANES), f32)
    sending = [
        pltpu.VMEM((peers * slots, LANES), f32),
        pltpu.VMEM((peers, packed, LANES), bf16),
        pltpu.VMEM((rows, LANES), bf16),
    ]
    peer_sems = pltpu.SemaphoreType.DMA((peers,))

    counts = send_count[0]
    whole_tiles = slots % LANES == 0
    first_rows = send_rows[0] if whole_tiles else send_rows[0].reshape(-1)
    out, value = pl.pallas_call(
        functools.partial(first_kernel, class_half),
        out_shape=(out_type, value_type),
        in_specs=[smem()] * 3 + [vmem() if whole_tiles else smem()] + [hbm()] * 3,
        out_specs=(hbm(), hbm()),
        scratch_shapes=[
            pltpu.VMEM((1, batch), jnp.int32),
            pltpu.VMEM((classes, 1, batch), f32),
            pltpu.VMEM((blocks, block), jnp.int32),
            pltpu.VMEM((2 * LANES, batch), f32),
            pltpu.VMEM((batch, LANES), f32),
            acc,
            *sending,
            pltpu.SMEM((peers * slots,), jnp.int32),
            peer_sems,
            peer_sems,
            pltpu.SemaphoreType.DMA((4,)),
        ],
        compiler_params=params(),
        name="first",
    )(core_arg, counts, batch_nodes[0], first_rows, labels, jnp.transpose(batch_logits, (2, 0, 1)), degree_blocks)
    first_w, first_b, second_w, _ = lax.optimization_barrier((first_weight, first_bias, second_weight, value))
    first_turned, bias_turned, second_turned = pl.pallas_call(
        turn_kernel,
        out_shape=(
            jax.ShapeDtypeStruct(first_w.shape, bf16),
            jax.ShapeDtypeStruct((1, hidden), f32),
            jax.ShapeDtypeStruct(second_w.shape, bf16),
        ),
        in_specs=[smem(), hbm(), hbm(), hbm()],
        out_specs=(hbm(), hbm(), hbm()),
        scratch_shapes=[
            pltpu.VMEM(first_w.shape, bf16),
            pltpu.VMEM((1, hidden), f32),
            pltpu.VMEM(second_w.shape, bf16),
            pltpu.SemaphoreType.DMA((6,)),
            pltpu.SemaphoreType.DMA((6,)),
        ],
        compiler_params=params(),
        name="turn",
    )(core_arg, first_w, first_b.reshape(1, hidden), second_w)
    tied_rows, *lists, first_turned = lax.optimization_barrier(
        (send_rows, local_target, local_source, halo_target, halo_block, first_turned)
    )
    meta_own = jnp.concatenate([part[0, 0] for part in lists])
    total_ints = LANES + 2 * stride + peers * slots
    ints = jnp.concatenate(
        [
            core_arg,
            counts,
            jnp.zeros((LANES - 1 - peers,), jnp.int32),
            meta_own,
            swap_cores(meta_own),
            tied_rows.reshape(-1),
            jnp.zeros((-total_ints % 1024,), jnp.int32),
        ]
    )
    own_local, own_halo = local_tiles[0, 0], halo_tiles[0, 0]
    other_local, other_halo = swap_cores(own_local), swap_cores(own_halo)

    values = []
    for hop in range(HOPS):
        last = hop + 1 == HOPS
        values.insert(0, value)
        landed = lax.all_to_all(out, "dom", split_axis=0, concat_axis=0, tiled=True)
        extra = []
        if hop == 0:
            value, first_turned, bias_turned, second_turned = lax.optimization_barrier(
                (value, first_turned, bias_turned, second_turned)
            )
        if hop == 1:
            x, third_w, _ = lax.optimization_barrier((features, third_weight, value))
            pre_first = jnp.dot(x, first_turned, preferred_element_type=f32) + bias_turned
            low = jnp.pad(third_w[:, :class_half], ((0, 0), (0, LANES - class_half)))
            high = jnp.pad(third_w[:, class_half:], ((0, 0), (0, LANES - classes + class_half)))
            third = jnp.where(core == 0, jnp.concatenate([low, high], 1), jnp.concatenate([high, low], 1))
            value, hidden_first, slope_first, third = lax.optimization_barrier((value, *gelu_parts(pre_first), third))
        if hop == 2:
            tied, _ = lax.optimization_barrier((hidden_first, value))
            pre_second = jnp.dot(tied, second_turned, preferred_element_type=f32)
            value, pre_second = lax.optimization_barrier((value, pre_second))
        if last:
            tied, *earlier, _ = lax.optimization_barrier((pre_second, *values[1:], value))
            total = sum(part.astype(f32) for part in earlier).astype(bf16)
            value, hidden_second, slope_second, total = lax.optimization_barrier(
                (value, *gelu_parts(tied + second_bias), total)
            )
            extra = [total]
        result = pl.pallas_call(
            functools.partial(far_kernel, slots, class_half, stride, last),
            out_shape=(half_type, half_type) if last else (out_type, value_type),
            in_specs=[hbm()] * (8 + len(extra)),
            out_specs=(vmem(), vmem()) if last else (hbm(), hbm()),
            scratch_shapes=[
                pltpu.SMEM(ints.shape, jnp.int32),
                pltpu.VMEM((blocks, block), jnp.int32),
                pltpu.VMEM((peers, packed, LANES), bf16),
                pltpu.VMEM((2 * (local_count + halo_count), block, block), bf16),
                pltpu.VMEM((rows, LANES), bf16),
                pltpu.VMEM((peers * slots, LANES), bf16),
                acc,
            ]
            + ([pltpu.VMEM((rows, LANES), bf16)] if last else sending + [peer_sems])
            + [pltpu.SemaphoreType.DMA((9,))],
            compiler_params=params(),
            name="far_last" if last else "far",
        )(ints, degree_blocks, landed, own_halo, other_halo, value, own_local, other_local, *extra)
        if last:
            keep, send = result
        else:
            out, value = result

    got = swap_cores(send)
    delta = jnp.concatenate([keep, got], axis=1)

    def contract(a, b):
        return lax.dot_general(a, b, (((0,), (0,)), ((), ())), preferred_element_type=f32).astype(bf16)

    half, feat = hidden // 2, x.shape[1]
    lead = half // 4 * 3
    back_second = lax.dot_general(delta, third, (((1,), (1,)), ((), ())), preferred_element_type=f32)
    second_delta = (slope_second.astype(f32) * back_second).astype(bf16)
    second_bias_grad = jnp.sum(second_delta.astype(f32), axis=0).astype(bf16)
    send_lead = contract(hidden_first[:, half : half + lead], second_delta)
    got_lead = swap_cores(send_lead)
    keep_lead = contract(hidden_first[:, :lead], second_delta)
    send_tail = contract(hidden_first[:, half + lead :], second_delta)
    keep_tail = contract(hidden_first[:, lead:half], second_delta)
    third_grad = contract(delta, hidden_second)
    back_first = lax.dot_general(
        second_delta, second_turned, (((1,), (1,)), ((), ())), preferred_element_type=f32
    )
    first_delta = (slope_first.astype(f32) * back_first).astype(bf16)
    first_grad = contract(x, first_delta)
    first_bias_grad = jnp.sum(first_delta.astype(f32), axis=0).astype(bf16)

    is_first = core == 0
    domains = lax.axis_size("dom")
    column_splits = (hidden // LANES).bit_length() - 1
    grain = 8 * max(1, domains >> column_splits)
    used = half - lead + feat // 2 + class_half
    tail_rows = -(-(used + 1) // grain) * grain

    def bundle(part, tail, third_rows, bias_half):
        at = slice(part * half, (part + 1) * half)
        first_rows = jnp.concatenate([first_grad[: feat // 2, at], first_grad[feat // 2 :, at]], 1)
        bias_row = jnp.concatenate([first_bias_grad[at], bias_half])
        bias = jnp.broadcast_to(bias_row[None], (tail_rows - used, hidden))
        return jnp.concatenate([tail, first_rows, third_rows[:class_half], bias], 0)

    low_bias, high_bias = split(second_bias_grad, 0)
    keep_rest = bundle(0, keep_tail, third_grad[:LANES], jnp.where(is_first, low_bias, high_bias))
    send_rest = bundle(1, send_tail, third_grad[LANES:], jnp.where(is_first, high_bias, low_bias))
    got_rest = swap_cores(send_rest)
    mine_lead = sum_over_domains((keep_lead.astype(f32) + got_lead.astype(f32)).astype(bf16))
    mine_rest = sum_over_domains((keep_rest.astype(f32) + got_rest.astype(f32)).astype(bf16))
    theirs_lead, theirs_rest = swap_cores(mine_lead), swap_cores(mine_rest)
    first_out, first_bias_out, second_out, second_bias_out, third_out = pl.pallas_call(
        functools.partial(finish_kernel, class_half),
        out_shape=(
            jax.ShapeDtypeStruct((feat, hidden), f32),
            jax.ShapeDtypeStruct((1, hidden), f32),
            jax.ShapeDtypeStruct((hidden, hidden), f32),
            jax.ShapeDtypeStruct((1, hidden), f32),
            jax.ShapeDtypeStruct((classes, hidden), f32),
        ),
        in_specs=[smem()] + [vmem()] * 4,
        out_specs=(vmem(), vmem(), hbm(), vmem(), vmem()),
        scratch_shapes=[
            pltpu.VMEM((hidden, hidden), f32),
            pltpu.SemaphoreType.DMA((2 * (half // math.gcd(lead, half)),)),
        ],
        compiler_params=pltpu.CompilerParams(vmem_limit_bytes=24 * 1024 * 1024),
        name="finish",
    )(core_arg, mine_lead, theirs_lead, mine_rest, theirs_rest)
    return first_out, first_bias_out.reshape(hidden), second_out, second_bias_out.reshape(hidden), third_out.T


def solution(mesh):
    return jax.shard_map(
        shards,
        mesh=mesh,
        in_specs=(
            P(("grp", "dom", "col"), None),
            P(),
            P(),
            P(),
            P(),
            P(),
            P(("grp", "dom"), "col", None, None, None),
            P(("grp", "dom"), "col", None),
            P(("grp", "dom"), "col", None),
            P(("grp", "dom"), "col", None, None, None),
            P(("grp", "dom"), "col", None),
            P(("grp", "dom"), "col", None),
            P(("grp", "dom"), None, None),
            P(("grp", "dom"), None),
            P(("grp", "dom")),
            P(("grp", "dom"), None),
            P(("grp", "dom"), None),
            P(("grp", "dom"), None, None),
        ),
        out_specs=(P("grp", None), P("grp"), P("grp", None), P("grp"), P("grp", None)),
        check_vma=False,
    )
```

```python
import functools
import math

import jax
import jax.numpy as jnp
from jax import lax
from jax.experimental import pallas as pl
from jax.experimental.pallas import tpu as pltpu
from jax.sharding import PartitionSpec as P

HOPS = 4
teleport = 0.1
LANES = 128
UNROLL = 16
VMEM_LIMIT = 60 * 1024 * 1024

bf16 = jnp.bfloat16
f32 = jnp.float32


def vmem():
    return pl.BlockSpec(memory_space=pltpu.VMEM)


def smem():
    return pl.BlockSpec(memory_space=pltpu.SMEM)


def hbm():
    return pl.BlockSpec(memory_space=pltpu.HBM)


def params():
    return pltpu.CompilerParams(vmem_limit_bytes=VMEM_LIMIT)


def is_packed(slots, class_half):
    return slots % 64 == 0 and class_half <= 96


def packed_rows(slots, class_half):
    return slots * 3 // 4 if is_packed(slots, class_half) else slots


def send_packed(v_ref, count_ref, idx_ref, stage_ref, packed_ref, out_ref, sems, slots, class_half):
    peers = packed_ref.shape[0]

    def gather(j, carry):
        first = j * slots

        def body(g, inner):
            base = pl.multiple_of(first + g * UNROLL, UNROLL)
            for u in range(UNROLL):
                stage_ref[pl.ds(base + u, 1), :] = v_ref[pl.ds(idx_ref[base + u], 1), :]
            return inner

        return lax.fori_loop(0, (count_ref[j] + (UNROLL - 1)) // UNROLL, body, carry)

    lax.fori_loop(0, peers, gather, 0)
    half, quarter = slots // 2, slots // 4
    row = lax.broadcasted_iota(jnp.int32, (slots, LANES), 0)
    lane_a = lax.broadcasted_iota(jnp.int32, (half, LANES), 1)
    lane_b = lax.broadcasted_iota(jnp.int32, (quarter, LANES), 1) // 32

    def peer(j, carry):
        base = pl.multiple_of(j * slots, slots)
        taken = jnp.where(row < count_ref[j], stage_ref[pl.ds(base, slots), :], 0.0)
        if is_packed(slots, class_half):
            low, high = taken[:half], taken[half:]
            packed_ref[j, 0:half] = jnp.where(lane_a < 64, low, pltpu.roll(high, 64, 1)).astype(bf16)
            parts = (low[:quarter], low[quarter:], high[:quarter], high[quarter:])
            narrow = jnp.zeros((quarter, LANES), f32)
            for g in range(4):
                narrow = jnp.where(lane_b == g, pltpu.roll(parts[g], (g * 32 - 64) % LANES, 1), narrow)
            packed_ref[j, half : half + quarter] = narrow.astype(bf16)
        else:
            packed_ref[j] = taken.astype(bf16)
        pltpu.make_async_copy(packed_ref.at[j], out_ref.at[j], sems.at[j]).start()
        return carry

    lax.fori_loop(0, peers, peer, 0)


def wait_packed(packed_ref, out_ref, sems):
    def peer(j, carry):
        pltpu.make_async_copy(packed_ref.at[j], out_ref.at[j], sems.at[j]).wait()
        return carry

    lax.fori_loop(0, packed_ref.shape[0], peer, 0)


def unpack_rows(recv_ref, rows_ref, slots, class_half):
    peers = recv_ref.shape[0]
    if not is_packed(slots, class_half):

        def plain(j, carry):
            rows_ref[pl.ds(pl.multiple_of(j * slots, slots), slots), :] = recv_ref[j]
            return carry

        lax.fori_loop(0, peers, plain, 0)
        return
    half, quarter = slots // 2, slots // 4
    lane = lax.broadcasted_iota(jnp.int32, (quarter, LANES), 1)

    def body(j, carry):
        base = pl.multiple_of(j * slots, slots)
        wide = recv_ref[j, 0:half].astype(f32)
        narrow = recv_ref[j, half : half + quarter].astype(f32)
        turned = pltpu.roll(wide, 64, 1)
        fronts = (wide[:quarter], wide[quarter:], turned[:quarter], turned[quarter:])
        for g in range(4):
            back = pltpu.roll(narrow, (64 - g * 32) % LANES, 1)
            back = jnp.where(lane < 96, back, 0.0)
            rows_ref[pl.ds(base + g * quarter, quarter), :] = jnp.where(
                lane < 64, fronts[g], back
            ).astype(bf16)
        return carry

    lax.fori_loop(0, peers, body, 0)


def root_columns(degree_ref, function):
    blocks, block = degree_ref.shape
    values = function(degree_ref[...].astype(f32))
    return jnp.transpose(jnp.concatenate([values, jnp.zeros((block - blocks, block), f32)], 0))


def over_lanes(columns, b):
    return jnp.broadcast_to(columns[:, b : b + 1], columns.shape)


def first_kernel(class_half, core_ref, count_ref, nodes_ref, rows_ref, labels_ref, logits_ref, degree_ref,
                 out_ref, value_ref, wide_ref, diff_ref, v_ref, stage_ref, packed_ref, value_v, idx_ref, idx_sems,
                 sems, own_sems):
    classes, unused, batch = logits_ref.shape
    peers = packed_ref.shape[0]
    slots = stage_ref.shape[0] // peers
    flat = []
    if rows_ref.ndim == 1:
        idx_ref = rows_ref
    else:
        for j in range(peers):
            to = idx_ref.at[pl.ds(j * slots, slots)]
            flat.append(pltpu.make_async_copy(rows_ref.at[j], to, idx_sems.at[j]))
    for copy in flat:
        copy.start()
    blocks, block = degree_ref.shape
    core = core_ref[0]
    logits = logits_ref[...].reshape(classes, batch)
    shifted = jnp.exp(logits - jnp.max(logits, axis=0, keepdims=True))
    hot = lax.broadcasted_iota(jnp.int32, (classes, batch), 0) == labels_ref[...]
    probs = shifted / jnp.sum(shifted, axis=0, keepdims=True)
    wide_ref[...] = jnp.zeros_like(wide_ref)
    wide_ref[0:classes, :] = probs - jnp.where(hot, 1.0, 0.0)
    chosen = wide_ref[pl.ds(pl.multiple_of(core * class_half, 8), LANES), :]
    lane = lax.broadcasted_iota(jnp.int32, (batch, LANES), 1)
    diff_ref[...] = jnp.where(lane < class_half, jnp.transpose(chosen), 0.0)
    v_ref[...] = jnp.zeros_like(v_ref)

    def add_row(i, carry):
        at = pl.ds(nodes_ref[i], 1)
        v_ref[at, :] = v_ref[at, :] + diff_ref[pl.ds(i, 1), :]
        return carry

    lax.fori_loop(0, batch, add_row, 0, unroll=8)
    roots = root_columns(degree_ref, lax.rsqrt)
    for b in range(blocks):
        at = slice(b * block, (b + 1) * block)
        scaled = over_lanes(roots, b) * v_ref[at, :]
        value_v[at, :] = scaled.astype(bf16)
        v_ref[at, :] = scaled
    value_copy = pltpu.make_async_copy(value_v, value_ref, own_sems.at[0])
    value_copy.start()
    for copy in flat:
        copy.wait()
    send_packed(v_ref, count_ref, idx_ref, stage_ref, packed_ref, out_ref, sems, slots, class_half)
    value_copy.wait()
    wait_packed(packed_ref, out_ref, sems)


def add_tiles(acc_ref, source_ref, tile_refs, meta_ref, target_base, source_base, stride):
    count, block = tile_refs[0].shape[0], tile_refs[0].shape[1]
    for which, tiles in enumerate(tile_refs):
        for t in range(count):
            target = meta_ref[which * stride + target_base + t]
            source = meta_ref[which * stride + source_base + t]
            product = jnp.dot(
                tiles[t],
                source_ref[pl.ds(pl.multiple_of(source * block, block), block), :],
                preferred_element_type=f32,
            )
            at = pl.ds(pl.multiple_of(target * block, block), block)
            acc_ref[at, :] = acc_ref[at, :] + product


class Part:
    def __init__(self, ref, offset):
        self.ref, self.offset = ref, offset

    def __getitem__(self, i):
        return self.ref[self.offset + i]


def turn_kernel(core_ref, first_ref, bias_ref, second_ref, first_out, bias_out, second_out, first_v, bias_v, second_v,
                in_sems, out_sems):
    core = core_ref[0]
    half = second_ref.shape[0] // 2
    steps = []
    for i in range(2):
        source = pl.ds(pl.multiple_of((core ^ i) * half, half), half)
        to = pl.ds(i * half, half)
        for k, (array, held, out) in enumerate(
            (
                (second_ref.at[source], second_v.at[to], second_out.at[to]),
                (first_ref.at[:, source], first_v.at[:, to], first_out.at[:, to]),
                (bias_ref.at[:, source], bias_v.at[:, to], bias_out.at[:, to]),
            )
        ):
            steps.append(
                (
                    pltpu.make_async_copy(array, held, in_sems.at[3 * i + k]),
                    pltpu.make_async_copy(held, out, out_sems.at[3 * i + k]),
                )
            )
    for copy_in, unused in steps:
        copy_in.start()
    for copy_in, copy_out in steps:
        copy_in.wait()
        copy_out.start()
    for unused, copy_out in steps:
        copy_out.wait()


def far_kernel(slots, class_half, stride, last, ints_ref, degree_in_ref, recv_ref,
               own_halo_ref, other_halo_ref, value_in_ref, own_local_ref, other_local_ref, *rest):
    if last:
        (total_ref, keep_ref, send_ref, ints, degree_ref, recv_v, tiles_v, value_in_v, rows_ref, acc_ref, total_v,
         own_sems) = rest
    else:
        (out_ref, value_ref, ints, degree_ref, recv_v, tiles_v, value_in_v, rows_ref, acc_ref, stage_ref, packed_ref,
         value_v, sems, own_sems) = rest
    core_ref, count_ref = Part(ints, 0), Part(ints, 1)
    meta_ref, idx_ref = Part(ints, LANES), Part(ints, LANES + 2 * stride)
    degree_copy = pltpu.make_async_copy(degree_in_ref, degree_ref, own_sems.at[7])
    degree_copy.start()
    ints_copy = pltpu.make_async_copy(ints_ref, ints, own_sems.at[8])
    ints_copy.start()
    local_count, block = own_local_ref.shape[0], own_local_ref.shape[1]
    halo_count = own_halo_ref.shape[0]
    blocks = degree_ref.shape[0]
    tiles = []
    start = 0
    for ref in (own_local_ref, other_local_ref, own_halo_ref, other_halo_ref):
        tiles.append(tiles_v.at[pl.ds(start, ref.shape[0])])
        start += ref.shape[0]
    copies = [
        pltpu.make_async_copy(value_in_ref, value_in_v, own_sems.at[0]),
        pltpu.make_async_copy(own_local_ref, tiles[0], own_sems.at[1]),
        pltpu.make_async_copy(other_local_ref, tiles[1], own_sems.at[2]),
        pltpu.make_async_copy(recv_ref, recv_v, own_sems.at[3]),
        pltpu.make_async_copy(own_halo_ref, tiles[2], own_sems.at[4]),
        pltpu.make_async_copy(other_halo_ref, tiles[3], own_sems.at[5]),
    ]
    for copy in copies:
        copy.start()
    if last:
        total_copy = pltpu.make_async_copy(total_ref, total_v, own_sems.at[6])
        total_copy.start()
    degree_copy.wait()
    roots = root_columns(degree_ref, lax.rsqrt)
    if last:
        columns = root_columns(degree_ref, lambda degree: (teleport / (1.0 - teleport)) * degree)
        total_copy.wait()
        copies[0].wait()
        for b in range(blocks):
            at = slice(b * block, (b + 1) * block)
            total = total_v[at, :].astype(f32) + value_in_v[at, :].astype(f32)
            acc_ref[at, :] = over_lanes(columns, b) * total
    else:
        acc_ref[...] = jnp.zeros_like(acc_ref)
        copies[0].wait()
    for copy in copies[1:3]:
        copy.wait()
    ints_copy.wait()
    add_tiles(acc_ref, value_in_v, (tiles[0], tiles[1]), meta_ref, 0, local_count, stride)
    copies[3].wait()
    unpack_rows(recv_v, rows_ref, slots, class_half)
    for copy in copies[4:]:
        copy.wait()
    base = 2 * local_count
    add_tiles(acc_ref, rows_ref, (tiles[2], tiles[3]), meta_ref, base, base + halo_count, stride)
    rate = 1.0 - teleport
    if last:
        half_blocks = blocks // 2
        core = core_ref[0]
        for b in range(half_blocks):
            to = slice(b * block, (b + 1) * block)
            outs = []
            for b_at in (b, half_blocks + b):
                at = slice(b_at * block, (b_at + 1) * block)
                outs.append((rate * over_lanes(roots, b_at) * acc_ref[at, :]).astype(bf16))
            keep_ref[to, :] = jnp.where(core == 0, outs[0], outs[1])
            send_ref[to, :] = jnp.where(core == 0, outs[1], outs[0])
        return
    for b in range(blocks):
        at = slice(b * block, (b + 1) * block)
        root = over_lanes(roots, b)
        scaled = (rate * root * root) * acc_ref[at, :]
        value_v[at, :] = scaled.astype(bf16)
        acc_ref[at, :] = scaled
    value_copy = pltpu.make_async_copy(value_v, value_ref, own_sems.at[6])
    value_copy.start()
    send_packed(acc_ref, count_ref, idx_ref, stage_ref, packed_ref, out_ref, sems, slots, class_half)
    value_copy.wait()
    wait_packed(packed_ref, out_ref, sems)


def write_rows(core_ref, mine_ref, theirs_ref, second_ref, wide_v, out_sems, start, count, step):
    half = second_ref.shape[0] // 2
    is_first = core_ref[0] == 0
    outs = []
    for at in range(0, count, step):
        mine = mine_ref[at : at + step, :].astype(f32)
        theirs = theirs_ref[at : at + step, :].astype(f32)
        pair = jnp.where(is_first, mine, theirs), jnp.where(is_first, theirs, mine)
        for k in range(2):
            here = pl.ds(k * count + at, step)
            wide_v[here, :] = pair[k]
            out = pltpu.make_async_copy(
                wide_v.at[here],
                second_ref.at[pl.ds(k * half + start + at, step)],
                out_sems.at[2 * (at // step) + k],
            )
            out.start()
            outs.append(out)
    return outs


def finish_lead_kernel(step, core_ref, mine_ref, theirs_ref, second_ref, wide_v, out_sems):
    count = mine_ref.shape[0]
    for out in write_rows(core_ref, mine_ref, theirs_ref, second_ref, wide_v, out_sems, 0, count, step):
        out.wait()


def finish_kernel(class_half, lead, step, core_ref, mine_ref, theirs_ref, unused_ref, first_ref, first_bias_ref,
                  second_ref, second_bias_ref, third_ref, wide_v, out_sems):
    half, feat = second_ref.shape[0] // 2, first_ref.shape[0]
    classes = third_ref.shape[0]
    feat_half = feat // 2
    count = half - lead
    outs = write_rows(core_ref, mine_ref, theirs_ref, second_ref, wide_v, out_sems, lead, count, step)
    is_first = core_ref[0] == 0

    def both(start, size):
        mine = mine_ref[start : start + size, :].astype(f32)
        theirs = theirs_ref[start : start + size, :].astype(f32)
        return jnp.where(is_first, mine, theirs), jnp.where(is_first, theirs, mine)

    low, high = both(count + feat_half, class_half)
    third_ref[0:class_half, :] = low
    third_ref[class_half:classes, :] = high[: classes - class_half]
    firsts = both(count, feat_half)
    biases = both(count + feat_half + class_half, 8)
    for k in range(2):
        at = slice(k * half, (k + 1) * half)
        first_ref[0:feat_half, at] = firsts[k][:, :half]
        first_ref[feat_half:feat, at] = firsts[k][:, half:]
        first_bias_ref[:, at] = biases[k][:1, :half]
        second_bias_ref[:, at] = biases[k][:1, half:]
    for out in outs:
        out.wait()


def gelu_parts(x):
    k = math.sqrt(2.0 / math.pi)
    square = x * x
    t = jnp.tanh(x * (k + (k * 0.044715) * square))
    half_up = 0.5 + 0.5 * t
    slope = half_up + (0.5 * x) * (1.0 - t * t) * (k + (3.0 * k * 0.044715) * square)
    return (x * half_up).astype(bf16), slope.astype(bf16)


def swap_cores(x):
    return lax.ppermute(x, "col", [(0, 1), (1, 0)])


def exchange(x, first_step, second_step):
    domains, cores = lax.axis_size("dom"), lax.axis_size("col")
    steps = (first_step, second_step)
    pairs = [
        (d * cores + c, (d ^ steps[c]) * cores + c) for d in range(domains) for c in range(cores)
    ]
    return lax.ppermute(x, ("dom", "col"), pairs)


def halving_steps():
    domains = lax.axis_size("dom")
    bits = [1 << b for b in range(domains.bit_length() - 1)]
    other = list(bits)
    if len(bits) > 1:
        other[0], other[1] = other[1], other[0]
    return list(zip(bits, other))


def split(x, axis):
    half = x.shape[axis] // 2
    return lax.slice_in_dim(x, 0, half, axis=axis), lax.slice_in_dim(x, half, 2 * half, axis=axis)


def sum_over_domains(x):
    me, core = lax.axis_index("dom"), lax.axis_index("col")
    plan = []
    width, depth = x.shape[1], x.shape[0]
    for steps in halving_steps():
        if width > LANES:
            plan.append((steps, 1))
            width //= 2
        else:
            plan.append((steps, 0))
            depth //= 2
    current = x
    bits = []
    for (a, b), axis in plan:
        up = jnp.where(core == 0, me & a, me & b) != 0
        bits.append(up)
        low, high = split(current, axis)
        got = exchange(jnp.where(up, low, high), a, b)
        keep = jnp.where(up, high, low)
        current = (keep.astype(f32) + got.astype(f32)).astype(bf16)
    for ((a, b), axis), up in zip(plan[::-1], bits[::-1]):
        got = exchange(current, a, b)
        current = jnp.where(
            up,
            jnp.concatenate([got, current], axis),
            jnp.concatenate([current, got], axis),
        )
    return current


def shards(
    features,
    first_weight,
    first_bias,
    second_weight,
    second_bias,
    third_weight,
    local_tiles,
    local_target,
    local_source,
    halo_tiles,
    halo_target,
    halo_block,
    send_rows,
    send_count,
    degree,
    batch_nodes,
    labels,
    batch_logits,
):
    rows = degree.shape[0]
    classes = batch_logits.shape[-1]
    batch = batch_logits.shape[1]
    block = local_tiles.shape[-1]
    blocks = rows // block
    peers, slots = send_rows.shape[1], send_rows.shape[2]
    hidden = second_weight.shape[0]
    class_half = (classes // 2 + 7) // 8 * 8
    core = lax.axis_index("col").astype(jnp.int32)
    core_arg = core.reshape(1)
    packed = packed_rows(slots, class_half)
    local_count, halo_count = local_tiles.shape[2], halo_tiles.shape[2]

    stride = 2 * (local_count + halo_count)
    degree_blocks = degree.reshape(blocks, block)
    out_type = jax.ShapeDtypeStruct((peers, packed, LANES), bf16)
    value_type = jax.ShapeDtypeStruct((rows, LANES), bf16)
    half_type = jax.ShapeDtypeStruct((rows // 2, LANES), bf16)
    acc = pltpu.VMEM((rows, LANES), f32)
    sending = [
        pltpu.VMEM((peers * slots, LANES), f32),
        pltpu.VMEM((peers, packed, LANES), bf16),
        pltpu.VMEM((rows, LANES), bf16),
    ]
    peer_sems = pltpu.SemaphoreType.DMA((peers,))

    counts = send_count[0]
    whole_tiles = slots % LANES == 0
    first_rows = send_rows[0] if whole_tiles else send_rows[0].reshape(-1)
    out, value = pl.pallas_call(
        functools.partial(first_kernel, class_half),
        out_shape=(out_type, value_type),
        in_specs=[smem()] * 3 + [vmem() if whole_tiles else smem()] + [vmem()] * 3,
        out_specs=(hbm(), hbm()),
        scratch_shapes=[
            pltpu.VMEM((2 * LANES, batch), f32),
            pltpu.VMEM((batch, LANES), f32),
            acc,
            *sending,
            pltpu.SMEM((peers * slots,), jnp.int32),
            peer_sems,
            peer_sems,
            pltpu.SemaphoreType.DMA((1,)),
        ],
        compiler_params=params(),
        name="first",
    )(core_arg, counts, batch_nodes[0], first_rows, labels, jnp.transpose(batch_logits, (2, 0, 1)), degree_blocks)
    first_w, first_b, second_w, _ = lax.optimization_barrier((first_weight, first_bias, second_weight, value))
    first_turned, bias_turned, second_turned = pl.pallas_call(
        turn_kernel,
        out_shape=(
            jax.ShapeDtypeStruct(first_w.shape, bf16),
            jax.ShapeDtypeStruct((1, hidden), f32),
            jax.ShapeDtypeStruct(second_w.shape, bf16),
        ),
        in_specs=[smem(), hbm(), hbm(), hbm()],
        out_specs=(hbm(), hbm(), hbm()),
        scratch_shapes=[
            pltpu.VMEM(first_w.shape, bf16),
            pltpu.VMEM((1, hidden), f32),
            pltpu.VMEM(second_w.shape, bf16),
            pltpu.SemaphoreType.DMA((6,)),
            pltpu.SemaphoreType.DMA((6,)),
        ],
        compiler_params=params(),
        name="turn",
    )(core_arg, first_w, first_b.reshape(1, hidden), second_w)
    tied_rows, *lists, first_turned = lax.optimization_barrier(
        (send_rows, local_target, local_source, halo_target, halo_block, first_turned)
    )
    meta_own = jnp.concatenate([part[0, 0] for part in lists])
    total_ints = LANES + 2 * stride + peers * slots
    ints = jnp.concatenate(
        [
            core_arg,
            counts,
            jnp.zeros((LANES - 1 - peers,), jnp.int32),
            meta_own,
            swap_cores(meta_own),
            tied_rows.reshape(-1),
            jnp.zeros((-total_ints % 1024,), jnp.int32),
        ]
    )
    own_local, own_halo = local_tiles[0, 0], halo_tiles[0, 0]
    other_local, other_halo = swap_cores(own_local), swap_cores(own_halo)

    values = []
    for hop in range(HOPS):
        last = hop + 1 == HOPS
        values.insert(0, value)
        landed = lax.all_to_all(out, "dom", split_axis=0, concat_axis=0, tiled=True)
        extra = []
        if hop == 0:
            value, first_turned, bias_turned, second_turned = lax.optimization_barrier(
                (value, first_turned, bias_turned, second_turned)
            )
        if hop == 1:
            x, third_w, _ = lax.optimization_barrier((features, third_weight, value))
            pre_first = jnp.dot(x, first_turned, preferred_element_type=f32) + bias_turned
            low = jnp.pad(third_w[:, :class_half], ((0, 0), (0, LANES - class_half)))
            high = jnp.pad(third_w[:, class_half:], ((0, 0), (0, LANES - classes + class_half)))
            third = jnp.where(core == 0, jnp.concatenate([low, high], 1), jnp.concatenate([high, low], 1))
            value, hidden_first, slope_first, third = lax.optimization_barrier((value, *gelu_parts(pre_first), third))
        if hop == 2:
            tied, _ = lax.optimization_barrier((hidden_first, value))
            pre_second = jnp.dot(tied, second_turned, preferred_element_type=f32)
            value, pre_second = lax.optimization_barrier((value, pre_second))
        if last:
            tied, *earlier, _ = lax.optimization_barrier((pre_second, *values[1:], value))
            total = sum(part.astype(f32) for part in earlier).astype(bf16)
            value, hidden_second, slope_second, total = lax.optimization_barrier(
                (value, *gelu_parts(tied + second_bias), total)
            )
            extra = [total]
        result = pl.pallas_call(
            functools.partial(far_kernel, slots, class_half, stride, last),
            out_shape=(half_type, half_type) if last else (out_type, value_type),
            in_specs=[hbm()] * (8 + len(extra)),
            out_specs=(vmem(), vmem()) if last else (hbm(), hbm()),
            scratch_shapes=[
                pltpu.SMEM(ints.shape, jnp.int32),
                pltpu.VMEM((blocks, block), jnp.int32),
                pltpu.VMEM((peers, packed, LANES), bf16),
                pltpu.VMEM((2 * (local_count + halo_count), block, block), bf16),
                pltpu.VMEM((rows, LANES), bf16),
                pltpu.VMEM((peers * slots, LANES), bf16),
                acc,
            ]
            + ([pltpu.VMEM((rows, LANES), bf16)] if last else sending + [peer_sems])
            + [pltpu.SemaphoreType.DMA((9,))],
            compiler_params=params(),
            name="far_last" if last else "far",
        )(ints, degree_blocks, landed, own_halo, other_halo, value, own_local, other_local, *extra)
        if last:
            keep, send = result
        else:
            out, value = result

    got = swap_cores(send)
    delta = jnp.concatenate([keep, got], axis=1)

    def contract(a, b):
        return lax.dot_general(a, b, (((0,), (0,)), ((), ())), preferred_element_type=f32).astype(bf16)

    half, feat = hidden // 2, x.shape[1]
    lead = half // 4 * 3
    back_second = lax.dot_general(delta, third, (((1,), (1,)), ((), ())), preferred_element_type=f32)
    second_delta = (slope_second.astype(f32) * back_second).astype(bf16)
    second_bias_grad = jnp.sum(second_delta.astype(f32), axis=0).astype(bf16)
    send_lead = contract(hidden_first[:, half : half + lead], second_delta)
    got_lead = swap_cores(send_lead)
    keep_lead = contract(hidden_first[:, :lead], second_delta)
    send_tail = contract(hidden_first[:, half + lead :], second_delta)
    keep_tail = contract(hidden_first[:, lead:half], second_delta)
    third_grad = contract(delta, hidden_second)
    back_first = lax.dot_general(
        second_delta, second_turned, (((1,), (1,)), ((), ())), preferred_element_type=f32
    )
    first_delta = (slope_first.astype(f32) * back_first).astype(bf16)
    first_grad = contract(x, first_delta)
    first_bias_grad = jnp.sum(first_delta.astype(f32), axis=0).astype(bf16)

    is_first = core == 0
    domains = lax.axis_size("dom")
    column_splits = (hidden // LANES).bit_length() - 1
    grain = 8 * max(1, domains >> column_splits)
    used = half - lead + feat // 2 + class_half
    tail_rows = -(-(used + 1) // grain) * grain

    def bundle(part, tail, third_rows, bias_half):
        at = slice(part * half, (part + 1) * half)
        first_rows = jnp.concatenate([first_grad[: feat // 2, at], first_grad[feat // 2 :, at]], 1)
        bias_row = jnp.concatenate([first_bias_grad[at], bias_half])
        bias = jnp.broadcast_to(bias_row[None], (tail_rows - used, hidden))
        return jnp.concatenate([tail, first_rows, third_rows[:class_half], bias], 0)

    low_bias, high_bias = split(second_bias_grad, 0)
    keep_rest = bundle(0, keep_tail, third_grad[:LANES], jnp.where(is_first, low_bias, high_bias))
    send_rest = bundle(1, send_tail, third_grad[LANES:], jnp.where(is_first, high_bias, low_bias))
    got_rest = swap_cores(send_rest)
    mine_lead = sum_over_domains((keep_lead.astype(f32) + got_lead.astype(f32)).astype(bf16))
    mine_rest = sum_over_domains((keep_rest.astype(f32) + got_rest.astype(f32)).astype(bf16))
    theirs_lead, theirs_rest = swap_cores(mine_lead), swap_cores(mine_rest)
    step = math.gcd(lead, half)
    second_type = jax.ShapeDtypeStruct((hidden, hidden), f32)
    small_grant = pltpu.CompilerParams(vmem_limit_bytes=24 * 1024 * 1024)
    second_lead = pl.pallas_call(
        functools.partial(finish_lead_kernel, step),
        out_shape=second_type,
        in_specs=[smem(), vmem(), vmem()],
        out_specs=hbm(),
        scratch_shapes=[pltpu.VMEM((2 * lead, hidden), f32), pltpu.SemaphoreType.DMA((2 * (lead // step),))],
        compiler_params=small_grant,
        cost_estimate=pl.CostEstimate(flops=2 * lead * hidden, bytes_accessed=12 * lead * hidden, transcendentals=0),
        name="finish_lead",
    )(core_arg, mine_lead, theirs_lead)
    first_out, first_bias_out, second_out, second_bias_out, third_out = pl.pallas_call(
        functools.partial(finish_kernel, class_half, lead, step),
        out_shape=(
            jax.ShapeDtypeStruct((feat, hidden), f32),
            jax.ShapeDtypeStruct((1, hidden), f32),
            second_type,
            jax.ShapeDtypeStruct((1, hidden), f32),
            jax.ShapeDtypeStruct((classes, hidden), f32),
        ),
        in_specs=[smem(), vmem(), vmem(), hbm()],
        out_specs=(vmem(), vmem(), hbm(), vmem(), vmem()),
        scratch_shapes=[
            pltpu.VMEM((2 * (half - lead), hidden), f32),
            pltpu.SemaphoreType.DMA((2 * ((half - lead) // step),)),
        ],
        input_output_aliases={3: 2},
        compiler_params=small_grant,
        name="finish",
    )(core_arg, mine_rest, theirs_rest, second_lead)
    return first_out, first_bias_out.reshape(hidden), second_out, second_bias_out.reshape(hidden), third_out.T


def solution(mesh):
    return jax.shard_map(
        shards,
        mesh=mesh,
        in_specs=(
            P(("grp", "dom", "col"), None),
            P(),
            P(),
            P(),
            P(),
            P(),
            P(("grp", "dom"), "col", None, None, None),
            P(("grp", "dom"), "col", None),
            P(("grp", "dom"), "col", None),
            P(("grp", "dom"), "col", None, None, None),
            P(("grp", "dom"), "col", None),
            P(("grp", "dom"), "col", None),
            P(("grp", "dom"), None, None),
            P(("grp", "dom"), None),
            P(("grp", "dom")),
            P(("grp", "dom"), None),
            P(("grp", "dom"), None),
            P(("grp", "dom"), None, None),
        ),
        out_specs=(P("grp", None), P("grp"), P("grp", None), P("grp"), P("grp", None)),
        check_vma=False,
    )
```
